32 devices in a mesh: dp: 2 (over core), pipe: 4 (over y, x), tensor: 4 (over z).
Axes of the slice: x: 2, y: 2, z: 4, core: 2. Of those that a mesh axis runs over, the one named last changes fastest.
Arguments:
- forward_acts: bfloat16 [256, 8192], P(('dp', 'tensor'), 'pipe'), parts along dimension 0, may hold values from -6 to 6
- backward_grad: bfloat16 [256, 8192], P(('dp', 'tensor'), 'pipe'), parts along dimension 0, may hold values from -6 to 6
- stored_gate: bfloat16 [256, 14336], P(('dp', 'pipe'), 'tensor'), parts along dimension 0, may hold values from -8 to 8
- stored_up: bfloat16 [256, 14336], P(('dp', 'pipe'), 'tensor'), parts along dimension 0, may hold values from -6 to 6
- gate_weight: bfloat16 [8192, 14336], P('pipe', 'tensor'), may hold values from -0.0625 to 0.0625
- up_weight: bfloat16 [8192, 14336], P('pipe', 'tensor'), may hold values from -0.0625 to 0.0625
- down_weight: bfloat16 [14336, 8192], P('tensor', 'pipe'), may hold values from -0.046875 to 0.046875
Outputs:
- layer_output: bfloat16 [256, 8192], P(('dp', 'tensor'), 'pipe'), parts along dimension 0
- input_grad: bfloat16 [256, 8192], P(('dp', 'tensor'), 'pipe'), parts along dimension 0
The draws below stay inside these ranges and needn't reach their ends.
There are 2 independent parts, one for each index of `dp`. The reference program is written for one: setup_inputs(seed, part) draws one part's arguments, and reference() takes and returns one part's arrays. A program takes and returns all parts, laid end to end along the dimension named above; an argument that names none is the same for every part. Nothing has to cross between parts.
All inputs are finite; a program needn't handle non-finite values.
Results may differ from the reference program's by a relative error of at most 0.005.
Values may be sent and summed in bfloat16 or wider, within the bound.
No kernel may reach another device: no remote copies, remote signals or barrier semaphores. Data moves between devices by JAX's collectives and lax.ppermute only.
A program may use at most 128 MiB of HBM per device.

```python
import jax
import jax.numpy as jnp
from jax import lax

D = 8192
FF = 14336
TOK = 128


def block_levels(stream_key, dims, cuts, smallest, top_value):
    factor_of = 1.0
    for position, parts in cuts:
        draws = jax.random.uniform(jax.random.fold_in(jax.random.fold_in(stream_key, 6), position), (parts,), jnp.float32, smallest / len(cuts), top_value / len(cuts))
        factor_of = factor_of * jnp.repeat(jnp.exp(draws), dims[position] // parts).reshape((-1,) + (1,) * (len(dims) - 1 - position))
    return factor_of


def scatter_about(stream_key, shape, scale, bound, cuts=(), dtype=jnp.bfloat16):
    result = jax.random.normal(stream_key, shape, jnp.float32) * scale
    if len(cuts) > 0:
        result = block_levels(stream_key, shape, cuts, -0.22, 0.18) * result
    return jnp.clip(result, min=-bound, max=bound).astype(dtype)


def setup_inputs(seed: int = 0, part: int = 0) -> dict:
    key_list = jax.random.split(jax.random.key(seed), 8)
    part_keys = jax.random.split(jax.random.fold_in(key_list[7], part), 8)
    forward_acts = scatter_about(part_keys[0], (TOK, D), 1.0, 6.0, ((0, 4), (1, 4)))
    backward_grad = scatter_about(part_keys[1], (TOK, D), 1.0, 6.0, ((0, 4), (1, 4)))
    stored_gate = scatter_about(part_keys[2], (TOK, FF), 1.5, 8.0, ((0, 4), (1, 4)))
    stored_up = scatter_about(part_keys[3], (TOK, FF), 1.0, 6.0, ((0, 4), (1, 4)))
    gate_weight = scatter_about(key_list[4], (D, FF), D ** -0.5, 0.0625, ((0, 4), (1, 4)))
    up_weight = scatter_about(key_list[5], (D, FF), D ** -0.5, 0.0625, ((0, 4), (1, 4)))
    down_weight = scatter_about(key_list[6], (FF, D), FF ** -0.5, 0.046875, ((0, 4), (1, 4)))
    return {"forward_acts": forward_acts, "backward_grad": backward_grad, "stored_gate": stored_gate, "stored_up": stored_up, "gate_weight": gate_weight, "up_weight": up_weight, "down_weight": down_weight}


def reference(forward_acts, backward_grad, stored_gate, stored_up, gate_weight, up_weight, down_weight):
    paired = jnp.concatenate([gate_weight, up_weight], axis=1)
    projected = jnp.dot(forward_acts, paired, preferred_element_type=jnp.float32)
    hidden = (jax.nn.silu(projected[:, :FF]) * projected[:, FF:]).astype(jnp.bfloat16)
    layer_output = jnp.dot(hidden, down_weight, preferred_element_type=jnp.float32).astype(jnp.bfloat16)
    hidden_grad = lax.dot_general(backward_grad, down_weight, (((1,), (1,)), ((), ())), preferred_element_type=jnp.float32)
    gate_vals = stored_gate.astype(jnp.float32)
    up_vals = stored_up.astype(jnp.float32)
    sigma = jax.nn.sigmoid(gate_vals)
    gate_slope = (hidden_grad * up_vals * sigma * (1.0 + gate_vals * (1.0 - sigma))).astype(jnp.bfloat16)
    up_slope = (hidden_grad * gate_vals * sigma).astype(jnp.bfloat16)
    slopes = jnp.concatenate([gate_slope, up_slope], axis=1)
    input_grad = lax.dot_general(slopes, paired, (((1,), (1,)), ((), ())), preferred_element_type=jnp.float32).astype(jnp.bfloat16)
    return layer_output, input_grad
```

```python
import functools

import jax
import jax.numpy as jnp
from jax import lax
from jax.experimental import pallas as pl
from jax.experimental.pallas import tpu as pltpu
from jax.sharding import PartitionSpec as P

F32 = jnp.float32
BF16 = jnp.bfloat16
VMEM_BYTES = 40 * 1024 * 1024
CONTRACT_LAST = (((1,), (1,)), ((), ()))


def exchange(value, axis, size, step):
    return lax.ppermute(value, axis, [(i, i ^ step) for i in range(size)])


def pick_tile(width):
    return 256 if width % 256 == 0 else 128


def split_tiles(width, parts):
    tiles = width // pick_tile(width)
    edges = [tiles * i // parts for i in range(parts + 1)]
    return [(a, b - a) for a, b in zip(edges[:-1], edges[1:]) if b > a]


def arrange(blocks, from_index, to_index, to_size, tokens, natural, ordered):
    col = 0
    for chunk in blocks:
        for s, ref in enumerate(chunk):
            rows, cols = ref.shape
            start = pl.multiple_of((from_index ^ s) * rows, rows)
            natural[pl.ds(start, rows), col : col + cols] = ref[...]
        col += cols
    rows = tokens // to_size
    for s in range(to_size):
        start = pl.multiple_of((to_index ^ s) * rows, rows)
        ordered[s * rows : (s + 1) * rows, :] = natural[pl.ds(start, rows), :]


def whole(shape):
    return pl.BlockSpec(shape, lambda j: (0,) * len(shape))


def params():
    return pltpu.CompilerParams(
        dimension_semantics=("arbitrary",), vmem_limit_bytes=VMEM_BYTES
    )


def cost(flops, moved):
    return pl.CostEstimate(flops=flops, bytes_accessed=moved, transcendentals=0)


def project(acts, weights, first, count, n_pipe, n_tensor):
    block, depth = acts[0].shape
    tokens = block * n_tensor
    tile = pick_tile(weights[0].shape[1])
    rows = tokens // n_pipe
    kinds = len(weights)

    def kernel(*refs):
        x_refs = refs[:n_tensor]
        w_refs = refs[n_tensor : n_tensor + kinds]
        out_refs = refs[n_tensor + kinds : n_tensor + kinds + n_pipe]
        natural, ordered = refs[n_tensor + kinds + n_pipe :]
        t = lax.axis_index("tensor")
        p = lax.axis_index("pipe")

        @pl.when(pl.program_id(0) == 0)
        def _():
            arrange([x_refs], t, p, n_pipe, tokens, natural, ordered)

        for k in range(kinds):
            total = jnp.dot(ordered[...], w_refs[k][...], preferred_element_type=F32)
            for s in range(n_pipe):
                out_refs[s][k] = total[s * rows : (s + 1) * rows].astype(out_refs[s].dtype)

    return pl.pallas_call(
        kernel,
        grid=(count,),
        in_specs=[whole((block, depth))] * n_tensor
        + [pl.BlockSpec((depth, tile), lambda j: (0, first + j))] * kinds,
        out_specs=[pl.BlockSpec((kinds, rows, tile), lambda j: (0, 0, j))] * n_pipe,
        out_shape=[
            jax.ShapeDtypeStruct((kinds, rows, count * tile), F32 if s == 0 else BF16)
            for s in range(n_pipe)
        ],
        scratch_shapes=[pltpu.VMEM((tokens, depth), BF16)] * 2,
        compiler_params=params(),
        cost_estimate=cost(2 * tokens * depth * tile * count * kinds, 2 * depth * tile * count * kinds),
        name="project",
    )(*acts, *weights)


def pull_back(grads, weight, first, count, n_pipe, n_tensor):
    block, depth = grads[0].shape
    tokens = block * n_tensor
    tile = pick_tile(weight.shape[0])
    rows = tokens // n_pipe

    def kernel(*refs):
        x_refs = refs[:n_tensor]
        w_ref = refs[n_tensor]
        out_refs = refs[n_tensor + 1 : n_tensor + 1 + n_pipe]
        natural, ordered = refs[n_tensor + 1 + n_pipe :]
        t = lax.axis_index("tensor")
        p = lax.axis_index("pipe")

        @pl.when(pl.program_id(0) == 0)
        def _():
            arrange([x_refs], t, p, n_pipe, tokens, natural, ordered)

        total = lax.dot_general(
            ordered[...], w_ref[...], CONTRACT_LAST, preferred_element_type=F32
        )
        for s in range(n_pipe):
            out_refs[s][...] = total[s * rows : (s + 1) * rows].astype(out_refs[s].dtype)

    return pl.pallas_call(
        kernel,
        grid=(count,),
        in_specs=[whole((block, depth))] * n_tensor
        + [pl.BlockSpec((tile, depth), lambda j: (first + j, 0))],
        out_specs=[pl.BlockSpec((rows, tile), lambda j: (0, j))] * n_pipe,
        out_shape=[
            jax.ShapeDtypeStruct((rows, count * tile), F32 if s == 0 else BF16)
            for s in range(n_pipe)
        ],
        scratch_shapes=[pltpu.VMEM((tokens, depth), BF16)] * 2,
        compiler_params=params(),
        cost_estimate=cost(2 * tokens * depth * tile * count, 2 * depth * tile * count),
        name="pull_back",
    )(*grads, weight)


def contract_units(groups, weights, transposed, first, count, n_pipe, n_tensor):
    kinds = len(groups)
    flat = [a for kind in groups for chunk in kind for a in chunk]
    n_in = len(flat)
    rows_in = flat[0].shape[0]
    tokens = rows_in * n_pipe
    units = sum(chunk[0].shape[1] for chunk in groups[0])
    width = weights[0].shape[0] if transposed else weights[0].shape[1]
    tile = pick_tile(width)
    rows = tokens // n_tensor

    def kernel(*refs):
        w_refs = refs[n_in : n_in + kinds]
        out_refs = refs[n_in + kinds : n_in + kinds + n_tensor]
        natural, ordered = refs[n_in + kinds + n_tensor :]
        t = lax.axis_index("tensor")
        p = lax.axis_index("pipe")

        @pl.when(pl.program_id(0) == 0)
        def _():
            place = 0
            for k in range(kinds):
                blocks = []
                for chunk in groups[k]:
                    blocks.append(refs[place : place + len(chunk)])
                    place += len(chunk)
                arrange(blocks, p, t, n_tensor, tokens, natural, ordered.at[k])

        total = None
        for k in range(kinds):
            if transposed:
                part = lax.dot_general(
                    ordered[k], w_refs[k][...], CONTRACT_LAST, preferred_element_type=F32
                )
            else:
                part = jnp.dot(ordered[k], w_refs[k][...], preferred_element_type=F32)
            total = part if total is None else total + part
        for s in range(n_tensor):
            out_refs[s][...] = total[s * rows : (s + 1) * rows].astype(out_refs[s].dtype)

    if transposed:
        weight_spec = pl.BlockSpec((tile, units), lambda j: (first + j, 0))
    else:
        weight_spec = pl.BlockSpec((units, tile), lambda j: (0, first + j))
    return pl.pallas_call(
        kernel,
        grid=(count,),
        in_specs=[whole(a.shape) for a in flat] + [weight_spec] * kinds,
        out_specs=[pl.BlockSpec((rows, tile), lambda j: (0, j))] * n_tensor,
        out_shape=[
            jax.ShapeDtypeStruct((rows, count * tile), F32 if s == 0 else BF16)
            for s in range(n_tensor)
        ],
        scratch_shapes=[
            pltpu.VMEM((tokens, units), BF16),
            pltpu.VMEM((kinds, tokens, units), BF16),
        ],
        compiler_params=params(),
        cost_estimate=cost(2 * tokens * units * tile * count * kinds, 2 * units * tile * count * kinds),
        name="contract_units",
    )(*flat, *weights)


def gather_parts(value, axis, size):
    return [value] + [exchange(value, axis, size, s) for s in range(1, size)]


def sum_parts(parts, axis, size):
    total = parts[0]
    for s in range(1, size):
        total = total + exchange(parts[s], axis, size, s).astype(F32)
    return total


def per_device(
    n_pipe,
    n_tensor,
    forward_acts,
    backward_grad,
    stored_gate,
    stored_up,
    gate_weight,
    up_weight,
    down_weight,
):
    hidden_width = gate_weight.shape[1]
    model_width = gate_weight.shape[0]
    unit_parts = split_tiles(hidden_width, 2)
    out_parts = split_tiles(model_width, 2)
    unit_tile = pick_tile(hidden_width)

    acts = gather_parts(forward_acts, "tensor", n_tensor)
    grads = gather_parts(backward_grad, "tensor", n_tensor)

    hidden = []
    slopes = []
    for first, count in unit_parts:
        parts = project(acts, [gate_weight, up_weight], first, count, n_pipe, n_tensor)
        summed = sum_parts(parts, "pipe", n_pipe)
        hidden_part = (jax.nn.silu(summed[0]) * summed[1]).astype(BF16)
        hidden.append(gather_parts(hidden_part, "pipe", n_pipe))
    for first, count in unit_parts:
        parts = pull_back(grads, down_weight, first, count, n_pipe, n_tensor)
        grad = sum_parts(parts, "pipe", n_pipe)
        columns = slice(first * unit_tile, (first + count) * unit_tile)
        gate_wide = stored_gate[:, columns].astype(F32)
        up_wide = stored_up[:, columns].astype(F32)
        sigma = jax.nn.sigmoid(gate_wide)
        gate_slope = (grad * up_wide * sigma * (1.0 + gate_wide * (1.0 - sigma))).astype(BF16)
        up_slope = (grad * gate_wide * sigma).astype(BF16)
        slopes.append(
            (gather_parts(gate_slope, "pipe", n_pipe), gather_parts(up_slope, "pipe", n_pipe))
        )

    out = []
    for first, count in out_parts:
        parts = contract_units(
            [hidden], [down_weight], False, first, count, n_pipe, n_tensor
        )
        out.append(sum_parts(parts, "tensor", n_tensor).astype(BF16))
    back = []
    for first, count in out_parts:
        parts = contract_units(
            [[a for a, _ in slopes], [b for _, b in slopes]],
            [gate_weight, up_weight],
            True,
            first,
            count,
            n_pipe,
            n_tensor,
        )
        back.append(sum_parts(parts, "tensor", n_tensor).astype(BF16))
    return jnp.concatenate(out, axis=1), jnp.concatenate(back, axis=1)


def solution(mesh):
    in_specs = (
        P(("dp", "tensor"), "pipe"),
        P(("dp", "tensor"), "pipe"),
        P(("dp", "pipe"), "tensor"),
        P(("dp", "pipe"), "tensor"),
        P("pipe", "tensor"),
        P("pipe", "tensor"),
        P("tensor", "pipe"),
    )
    out_specs = (P(("dp", "tensor"), "pipe"), P(("dp", "tensor"), "pipe"))
    body = functools.partial(per_device, mesh.shape["pipe"], mesh.shape["tensor"])
    return jax.shard_map(
        body, mesh=mesh, in_specs=in_specs, out_specs=out_specs, check_vma=False
    )
```

```python
import functools

import jax
import jax.numpy as jnp
from jax import lax
from jax.experimental import pallas as pl
from jax.experimental.pallas import tpu as pltpu
from jax.sharding import PartitionSpec as P

F32 = jnp.float32
BF16 = jnp.bfloat16
VMEM_BYTES = 40 * 1024 * 1024
CONTRACT_LAST = (((1,), (1,)), ((), ()))
AHEAD = 4
IN_VMEM = pl.BlockSpec(memory_space=pltpu.VMEM)
IN_PLACE = pl.BlockSpec(memory_space=pl.ANY)


def exchange(value, axis, size, step):
    return lax.ppermute(value, axis, [(i, i ^ step) for i in range(size)])


def gather_parts(value, axis, size):
    return [value] + [exchange(value, axis, size, s) for s in range(1, size)]


def sum_parts(parts, axis, size):
    total = parts[0]
    for s in range(1, size):
        total = total + exchange(parts[s], axis, size, s).astype(F32)
    return total


def pick_tile(width):
    return 256 if width % 256 == 0 else 128


def cost(flops, moved):
    return pl.CostEstimate(flops=flops, bytes_accessed=moved, transcendentals=0)


def params():
    return pltpu.CompilerParams(vmem_limit_bytes=VMEM_BYTES)


def reorder(source, target, from_index, from_rows, to_index, to_rows, tokens):
    unit = min(from_rows, to_rows)
    per_source, per_target = from_rows // unit, to_rows // unit
    for s in range(tokens // to_rows):
        for i in range(per_target):
            n = (to_index ^ s) * per_target + i
            at = (((n // per_source) ^ from_index) * per_source + n % per_source) * unit
            target(s, i * unit, unit, source[pl.ds(pl.multiple_of(at, unit), unit), :])


def stream(count, copies, work):
    for j in range(min(AHEAD, count)):
        for copy in copies(j):
            copy.start()

    def step(j, carry):
        @pl.when(j + AHEAD < count)
        def _():
            for copy in copies(j + AHEAD):
                copy.start()

        for copy in copies(j):
            copy.wait()
        work(j)
        return carry

    lax.fori_loop(0, count, step, 0)


def project(inputs, weights, transposed, n_pipe, n_tensor):
    cores = len(inputs)
    kinds = len(weights)
    tokens, depth = inputs[0].shape
    units = (weights[0].shape[0] if transposed else weights[0].shape[1]) // cores
    tile = pick_tile(units)
    count = units // tile
    rows = tokens // n_pipe
    block = tokens // n_tensor

    def kernel(*refs):
        x_refs = refs[:cores]
        w_refs = refs[cores : cores + kinds]
        out_refs = refs[cores + kinds : cores + kinds + n_pipe]
        ordered, held, sems = refs[cores + kinds + n_pipe :]
        t = lax.axis_index("tensor")
        p = lax.axis_index("pipe")
        first = lax.axis_index("dp") * units if cores > 1 else 0

        def copies(j):
            at = pl.multiple_of(first + j * tile, tile)
            window = (pl.ds(at, tile), slice(None)) if transposed else (slice(None), pl.ds(at, tile))
            return [
                pltpu.make_async_copy(w_refs[k].at[window], held.at[k, j], sems.at[k, j])
                for k in range(kinds)
            ]

        def work(j):
            at = pl.multiple_of(j * tile, tile)
            for k in range(kinds):
                if transposed:
                    total = lax.dot_general(
                        ordered[...], held[k, j], CONTRACT_LAST, preferred_element_type=F32
                    )
                else:
                    total = jnp.dot(ordered[...], held[k, j], preferred_element_type=F32)
                for s in range(n_pipe):
                    part = total[s * cores * rows : (s + 1) * cores * rows]
                    out_refs[s][k, :, pl.ds(at, tile)] = part.astype(out_refs[s].dtype)

        for a in range(cores):
            def put(s, row, size, value, a=a):
                start = (s * cores + a) * rows + row
                ordered[start : start + size, :] = value

            reorder(x_refs[a], put, t, block, p, rows, tokens)
        stream(count, copies, work)

    window_shape = (tile, depth) if transposed else (depth, tile)
    return pl.pallas_call(
        kernel,
        in_specs=[IN_VMEM] * cores + [IN_PLACE] * kinds,
        out_specs=[IN_VMEM] * n_pipe,
        out_shape=[
            jax.ShapeDtypeStruct((kinds, cores * rows, units), F32 if s == 0 else BF16)
            for s in range(n_pipe)
        ],
        scratch_shapes=[
            pltpu.VMEM((cores * tokens, depth), BF16),
            pltpu.VMEM((kinds, count) + window_shape, BF16),
            pltpu.SemaphoreType.DMA((kinds, count)),
        ],
        compiler_params=params(),
        cost_estimate=cost(2 * cores * tokens * depth * units * kinds, 2 * depth * units * kinds),
        name="pull_back" if transposed else "project",
    )(*inputs, *weights)


def contract(blocks, weights, transposed, cores, n_pipe, n_tensor):
    kinds, block_rows, units = blocks[0].shape
    from_rows = block_rows // cores
    tokens = from_rows * n_pipe
    to_rows = tokens // n_tensor
    width = weights[0].shape[0] if transposed else weights[0].shape[1]
    tile = pick_tile(width)
    count = width // tile

    def kernel(*refs):
        x_refs = refs[:n_pipe]
        w_refs = refs[n_pipe : n_pipe + kinds]
        out_refs = refs[n_pipe + kinds : n_pipe + kinds + cores]
        natural, ordered, held, sems = refs[n_pipe + kinds + cores :]
        t = lax.axis_index("tensor")
        p = lax.axis_index("pipe")
        first = pl.multiple_of(lax.axis_index("dp") * units, units) if cores > 1 else 0

        def copies(j):
            at = pl.multiple_of(j * tile, tile)
            window = (
                (pl.ds(at, tile), pl.ds(first, units))
                if transposed
                else (pl.ds(first, units), pl.ds(at, tile))
            )
            return [
                pltpu.make_async_copy(w_refs[k].at[window], held.at[k, j], sems.at[k, j])
                for k in range(kinds)
            ]

        def work(j):
            at = pl.multiple_of(j * tile, tile)
            total = None
            for k in range(kinds):
                if transposed:
                    part = lax.dot_general(
                        ordered[k], held[k, j], CONTRACT_LAST, preferred_element_type=F32
                    )
                else:
                    part = jnp.dot(ordered[k], held[k, j], preferred_element_type=F32)
                total = part if total is None else total + part
            for a in range(cores):
                part = total[a * tokens : (a + 1) * tokens]
                out_refs[a][:, pl.ds(at, tile)] = part.astype(out_refs[a].dtype)

        for k in range(kinds):
            for a in range(cores):
                for s in range(n_pipe):
                    start = pl.multiple_of((p ^ s) * from_rows, from_rows)
                    natural[pl.ds(start, from_rows), :] = x_refs[s][
                        k, a * from_rows : (a + 1) * from_rows, :
                    ]
                for s in range(n_tensor):
                    start = pl.multiple_of((t ^ s) * to_rows, to_rows)
                    at = a * tokens + s * to_rows
                    ordered[k, at : at + to_rows, :] = natural[pl.ds(start, to_rows), :]
        stream(count, copies, work)

    window_shape = (tile, units) if transposed else (units, tile)
    return pl.pallas_call(
        kernel,
        in_specs=[IN_VMEM] * n_pipe + [IN_PLACE] * kinds,
        out_specs=[IN_VMEM] * cores,
        out_shape=[
            jax.ShapeDtypeStruct((tokens, width), BF16 if a else F32) for a in range(cores)
        ],
        scratch_shapes=[
            pltpu.VMEM((tokens, units), BF16),
            pltpu.VMEM((kinds, cores * tokens, units), BF16),
            pltpu.VMEM((kinds, count) + window_shape, BF16),
            pltpu.SemaphoreType.DMA((kinds, count)),
        ],
        compiler_params=params(),
        cost_estimate=cost(2 * cores * tokens * units * width * kinds, 2 * units * width * kinds),
        name="input_grad" if transposed else "layer_output",
    )(*blocks, *weights)


def per_device(
    n_pipe,
    n_tensor,
    cores,
    forward_acts,
    backward_grad,
    stored_gate,
    stored_up,
    gate_weight,
    up_weight,
    down_weight,
):
    units = gate_weight.shape[1] // cores

    def all_tokens(value):
        own = jnp.concatenate(gather_parts(value, "tensor", n_tensor), axis=0)
        return gather_parts(own, "dp", cores)

    def finish(partials):
        total = sum_parts(partials, "dp", cores)
        rows = total.shape[0] // n_tensor
        parts = [total[:rows]] + [
            total[s * rows : (s + 1) * rows].astype(BF16) for s in range(1, n_tensor)
        ]
        return sum_parts(parts, "tensor", n_tensor).astype(BF16)

    stored = jnp.stack([stored_gate, stored_up])
    if cores > 1:
        core = lax.axis_index("dp")
        mine = lax.dynamic_slice_in_dim(stored, core * units, units, 2)
        other = lax.dynamic_slice_in_dim(stored, (1 - core) * units, units, 2)
        stored = jnp.concatenate([mine, exchange(other, "dp", cores, 1)], axis=1)

    grads = all_tokens(backward_grad)
    acts = all_tokens(forward_acts)

    parts = project(grads, [down_weight], True, n_pipe, n_tensor)
    grad = sum_parts(parts, "pipe", n_pipe)[0]
    gate_wide = stored[0].astype(F32)
    up_wide = stored[1].astype(F32)
    sigma = jax.nn.sigmoid(gate_wide)
    gate_slope = (grad * up_wide * sigma * (1.0 + gate_wide * (1.0 - sigma))).astype(BF16)
    up_slope = (grad * gate_wide * sigma).astype(BF16)
    slopes = gather_parts(jnp.stack([gate_slope, up_slope]), "pipe", n_pipe)

    parts = project(acts, [gate_weight, up_weight], False, n_pipe, n_tensor)
    summed = sum_parts(parts, "pipe", n_pipe)
    hidden = (jax.nn.silu(summed[:1]) * summed[1:]).astype(BF16)
    hidden = gather_parts(hidden, "pipe", n_pipe)

    back = contract(slopes, [gate_weight, up_weight], True, cores, n_pipe, n_tensor)
    input_grad = finish(back)
    out = contract(hidden, [down_weight], False, cores, n_pipe, n_tensor)
    layer_output = finish(out)
    return layer_output, input_grad


def solution(mesh):
    in_specs = (
        P(("dp", "tensor"), "pipe"),
        P(("dp", "tensor"), "pipe"),
        P(("dp", "pipe"), "tensor"),
        P(("dp", "pipe"), "tensor"),
        P("pipe", "tensor"),
        P("pipe", "tensor"),
        P("tensor", "pipe"),
    )
    out_specs = (P(("dp", "tensor"), "pipe"), P(("dp", "tensor"), "pipe"))

    def whole(*args):
        hidden_width = args[4].shape[1] // mesh.shape["tensor"]
        cores = 2 if mesh.shape["dp"] == 2 and hidden_width % 256 == 0 else 1
        body = functools.partial(per_device, mesh.shape["pipe"], mesh.shape["tensor"], cores)
        return jax.shard_map(
            body, mesh=mesh, in_specs=in_specs, out_specs=out_specs, check_vma=False
        )(*args)

    return whole
```

```python
import functools

import jax
import jax.numpy as jnp
from jax import lax
from jax.experimental import pallas as pl
from jax.experimental.pallas import tpu as pltpu
from jax.sharding import PartitionSpec as P

F32 = jnp.float32
BF16 = jnp.bfloat16
VMEM_BYTES = 40 * 1024 * 1024
CONTRACT_LAST = (((1,), (1,)), ((), ()))
AHEAD = 4
IN_VMEM = pl.BlockSpec(memory_space=pltpu.VMEM)
IN_PLACE = pl.BlockSpec(memory_space=pl.ANY)


def exchange(value, axis, size, step):
    return lax.ppermute(value, axis, [(i, i ^ step) for i in range(size)])


def pick_tile(width):
    return 256 if width % 256 == 0 else 128


def cost(flops, moved):
    return pl.CostEstimate(flops=flops, bytes_accessed=moved, transcendentals=0)


def params():
    return pltpu.CompilerParams(vmem_limit_bytes=VMEM_BYTES)


def stream(count, copies, work):
    for j in range(min(AHEAD, count)):
        for copy in copies(j):
            copy.start()

    def step(j, carry):
        @pl.when(j + AHEAD < count)
        def _():
            for copy in copies(j + AHEAD):
                copy.start()

        for copy in copies(j):
            copy.wait()
        work(j)
        return carry

    lax.fori_loop(0, count, step, 0)


def small_kernel(body, outs, inputs, name, after=()):
    n_in, n_after = len(inputs), len(after)

    def kernel(*refs):
        body(refs[:n_in], refs[n_in + n_after :])

    moved = sum(a.size * a.dtype.itemsize for a in inputs)
    return pl.pallas_call(
        kernel,
        in_specs=[IN_VMEM] * n_in + [IN_PLACE] * n_after,
        out_specs=[IN_VMEM] * len(outs),
        out_shape=[jax.ShapeDtypeStruct(shape, dtype) for shape, dtype in outs],
        cost_estimate=cost(moved, moved),
        compiler_params=pltpu.CompilerParams(vmem_limit_bytes=VMEM_BYTES // 2),
        name=name,
    )(*inputs, *after)


def project(inputs, weights, transposed, layout, n_pipe, after=()):
    cores = len(inputs)
    n_in, n_after, n_out, kinds = len(inputs), len(after), len(layout), len(weights)
    tokens, depth = inputs[0].shape
    units = (weights[0].shape[0] if transposed else weights[0].shape[1]) // cores
    tile = pick_tile(units)
    count = units // tile
    rows = tokens // n_pipe
    places = [piece for _, pieces in layout for piece in pieces]

    def kernel(*refs):
        x_refs = refs[:n_in]
        w_refs = refs[n_in : n_in + kinds]
        out_refs = refs[n_in + kinds + n_after : n_in + kinds + n_after + n_out]
        ordered, held, sems = refs[n_in + kinds + n_after + n_out :]
        p = lax.axis_index("pipe")
        first = lax.axis_index("dp") * units if cores > 1 else 0

        def copies(j):
            at = pl.multiple_of(first + j * tile, tile)
            window = (pl.ds(at, tile), slice(None)) if transposed else (slice(None), pl.ds(at, tile))
            return [
                pltpu.make_async_copy(w_refs[k].at[window], held.at[k, j], sems.at[k, j])
                for k in range(kinds)
            ]

        def work(j):
            at = pl.multiple_of(j * tile, tile)
            for k in range(kinds):
                if transposed:
                    total = lax.dot_general(
                        ordered[...], held[k, j], CONTRACT_LAST, preferred_element_type=F32
                    )
                else:
                    total = jnp.dot(ordered[...], held[k, j], preferred_element_type=F32)
                row = 0
                for ref in out_refs:
                    size = ref.shape[1]
                    ref[k, :, pl.ds(at, tile)] = total[row : row + size].astype(ref.dtype)
                    row += size

        for i, (s, a) in enumerate(places):
            start = pl.multiple_of((p ^ s) * rows, rows)
            ordered[i * rows : (i + 1) * rows, :] = x_refs[a][pl.ds(start, rows), :]
        stream(count, copies, work)

    window_shape = (tile, depth) if transposed else (depth, tile)
    return pl.pallas_call(
        kernel,
        in_specs=[IN_VMEM] * n_in + [IN_PLACE] * (kinds + n_after),
        out_specs=[IN_VMEM] * n_out,
        out_shape=[
            jax.ShapeDtypeStruct((kinds, len(pieces) * rows, units), dtype)
            for dtype, pieces in layout
        ],
        scratch_shapes=[
            pltpu.VMEM((cores * tokens, depth), BF16),
            pltpu.VMEM((kinds, count) + window_shape, BF16),
            pltpu.SemaphoreType.DMA((kinds, count)),
        ],
        compiler_params=params(),
        cost_estimate=cost(2 * cores * tokens * depth * units * kinds, 2 * depth * units * kinds),
        name="pull_back" if transposed else "project",
    )(*inputs, *weights, *after)


def contract(blocks, pieces, weights, transposed, cores, n_pipe, n_tensor, after=()):
    kinds, _, units = blocks[0].shape
    n_in, n_after = len(blocks), len(after)
    from_rows = blocks[0].shape[1] // cores
    tokens = from_rows * n_pipe
    to_rows = tokens // n_tensor
    width = weights[0].shape[0] if transposed else weights[0].shape[1]
    tile = pick_tile(width)
    count = width // tile

    def kernel(*refs):
        x_refs = refs[:n_in]
        w_refs = refs[n_in : n_in + kinds]
        out_refs = refs[n_in + kinds + n_after : n_in + kinds + n_after + cores]
        natural, ordered, held, sems = refs[n_in + kinds + n_after + cores :]
        t = lax.axis_index("tensor")
        p = lax.axis_index("pipe")
        first = pl.multiple_of(lax.axis_index("dp") * units, units) if cores > 1 else 0

        def copies(j):
            at = pl.multiple_of(j * tile, tile)
            window = (
                (pl.ds(at, tile), pl.ds(first, units))
                if transposed
                else (pl.ds(first, units), pl.ds(at, tile))
            )
            return [
                pltpu.make_async_copy(w_refs[k].at[window], held.at[k, j], sems.at[k, j])
                for k in range(kinds)
            ]

        def work(j):
            at = pl.multiple_of(j * tile, tile)
            total = None
            for k in range(kinds):
                if transposed:
                    part = lax.dot_general(
                        ordered[k], held[k, j], CONTRACT_LAST, preferred_element_type=F32
                    )
                else:
                    part = jnp.dot(ordered[k], held[k, j], preferred_element_type=F32)
                total = part if total is None else total + part
            for a in range(cores):
                part = total[a * tokens : (a + 1) * tokens]
                out_refs[a][:, pl.ds(at, tile)] = part.astype(out_refs[a].dtype)

        for k in range(kinds):
            for a in range(cores):
                for s in range(n_pipe):
                    start = pl.multiple_of((p ^ s) * from_rows, from_rows)
                    place, row = pieces[s][a]
                    natural[pl.ds(start, from_rows), :] = x_refs[place][
                        k, row : row + from_rows, :
                    ]
                for s in range(n_tensor):
                    start = pl.multiple_of((t ^ s) * to_rows, to_rows)
                    at = a * tokens + s * to_rows
                    ordered[k, at : at + to_rows, :] = natural[pl.ds(start, to_rows), :]
        stream(count, copies, work)

    window_shape = (tile, units) if transposed else (units, tile)
    return pl.pallas_call(
        kernel,
        in_specs=[IN_VMEM] * n_in + [IN_PLACE] * (kinds + n_after),
        out_specs=[IN_VMEM] * cores,
        out_shape=[
            jax.ShapeDtypeStruct((tokens, width), BF16 if a else F32) for a in range(cores)
        ],
        scratch_shapes=[
            pltpu.VMEM((tokens, units), BF16),
            pltpu.VMEM((kinds, cores * tokens, units), BF16),
            pltpu.VMEM((kinds, count) + window_shape, BF16),
            pltpu.SemaphoreType.DMA((kinds, count)),
        ],
        compiler_params=params(),
        cost_estimate=cost(2 * cores * tokens * units * width * kinds, 2 * units * width * kinds),
        name="input_grad" if transposed else "layer_output",
    )(*blocks, *weights, *after)


def gather_first(value, n_tensor):
    return [exchange(value, "tensor", n_tensor, s) for s in range(n_tensor - 1, 0, -1)] + [value]


def gather_tokens(own, cores, n_tensor, after=()):
    rows, width = own[0].shape

    def body(ins, outs):
        t = lax.axis_index("tensor")
        for s, ref in zip(range(n_tensor - 1, -1, -1), ins):
            start = pl.multiple_of((t ^ s) * rows, rows)
            outs[0][pl.ds(start, rows), :] = ref[...]

    (own,) = small_kernel(body, [((rows * n_tensor, width), BF16)], own, "assemble", after)
    if cores == 1:
        return [own]
    return [own, exchange(own, "dp", cores, 1)]


def finish(partials, cores, n_tensor, after=()):
    if cores > 1:
        other = exchange(partials[1], "dp", cores, 1)
        rows, width = other.shape[0] // n_tensor, other.shape[1]

        def body(ins, outs):
            for s in range(n_tensor):
                at = slice(s * rows, (s + 1) * rows)
                outs[s][...] = (ins[0][at] + ins[1][at].astype(F32)).astype(outs[s].dtype)

        parts = small_kernel(
            body,
            [((rows, width), BF16 if s else F32) for s in range(n_tensor)],
            [partials[0], other],
            "add_core",
            after,
        )
    else:
        rows = partials[0].shape[0] // n_tensor
        parts = [
            partials[0][s * rows : (s + 1) * rows].astype(BF16 if s else F32)
            for s in range(n_tensor)
        ]

    came = [exchange(parts[s], "tensor", n_tensor, s) for s in range(1, n_tensor)]
    total = parts[0]
    for value in came:
        total = total + value.astype(F32)
    return came, total.astype(BF16)


def slope_values(grad, gate, up):
    gate, up = gate.astype(F32), up.astype(F32)
    sigma = jax.nn.sigmoid(gate)
    gate_slope = (grad * up * sigma * (1.0 + gate * (1.0 - sigma))).astype(BF16)
    up_slope = (grad * gate * sigma).astype(BF16)
    return gate_slope, up_slope


def direct(
    n_pipe, n_tensor, forward_acts, backward_grad, stored_gate, stored_up, gate_weight, up_weight, down_weight
):
    layout = [(BF16 if s else F32, [(s, 0)]) for s in range(n_pipe)]
    pieces = [[(s, 0)] for s in range(n_pipe)]

    def total_of(parts):
        total = parts[0]
        for s in range(1, n_pipe):
            total = total + exchange(parts[s], "pipe", n_pipe, s).astype(F32)
        return total

    def gather(value):
        return [value] + [exchange(value, "pipe", n_pipe, s) for s in range(1, n_pipe)]

    grads = gather_tokens(gather_first(backward_grad, n_tensor), 1, n_tensor)
    acts = gather_tokens(gather_first(forward_acts, n_tensor), 1, n_tensor)
    grad = total_of(project(grads, [down_weight], True, layout, n_pipe))[0]
    slopes = gather(jnp.stack(slope_values(grad, stored_gate, stored_up)))
    summed = total_of(project(acts, [gate_weight, up_weight], False, layout, n_pipe))
    hidden = gather((jax.nn.silu(summed[:1]) * summed[1:]).astype(BF16))
    back = contract(slopes, pieces, [gate_weight, up_weight], True, 1, n_pipe, n_tensor)
    out = contract(hidden, pieces, [down_weight], False, 1, n_pipe, n_tensor)
    return finish(out, 1, n_tensor)[1], finish(back, 1, n_tensor)[1]


def balanced(
    n_tensor, forward_acts, backward_grad, stored_gate, stored_up, gate_weight, up_weight, down_weight
):
    cores, n_pipe, x, y = 2, 4, 1, 2
    units = gate_weight.shape[1] // cores
    rows = stored_gate.shape[0]
    layout = [
        (F32, [(0, 0), (0, 1), (1, 1), (2, 0)]),
        (BF16, [(3, 0), (1, 0)]),
        (BF16, [(3, 1), (2, 1)]),
    ]
    pieces = [[(0, 0), (0, rows)], [(1, 0), (1, rows)], [(2, 0), (2, rows)], [(3, 0), (4, 0)]]

    def swap(value, step):
        return exchange(value, "pipe", n_pipe, step)

    def sum_first(parts, after=()):
        local, for_x, for_y = parts
        from_x, from_y = swap(for_x, x), swap(for_y, y)
        kinds = local.shape[0]

        def body(ins, outs):
            keep, came_x, came_y = ins
            for k in range(kinds):
                outs[0][k] = (
                    keep[k, 2 * rows : 3 * rows] + came_y[k, :rows].astype(F32)
                ).astype(BF16)
                outs[1][k] = (
                    keep[k, 3 * rows : 4 * rows] + came_x[k, :rows].astype(F32)
                ).astype(BF16)

        on_x, on_y = small_kernel(
            body, [((kinds, rows, units), BF16)] * 2, [local, from_x, from_y], "pass_on", after
        )
        return on_x, [local, from_x, from_y, swap(on_x, x), swap(on_y, y)]

    def totals(keep, came_x, came_y, then_x, then_y, k):
        first = keep[k, :rows] + came_x[k, rows:].astype(F32) + then_y[k].astype(F32)
        second = keep[k, rows : 2 * rows] + came_y[k, rows:].astype(F32) + then_x[k].astype(F32)
        return first, second

    def gather_near(value):
        return swap(value, x), swap(value, y)

    def gather_far(value, from_x, from_y):
        return [value, from_x, from_y, swap(from_x[:, :rows], y), swap(from_y[:, rows:], x)]

    core = lax.axis_index("dp")
    stored = jnp.stack([stored_gate, stored_up])
    mine = lax.dynamic_slice_in_dim(stored, core * units, units, 2)
    other = exchange(lax.dynamic_slice_in_dim(stored, (1 - core) * units, units, 2), "dp", cores, 1)

    grads = gather_tokens(gather_first(backward_grad, n_tensor), cores, n_tensor)
    forward_acts, _ = lax.optimization_barrier((forward_acts, grads[0]))
    acts = gather_first(forward_acts, n_tensor)
    parts = project(grads, [down_weight], True, layout, n_pipe)
    passed, sums = sum_first(parts)

    def slopes_body(ins, outs):
        for a, grad in enumerate(totals(*ins[:5], 0)):
            gate_slope, up_slope = slope_values(grad, ins[5 + a][0], ins[5 + a][1])
            outs[0][0, a * rows : (a + 1) * rows] = gate_slope
            outs[0][1, a * rows : (a + 1) * rows] = up_slope

    (slopes,) = small_kernel(
        slopes_body, [((2, cores * rows, units), BF16)], [*sums, mine, other], "slopes"
    )
    slopes_x, slopes_y = gather_near(slopes)

    acts = gather_tokens(acts, cores, n_tensor, after=[slopes])
    parts = project(
        acts, [gate_weight, up_weight], False, layout, n_pipe
    )
    slopes_all = gather_far(slopes, slopes_x, slopes_y)
    passed, sums = sum_first(parts)

    def hidden_body(ins, outs):
        gates, ups = totals(*ins, 0), totals(*ins, 1)
        for a in range(cores):
            outs[0][0, a * rows : (a + 1) * rows] = (jax.nn.silu(gates[a]) * ups[a]).astype(BF16)

    (hidden,) = small_kernel(hidden_body, [((1, cores * rows, units), BF16)], sums, "hidden")
    hidden_x, hidden_y = gather_near(hidden)

    back = contract(
        slopes_all,
        pieces,
        [gate_weight, up_weight],
        True,
        cores,
        n_pipe,
        n_tensor,
        after=[passed],
    )
    back_came, input_grad = finish(back, cores, n_tensor)
    hidden_all = gather_far(hidden, hidden_x, hidden_y)
    out = contract(
        hidden_all, pieces, [down_weight], False, cores, n_pipe, n_tensor, after=back_came[:2]
    )
    _, layer_output = finish(out, cores, n_tensor)
    return layer_output, input_grad


def solution(mesh):
    in_specs = (
        P(("dp", "tensor"), "pipe"),
        P(("dp", "tensor"), "pipe"),
        P(("dp", "pipe"), "tensor"),
        P(("dp", "pipe"), "tensor"),
        P("pipe", "tensor"),
        P("pipe", "tensor"),
        P("tensor", "pipe"),
    )
    out_specs = (P(("dp", "tensor"), "pipe"), P(("dp", "tensor"), "pipe"))

    def whole(*args):
        n_pipe, n_tensor = mesh.shape["pipe"], mesh.shape["tensor"]
        hidden_width = args[4].shape[1] // n_tensor
        if mesh.shape["dp"] == 2 and n_pipe == 4 and hidden_width % 256 == 0:
            body = functools.partial(balanced, n_tensor)
        else:
            body = functools.partial(direct, n_pipe, n_tensor)
        return jax.shard_map(
            body, mesh=mesh, in_specs=in_specs, out_specs=out_specs, check_vma=False
        )(*args)

    return whole
```

```python
import functools

import jax
import jax.numpy as jnp
from jax import lax
from jax.experimental import pallas as pl
from jax.experimental.pallas import tpu as pltpu
from jax.sharding import PartitionSpec as P

F32 = jnp.float32
BF16 = jnp.bfloat16
VMEM_BYTES = 40 * 1024 * 1024
CONTRACT_LAST = (((1,), (1,)), ((), ()))
AHEAD = 6
IN_VMEM = pl.BlockSpec(memory_space=pltpu.VMEM)
IN_PLACE = pl.BlockSpec(memory_space=pl.ANY)


def exchange(value, axis, size, step):
    return lax.ppermute(value, axis, [(i, i ^ step) for i in range(size)])


def pick_tile(width):
    return 256 if width % 256 == 0 else 128


def cost(flops, moved):
    return pl.CostEstimate(flops=flops, bytes_accessed=moved, transcendentals=0)


def params():
    return pltpu.CompilerParams(vmem_limit_bytes=VMEM_BYTES)


def stream(count, copies, prepare, work):
    for j in range(min(AHEAD, count)):
        for copy in copies(j):
            copy.start()
    prepare()

    def step(j, carry):
        @pl.when(j + AHEAD < count)
        def _():
            for copy in copies(j + AHEAD):
                copy.start()

        for copy in copies(j):
            copy.wait()
        work(j)
        return carry

    lax.fori_loop(0, count, step, 0)


def small_kernel(body, outs, inputs, name, after=()):
    n_in, n_after = len(inputs), len(after)

    def kernel(*refs):
        body(refs[:n_in], refs[n_in + n_after :])

    moved = sum(a.size * a.dtype.itemsize for a in inputs)
    return pl.pallas_call(
        kernel,
        in_specs=[IN_VMEM] * n_in + [IN_PLACE] * n_after,
        out_specs=[IN_VMEM] * len(outs),
        out_shape=[jax.ShapeDtypeStruct(shape, dtype) for shape, dtype in outs],
        cost_estimate=cost(moved, moved),
        compiler_params=pltpu.CompilerParams(vmem_limit_bytes=VMEM_BYTES // 2),
        name=name,
    )(*inputs, *after)


def project(inputs, weights, transposed, layout, n_pipe, after=()):
    cores = len(inputs)
    flat = [x for pair in inputs for x in pair]
    n_in, n_after, n_out, kinds = len(flat), len(after), len(layout), len(weights)
    block, depth = inputs[0][0].shape
    tokens = block + inputs[0][1].shape[0]
    units = (weights[0].shape[0] if transposed else weights[0].shape[1]) // cores
    tile = pick_tile(units)
    count = units // tile
    rows = tokens // n_pipe
    places = [piece for _, pieces in layout for piece in pieces]

    def kernel(*refs):
        x_refs = refs[:n_in]
        w_refs = refs[n_in : n_in + kinds]
        out_refs = refs[n_in + kinds + n_after : n_in + kinds + n_after + n_out]
        natural, ordered, held, sems, own_sems = refs[n_in + kinds + n_after + n_out :]
        t = lax.axis_index("tensor")
        p = lax.axis_index("pipe")
        first = lax.axis_index("dp") * units if cores > 1 else 0

        def copies(j):
            at = pl.multiple_of(first + j * tile, tile)
            window = (pl.ds(at, tile), slice(None)) if transposed else (slice(None), pl.ds(at, tile))
            return [
                pltpu.make_async_copy(w_refs[k].at[window], held.at[k, j], sems.at[k, j])
                for k in range(kinds)
            ]

        def work(j):
            at = pl.multiple_of(j * tile, tile)
            for k in range(kinds):
                if transposed:
                    total = lax.dot_general(
                        ordered[...], held[k, j], CONTRACT_LAST, preferred_element_type=F32
                    )
                else:
                    total = jnp.dot(ordered[...], held[k, j], preferred_element_type=F32)
                row = 0
                for ref in out_refs:
                    size = ref.shape[1]
                    ref[k, :, pl.ds(at, tile)] = total[row : row + size].astype(ref.dtype)
                    row += size

        def place(a, s):
            return pl.ds(pl.multiple_of(a * tokens + (t ^ s) * block, block), block)

        own = [
            pltpu.make_async_copy(x_refs[2 * a], natural.at[place(a, 0)], own_sems.at[a])
            for a in range(cores)
        ]

        def prepare():
            for a in range(cores):
                for s in range(1, tokens // block):
                    natural[place(a, s), :] = x_refs[2 * a + 1][(s - 1) * block : s * block, :]
            for copy in own:
                copy.wait()
            for i, (s, a) in enumerate(places):
                start = pl.multiple_of(a * tokens + (p ^ s) * rows, rows)
                ordered[i * rows : (i + 1) * rows, :] = natural[pl.ds(start, rows), :]

        for copy in own:
            copy.start()
        stream(count, copies, prepare, work)

    window_shape = (tile, depth) if transposed else (depth, tile)
    return pl.pallas_call(
        kernel,
        in_specs=[IN_PLACE, IN_VMEM] * cores + [IN_PLACE] * (kinds + n_after),
        out_specs=[IN_VMEM] * n_out,
        out_shape=[
            jax.ShapeDtypeStruct((kinds, len(pieces) * rows, units), dtype)
            for dtype, pieces in layout
        ],
        scratch_shapes=[
            pltpu.VMEM((cores * tokens, depth), BF16),
            pltpu.VMEM((cores * tokens, depth), BF16),
            pltpu.VMEM((kinds, count) + window_shape, BF16),
            pltpu.SemaphoreType.DMA((kinds, count)),
            pltpu.SemaphoreType.DMA((cores,)),
        ],
        compiler_params=params(),
        cost_estimate=cost(2 * cores * tokens * depth * units * kinds, 2 * depth * units * kinds),
        name="pull_back" if transposed else "project",
    )(*flat, *weights, *after)


def contract(blocks, pieces, weights, transposed, cores, n_pipe, n_tensor, after=()):
    kinds, _, units = blocks[0].shape
    n_in, n_after = len(blocks), len(after)
    from_rows = blocks[0].shape[1] // cores
    tokens = from_rows * n_pipe
    to_rows = tokens // n_tensor
    width = weights[0].shape[0] if transposed else weights[0].shape[1]
    tile = pick_tile(width)
    count = width // tile

    def kernel(*refs):
        x_refs = refs[:n_in]
        w_refs = refs[n_in : n_in + kinds]
        out_refs = refs[n_in + kinds + n_after : n_in + kinds + n_after + cores]
        natural, ordered, held, sems = refs[n_in + kinds + n_after + cores :]
        t = lax.axis_index("tensor")
        p = lax.axis_index("pipe")
        first = pl.multiple_of(lax.axis_index("dp") * units, units) if cores > 1 else 0

        def copies(j):
            at = pl.multiple_of(j * tile, tile)
            window = (
                (pl.ds(at, tile), pl.ds(first, units))
                if transposed
                else (pl.ds(first, units), pl.ds(at, tile))
            )
            return [
                pltpu.make_async_copy(w_refs[k].at[window], held.at[k, j], sems.at[k, j])
                for k in range(kinds)
            ]

        def work(j):
            at = pl.multiple_of(j * tile, tile)
            total = None
            for k in range(kinds):
                if transposed:
                    part = lax.dot_general(
                        ordered[k], held[k, j], CONTRACT_LAST, preferred_element_type=F32
                    )
                else:
                    part = jnp.dot(ordered[k], held[k, j], preferred_element_type=F32)
                total = part if total is None else total + part
            for a in range(cores):
                part = total[a * tokens : (a + 1) * tokens]
                out_refs[a][:, pl.ds(at, tile)] = part.astype(out_refs[a].dtype)

        def prepare():
            for k in range(kinds):
                for a in range(cores):
                    for s in range(n_pipe):
                        start = pl.multiple_of((p ^ s) * from_rows, from_rows)
                        place, row = pieces[s][a]
                        natural[pl.ds(start, from_rows), :] = x_refs[place][
                            k, row : row + from_rows, :
                        ]
                    for s in range(n_tensor):
                        start = pl.multiple_of((t ^ s) * to_rows, to_rows)
                        at = a * tokens + s * to_rows
                        ordered[k, at : at + to_rows, :] = natural[pl.ds(start, to_rows), :]

        stream(count, copies, prepare, work)

    window_shape = (tile, units) if transposed else (units, tile)
    return pl.pallas_call(
        kernel,
        in_specs=[IN_VMEM] * n_in + [IN_PLACE] * (kinds + n_after),
        out_specs=[IN_VMEM] * cores,
        out_shape=[
            jax.ShapeDtypeStruct((tokens, width), BF16 if a else F32) for a in range(cores)
        ],
        scratch_shapes=[
            pltpu.VMEM((tokens, units), BF16),
            pltpu.VMEM((kinds, cores * tokens, units), BF16),
            pltpu.VMEM((kinds, count) + window_shape, BF16),
            pltpu.SemaphoreType.DMA((kinds, count)),
        ],
        compiler_params=params(),
        cost_estimate=cost(2 * cores * tokens * units * width * kinds, 2 * units * width * kinds),
        name="input_grad" if transposed else "layer_output",
    )(*blocks, *weights, *after)


def gather_first(value, cores, n_tensor):
    steps = range(1, n_tensor)
    came = {s: exchange(value, "tensor", n_tensor, s) for s in reversed(steps)}
    other = [exchange(value, "dp", cores, 1)] if cores > 1 else []
    return [value] + other, [came[s] for s in steps]


def gather_tokens(first, cores, after=()):
    blocks, came = first
    rows, width = came[0].shape

    def body(ins, outs):
        for s, ref in enumerate(ins):
            outs[0][s * rows : (s + 1) * rows, :] = ref[...]

    (rest,) = small_kernel(body, [((rows * len(came), width), BF16)], came, "assemble", after)
    others = [exchange(rest, "dp", cores, 1)] if cores > 1 else []
    return list(zip(blocks, [rest] + others))


def finish(partials, cores, n_tensor, after=()):
    if cores > 1:
        other = exchange(partials[1], "dp", cores, 1)
        rows, width = other.shape[0] // n_tensor, other.shape[1]

        def body(ins, outs):
            for s in range(n_tensor):
                at = slice(s * rows, (s + 1) * rows)
                outs[s][...] = (ins[0][at] + ins[1][at].astype(F32)).astype(outs[s].dtype)

        parts = small_kernel(
            body,
            [((rows, width), BF16 if s else F32) for s in range(n_tensor)],
            [partials[0], other],
            "add_core",
            after,
        )
    else:
        rows = partials[0].shape[0] // n_tensor
        parts = [
            partials[0][s * rows : (s + 1) * rows].astype(BF16 if s else F32)
            for s in range(n_tensor)
        ]

    came = [exchange(parts[s], "tensor", n_tensor, s) for s in range(1, n_tensor)]
    total = parts[0]
    for value in came:
        total = total + value.astype(F32)
    return came, total.astype(BF16)


def slope_values(grad, gate, up):
    gate, up = gate.astype(F32), up.astype(F32)
    sigma = jax.nn.sigmoid(gate)
    gate_slope = (grad * up * sigma * (1.0 + gate * (1.0 - sigma))).astype(BF16)
    up_slope = (grad * gate * sigma).astype(BF16)
    return gate_slope, up_slope


def direct(
    n_pipe, n_tensor, forward_acts, backward_grad, stored_gate, stored_up, gate_weight, up_weight, down_weight
):
    layout = [(BF16 if s else F32, [(s, 0)]) for s in range(n_pipe)]
    pieces = [[(s, 0)] for s in range(n_pipe)]

    def total_of(parts):
        total = parts[0]
        for s in range(1, n_pipe):
            total = total + exchange(parts[s], "pipe", n_pipe, s).astype(F32)
        return total

    def gather(value):
        return [value] + [exchange(value, "pipe", n_pipe, s) for s in range(1, n_pipe)]

    grads = gather_tokens(gather_first(backward_grad, 1, n_tensor), 1)
    acts = gather_tokens(gather_first(forward_acts, 1, n_tensor), 1)
    grad = total_of(project(grads, [down_weight], True, layout, n_pipe))[0]
    slopes = gather(jnp.stack(slope_values(grad, stored_gate, stored_up)))
    summed = total_of(project(acts, [gate_weight, up_weight], False, layout, n_pipe))
    hidden = gather((jax.nn.silu(summed[:1]) * summed[1:]).astype(BF16))
    back = contract(slopes, pieces, [gate_weight, up_weight], True, 1, n_pipe, n_tensor)
    out = contract(hidden, pieces, [down_weight], False, 1, n_pipe, n_tensor)
    return finish(out, 1, n_tensor)[1], finish(back, 1, n_tensor)[1]


def balanced(
    n_tensor, forward_acts, backward_grad, stored_gate, stored_up, gate_weight, up_weight, down_weight
):
    cores, n_pipe, x, y = 2, 4, 1, 2
    units = gate_weight.shape[1] // cores
    rows = stored_gate.shape[0]
    straight = [(BF16 if s else F32, [(s, 0), (s, 1)]) for s in range(n_pipe)]
    balanced_layout = [
        (F32, [(0, 0), (0, 1), (1, 1), (2, 0)]),
        (BF16, [(3, 0), (1, 0)]),
        (BF16, [(3, 1), (2, 1)]),
    ]
    straight_pieces = [[(s, 0), (s, rows)] for s in range(n_pipe)]
    balanced_pieces = straight_pieces[:3] + [[(3, 0), (4, 0)]]

    def swap(value, step):
        return exchange(value, "pipe", n_pipe, step)

    def slopes_body(ins, outs):
        keep, came = ins[0], ins[1:n_pipe]
        for a in range(cores):
            at = slice(a * rows, (a + 1) * rows)
            grad = keep[0, at]
            for ref in came:
                grad = grad + ref[0, at].astype(F32)
            gate_slope, up_slope = slope_values(grad, ins[n_pipe + a][0], ins[n_pipe + a][1])
            outs[0][0, at] = gate_slope
            outs[0][1, at] = up_slope

    def pass_on_body(ins, outs):
        keep, came_x, came_y = ins
        for k in range(2):
            on_x = keep[k, 2 * rows : 3 * rows] + came_y[k, :rows].astype(F32)
            on_y = keep[k, 3 * rows : 4 * rows] + came_x[k, :rows].astype(F32)
            outs[0][k] = on_x.astype(BF16)
            outs[1][k] = on_y.astype(BF16)

    def hidden_body(ins, outs):
        keep, came_x, came_y, then_x, then_y = ins
        for a, near, far in ((0, came_x, then_y), (1, came_y, then_x)):
            at = slice(a * rows, (a + 1) * rows)
            gate, up = [
                keep[k, at] + near[k, rows:].astype(F32) + far[k].astype(F32) for k in range(2)
            ]
            outs[0][0, at] = (jax.nn.silu(gate) * up).astype(BF16)

    core = lax.axis_index("dp")
    stored = jnp.stack([stored_gate, stored_up])
    mine = lax.dynamic_slice_in_dim(stored, core * units, units, 2)
    other = exchange(lax.dynamic_slice_in_dim(stored, (1 - core) * units, units, 2), "dp", cores, 1)

    acts = gather_first(forward_acts, cores, n_tensor)
    grads = gather_first(backward_grad, cores, n_tensor)
    acts = gather_tokens(acts, cores, after=[other, acts[0][1]])
    keep, for_x, for_y = project(
        acts, [gate_weight, up_weight], False, balanced_layout, n_pipe, after=[grads[0][1]]
    )
    came_x, came_y = swap(for_x, x), swap(for_y, y)

    grads = gather_tokens(grads, cores, after=[keep])
    parts = project(grads, [down_weight], True, straight, n_pipe)
    parts = [parts[0]] + [swap(parts[s], s) for s in (3, 1, 2)]

    half = ((2, rows, units), BF16)
    on_x, on_y = small_kernel(
        pass_on_body, [half, half], [keep, came_x, came_y], "pass_on", after=[parts[0]]
    )
    sums = [keep, came_x, came_y, swap(on_x, x), swap(on_y, y)]
    (hidden,) = small_kernel(hidden_body, [((1, cores * rows, units), BF16)], sums, "hidden")
    hidden_all = [hidden] + [swap(hidden, s) for s in range(1, n_pipe)]

    (slopes,) = small_kernel(
        slopes_body,
        [((2, cores * rows, units), BF16)],
        [*parts, mine, other],
        "slopes",
        after=[hidden],
    )
    slopes_x, slopes_y = swap(slopes, x), swap(slopes, y)

    out = contract(
        hidden_all, straight_pieces, [down_weight], False, cores, n_pipe, n_tensor, after=[slopes]
    )
    slopes_all = [
        slopes,
        slopes_x,
        slopes_y,
        swap(slopes_x[:, :rows], y),
        swap(slopes_y[:, rows:], x),
    ]
    came, layer_output = finish(out, cores, n_tensor)
    back = contract(
        slopes_all,
        balanced_pieces,
        [gate_weight, up_weight],
        True,
        cores,
        n_pipe,
        n_tensor,
        after=came[:2],
    )
    _, input_grad = finish(back, cores, n_tensor)
    return layer_output, input_grad


def solution(mesh):
    in_specs = (
        P(("dp", "tensor"), "pipe"),
        P(("dp", "tensor"), "pipe"),
        P(("dp", "pipe"), "tensor"),
        P(("dp", "pipe"), "tensor"),
        P("pipe", "tensor"),
        P("pipe", "tensor"),
        P("tensor", "pipe"),
    )
    out_specs = (P(("dp", "tensor"), "pipe"), P(("dp", "tensor"), "pipe"))

    def whole(*args):
        n_pipe, n_tensor = mesh.shape["pipe"], mesh.shape["tensor"]
        hidden_width = args[4].shape[1] // n_tensor
        if mesh.shape["dp"] == 2 and n_pipe == 4 and hidden_width % 256 == 0:
            body = functools.partial(balanced, n_tensor)
        else:
            body = functools.partial(direct, n_pipe, n_tensor)
        return jax.shard_map(
            body, mesh=mesh, in_specs=in_specs, out_specs=out_specs, check_vma=False
        )(*args)

    return whole
```

```python
import functools

import jax
import jax.numpy as jnp
from jax import lax
from jax.experimental import pallas as pl
from jax.experimental.pallas import tpu as pltpu
from jax.sharding import PartitionSpec as P

F32 = jnp.float32
BF16 = jnp.bfloat16
VMEM_BYTES = 40 * 1024 * 1024
CONTRACT_LAST = (((1,), (1,)), ((), ()))
AHEAD = 6
IN_VMEM = pl.BlockSpec(memory_space=pltpu.VMEM)
IN_PLACE = pl.BlockSpec(memory_space=pl.ANY)


def exchange(value, axis, size, step):
    return lax.ppermute(value, axis, [(i, i ^ step) for i in range(size)])


def pick_tile(width):
    return 256 if width % 256 == 0 else 128


def cost(flops, moved):
    return pl.CostEstimate(flops=flops, bytes_accessed=moved, transcendentals=0)


def params():
    return pltpu.CompilerParams(vmem_limit_bytes=VMEM_BYTES)


def stream(count, copies, prepare, work):
    for j in range(min(AHEAD, count)):
        for copy in copies(j):
            copy.start()
    prepare()

    def step(j, carry):
        @pl.when(j + AHEAD < count)
        def _():
            for copy in copies(j + AHEAD):
                copy.start()

        for copy in copies(j):
            copy.wait()
        work(j)
        return carry

    lax.fori_loop(0, count, step, 0)


def small_kernel(body, outs, inputs, name, after=()):
    n_in, n_after = len(inputs), len(after)

    def kernel(*refs):
        body(refs[:n_in], refs[n_in + n_after :])

    moved = sum(a.size * a.dtype.itemsize for a in inputs)
    return pl.pallas_call(
        kernel,
        in_specs=[IN_VMEM] * n_in + [IN_PLACE] * n_after,
        out_specs=[IN_VMEM] * len(outs),
        out_shape=[jax.ShapeDtypeStruct(shape, dtype) for shape, dtype in outs],
        cost_estimate=cost(moved, moved),
        compiler_params=pltpu.CompilerParams(vmem_limit_bytes=VMEM_BYTES // 2),
        name=name,
    )(*inputs, *after)


def project(inputs, weights, transposed, layout, n_pipe, after=()):
    cores = len(inputs)
    flat = [x for own, _, rest in inputs for x in (own, rest)]
    n_in, n_after, n_out, kinds = len(flat), len(after), len(layout), len(weights)
    block = inputs[0][0].shape[0]
    tokens, depth = block + inputs[0][2].shape[0], inputs[0][2].shape[1]
    units = (weights[0].shape[0] if transposed else weights[0].shape[1]) // cores
    tile = pick_tile(units)
    count = units // tile
    rows = tokens // n_pipe
    places = [piece for _, pieces in layout for piece in pieces]

    def kernel(*refs):
        x_refs = refs[:n_in]
        w_refs = refs[n_in : n_in + kinds]
        out_refs = refs[n_in + kinds + n_after : n_in + kinds + n_after + n_out]
        natural, ordered, held, sems = refs[n_in + kinds + n_after + n_out :]
        t = lax.axis_index("tensor")
        p = lax.axis_index("pipe")
        first = lax.axis_index("dp") * units if cores > 1 else 0

        def copies(j):
            at = pl.multiple_of(first + j * tile, tile)
            window = (pl.ds(at, tile), slice(None)) if transposed else (slice(None), pl.ds(at, tile))
            return [
                pltpu.make_async_copy(w_refs[k].at[window], held.at[k, j], sems.at[k, j])
                for k in range(kinds)
            ]

        def work(j):
            at = pl.multiple_of(j * tile, tile)
            for k in range(kinds):
                if transposed:
                    total = lax.dot_general(
                        ordered[...], held[k, j], CONTRACT_LAST, preferred_element_type=F32
                    )
                else:
                    total = jnp.dot(ordered[...], held[k, j], preferred_element_type=F32)
                row = 0
                for ref in out_refs:
                    size = ref.shape[1]
                    ref[k, :, pl.ds(at, tile)] = total[row : row + size].astype(ref.dtype)
                    row += size

        def place(a, s):
            return pl.ds(pl.multiple_of(a * tokens + (t ^ s) * block, block), block)

        def prepare():
            for a in range(cores):
                column = inputs[a][1]
                natural[place(a, 0), :] = x_refs[2 * a][:, column : column + depth]
                for s in range(1, tokens // block):
                    natural[place(a, s), :] = x_refs[2 * a + 1][(s - 1) * block : s * block, :]
            for i, (s, a) in enumerate(places):
                start = pl.multiple_of(a * tokens + (p ^ s) * rows, rows)
                ordered[i * rows : (i + 1) * rows, :] = natural[pl.ds(start, rows), :]

        stream(count, copies, prepare, work)

    window_shape = (tile, depth) if transposed else (depth, tile)
    return pl.pallas_call(
        kernel,
        in_specs=[IN_VMEM] * n_in + [IN_PLACE] * (kinds + n_after),
        out_specs=[IN_VMEM] * n_out,
        out_shape=[
            jax.ShapeDtypeStruct((kinds, len(pieces) * rows, units), dtype)
            for dtype, pieces in layout
        ],
        scratch_shapes=[
            pltpu.VMEM((cores * tokens, depth), BF16),
            pltpu.VMEM((cores * tokens, depth), BF16),
            pltpu.VMEM((kinds, count) + window_shape, BF16),
            pltpu.SemaphoreType.DMA((kinds, count)),
        ],
        compiler_params=params(),
        cost_estimate=cost(0, 0) if transposed else cost(2 * cores * tokens * depth * units * kinds, 2 * depth * units * kinds),
        name="pull_back" if transposed else "project",
    )(*flat, *weights, *after)


def contract(blocks, pieces, weights, transposed, cores, n_pipe, n_tensor, after=()):
    kinds, _, units = blocks[0].shape
    n_in, n_after = len(blocks), len(after)
    from_rows = blocks[0].shape[1] // cores
    tokens = from_rows * n_pipe
    to_rows = tokens // n_tensor
    width = weights[0].shape[0] if transposed else weights[0].shape[1]
    tile = pick_tile(width)
    count = width // tile

    def kernel(*refs):
        x_refs = refs[:n_in]
        w_refs = refs[n_in : n_in + kinds]
        out_refs = refs[n_in + kinds + n_after : n_in + kinds + n_after + cores]
        natural, ordered, held, sems = refs[n_in + kinds + n_after + cores :]
        t = lax.axis_index("tensor")
        p = lax.axis_index("pipe")
        first = pl.multiple_of(lax.axis_index("dp") * units, units) if cores > 1 else 0

        def copies(j):
            at = pl.multiple_of(j * tile, tile)
            window = (
                (pl.ds(at, tile), pl.ds(first, units))
                if transposed
                else (pl.ds(first, units), pl.ds(at, tile))
            )
            return [
                pltpu.make_async_copy(w_refs[k].at[window], held.at[k, j], sems.at[k, j])
                for k in range(kinds)
            ]

        def work(j):
            at = pl.multiple_of(j * tile, tile)
            total = None
            for k in range(kinds):
                if transposed:
                    part = lax.dot_general(
                        ordered[k], held[k, j], CONTRACT_LAST, preferred_element_type=F32
                    )
                else:
                    part = jnp.dot(ordered[k], held[k, j], preferred_element_type=F32)
                total = part if total is None else total + part
            for a in range(cores):
                part = total[a * tokens : (a + 1) * tokens]
                out_refs[a][:, pl.ds(at, tile)] = part.astype(out_refs[a].dtype)

        def prepare():
            for k in range(kinds):
                for a in range(cores):
                    for s in range(n_pipe):
                        start = pl.multiple_of((p ^ s) * from_rows, from_rows)
                        place, row = pieces[s][a]
                        natural[pl.ds(start, from_rows), :] = x_refs[place][
                            k, row : row + from_rows, :
                        ]
                    for s in range(n_tensor):
                        start = pl.multiple_of((t ^ s) * to_rows, to_rows)
                        at = a * tokens + s * to_rows
                        ordered[k, at : at + to_rows, :] = natural[pl.ds(start, to_rows), :]

        stream(count, copies, prepare, work)

    window_shape = (tile, units) if transposed else (units, tile)
    return pl.pallas_call(
        kernel,
        in_specs=[IN_VMEM] * n_in + [IN_PLACE] * (kinds + n_after),
        out_specs=[IN_VMEM] * cores,
        out_shape=[
            jax.ShapeDtypeStruct((tokens, width), BF16 if a else F32) for a in range(cores)
        ],
        scratch_shapes=[
            pltpu.VMEM((tokens, units), BF16),
            pltpu.VMEM((kinds, cores * tokens, units), BF16),
            pltpu.VMEM((kinds, count) + window_shape, BF16),
            pltpu.SemaphoreType.DMA((kinds, count)),
        ],
        compiler_params=params(),
        cost_estimate=cost(2 * cores * tokens * units * width * kinds, 2 * units * width * kinds),
        name="input_grad" if transposed else "layer_output",
    )(*blocks, *weights, *after)


def gather_first(value, n_tensor):
    came = {s: exchange(value, "tensor", n_tensor, s) for s in range(n_tensor - 1, 0, -1)}
    return [came[s] for s in range(1, n_tensor)]


def gather_tokens(owns, came, after=()):
    rows, width = came[0].shape

    def body(ins, outs):
        for s, ref in enumerate(ins):
            outs[0][s * rows : (s + 1) * rows, :] = ref[...]

    (rest,) = small_kernel(body, [((rows * len(came), width), BF16)], came, "assemble", after)
    rests = [rest] + [exchange(rest, "dp", 2, 1)] * (len(owns) - 1)
    return [(own, column, rest) for (own, column), rest in zip(owns, rests)]


def finish(partials, cores, n_tensor, after=()):
    if cores > 1:
        other = exchange(partials[1], "dp", cores, 1)
        rows, width = other.shape[0] // n_tensor, other.shape[1]

        def body(ins, outs):
            for s in range(n_tensor):
                at = slice(s * rows, (s + 1) * rows)
                outs[s][...] = (ins[0][at] + ins[1][at].astype(F32)).astype(outs[s].dtype)

        parts = small_kernel(
            body,
            [((rows, width), BF16 if s else F32) for s in range(n_tensor)],
            [partials[0], other],
            "add_core",
            after,
        )
    else:
        rows = partials[0].shape[0] // n_tensor
        parts = [
            partials[0][s * rows : (s + 1) * rows].astype(BF16 if s else F32)
            for s in range(n_tensor)
        ]

    came = [exchange(parts[s], "tensor", n_tensor, s) for s in range(1, n_tensor)]
    total = parts[0]
    for value in came:
        total = total + value.astype(F32)
    return came, total.astype(BF16)


def slope_values(grad, gate, up):
    gate, up = gate.astype(F32), up.astype(F32)
    sigma = jax.nn.sigmoid(gate)
    gate_slope = (grad * up * sigma * (1.0 + gate * (1.0 - sigma))).astype(BF16)
    up_slope = (grad * gate * sigma).astype(BF16)
    return gate_slope, up_slope


def direct(
    n_pipe, n_tensor, forward_acts, backward_grad, stored_gate, stored_up, gate_weight, up_weight, down_weight
):
    layout = [(BF16 if s else F32, [(s, 0)]) for s in range(n_pipe)]
    pieces = [[(s, 0)] for s in range(n_pipe)]

    def total_of(parts):
        total = parts[0]
        for s in range(1, n_pipe):
            total = total + exchange(parts[s], "pipe", n_pipe, s).astype(F32)
        return total

    def gather(value):
        return [value] + [exchange(value, "pipe", n_pipe, s) for s in range(1, n_pipe)]

    grads = gather_tokens([(backward_grad, 0)], gather_first(backward_grad, n_tensor))
    acts = gather_tokens([(forward_acts, 0)], gather_first(forward_acts, n_tensor))
    grad = total_of(project(grads, [down_weight], True, layout, n_pipe))[0]
    slopes = gather(jnp.stack(slope_values(grad, stored_gate, stored_up)))
    summed = total_of(project(acts, [gate_weight, up_weight], False, layout, n_pipe))
    hidden = gather((jax.nn.silu(summed[:1]) * summed[1:]).astype(BF16))
    back = contract(slopes, pieces, [gate_weight, up_weight], True, 1, n_pipe, n_tensor)
    out = contract(hidden, pieces, [down_weight], False, 1, n_pipe, n_tensor)
    return finish(out, 1, n_tensor)[1], finish(back, 1, n_tensor)[1]


def balanced(
    n_tensor, forward_acts, backward_grad, stored_gate, stored_up, gate_weight, up_weight, down_weight
):
    cores, n_pipe, x, y = 2, 4, 1, 2
    units = gate_weight.shape[1] // cores
    rows = stored_gate.shape[0]
    straight = [(BF16 if s else F32, [(s, 0), (s, 1)]) for s in range(n_pipe)]
    balanced_layout = [
        (F32, [(0, 0), (0, 1), (1, 1), (2, 0)]),
        (BF16, [(3, 0), (1, 0)]),
        (BF16, [(3, 1), (2, 1)]),
    ]
    straight_pieces = [[(s, 0), (s, rows)] for s in range(n_pipe)]
    balanced_pieces = straight_pieces[:3] + [[(3, 0), (4, 0)]]

    width = forward_acts.shape[1]
    columns = [0, width, 2 * width, 2 * width + units, 2 * width + 2 * units]

    def swap(value, step):
        return exchange(value, "pipe", n_pipe, step)

    def slopes_body(ins, outs):
        keep, came = ins[0], ins[1:n_pipe]
        for a in range(cores):
            at = slice(a * rows, (a + 1) * rows)
            grad = keep[0, at]
            for ref in came:
                grad = grad + ref[0, at].astype(F32)
            stored = ins[n_pipe + a]
            gate_slope, up_slope = slope_values(
                grad, stored[:, columns[2] : columns[3]], stored[:, columns[3] :]
            )
            outs[0][0, at] = gate_slope
            outs[0][1, at] = up_slope

    def pass_on_body(ins, outs):
        keep, came_x, came_y = ins
        for k in range(2):
            on_x = keep[k, 2 * rows : 3 * rows] + came_y[k, :rows].astype(F32)
            on_y = keep[k, 3 * rows : 4 * rows] + came_x[k, :rows].astype(F32)
            outs[0][k] = on_x.astype(BF16)
            outs[1][k] = on_y.astype(BF16)

    def hidden_body(ins, outs):
        keep, came_x, came_y, then_x, then_y = ins
        for a, near, far in ((0, came_x, then_y), (1, came_y, then_x)):
            at = slice(a * rows, (a + 1) * rows)
            gate, up = [
                keep[k, at] + near[k, rows:].astype(F32) + far[k].astype(F32) for k in range(2)
            ]
            outs[0][0, at] = (jax.nn.silu(gate) * up).astype(BF16)

    acts_came = gather_first(forward_acts, n_tensor)
    grads_came = gather_first(backward_grad, n_tensor)

    def prelude_body(ins, outs):
        core = lax.axis_index("dp")
        for k in range(2):
            for c in range(cores):
                outs[c][:, columns[k] : columns[k + 1]] = ins[k][...]
                start = pl.multiple_of((core ^ c) * units, units)
                outs[c][:, columns[k + 2] : columns[k + 3]] = ins[k + 2][:, pl.ds(start, units)]

    mine, sent = small_kernel(
        prelude_body,
        [((rows, columns[-1]), BF16)] * cores,
        [forward_acts, backward_grad, stored_gate, stored_up],
        "prelude",
        after=[acts_came[0]],
    )
    other = exchange(sent, "dp", cores, 1)
    acts = gather_tokens([(mine, 0), (other, 0)], acts_came, after=[grads_came[0]])
    keep, for_x, for_y = project(
        acts, [gate_weight, up_weight], False, balanced_layout, n_pipe
    )
    came_x, came_y = swap(for_x, x), swap(for_y, y)

    grads = gather_tokens([(mine, width), (other, width)], grads_came, after=[keep])
    parts = project(grads, [down_weight], True, straight, n_pipe)
    parts = [parts[0]] + [swap(parts[s], s) for s in (3, 1, 2)]

    half = ((2, rows, units), BF16)
    on_x, on_y = small_kernel(
        pass_on_body, [half, half], [keep, came_x, came_y], "pass_on", after=[parts[0]]
    )
    sums = [keep, came_x, came_y, swap(on_x, x), swap(on_y, y)]
    (hidden,) = small_kernel(hidden_body, [((1, cores * rows, units), BF16)], sums, "hidden")
    hidden_all = [hidden] + [swap(hidden, s) for s in range(1, n_pipe)]

    (slopes,) = small_kernel(
        slopes_body,
        [((2, cores * rows, units), BF16)],
        [*parts, mine, other],
        "slopes",
        after=[hidden],
    )
    slopes_x, slopes_y = swap(slopes, x), swap(slopes, y)

    out = contract(
        hidden_all, straight_pieces, [down_weight], False, cores, n_pipe, n_tensor, after=[slopes]
    )
    slopes_all = [
        slopes,
        slopes_x,
        slopes_y,
        swap(slopes_x[:, :rows], y),
        swap(slopes_y[:, rows:], x),
    ]
    came, layer_output = finish(out, cores, n_tensor)
    back = contract(
        slopes_all,
        balanced_pieces,
        [gate_weight, up_weight],
        True,
        cores,
        n_pipe,
        n_tensor,
        after=came[:2],
    )
    _, input_grad = finish(back, cores, n_tensor)
    return layer_output, input_grad


def solution(mesh):
    in_specs = (
        P(("dp", "tensor"), "pipe"),
        P(("dp", "tensor"), "pipe"),
        P(("dp", "pipe"), "tensor"),
        P(("dp", "pipe"), "tensor"),
        P("pipe", "tensor"),
        P("pipe", "tensor"),
        P("tensor", "pipe"),
    )
    out_specs = (P(("dp", "tensor"), "pipe"), P(("dp", "tensor"), "pipe"))

    def whole(*args):
        n_pipe, n_tensor = mesh.shape["pipe"], mesh.shape["tensor"]
        hidden_width = args[4].shape[1] // n_tensor
        if mesh.shape["dp"] == 2 and n_pipe == 4 and hidden_width % 256 == 0:
            body = functools.partial(balanced, n_tensor)
        else:
            body = functools.partial(direct, n_pipe, n_tensor)
        return jax.shard_map(
            body, mesh=mesh, in_specs=in_specs, out_specs=out_specs, check_vma=False
        )(*args)

    return whole
```

```python
import functools

import jax
import jax.numpy as jnp
from jax import lax
from jax.experimental import pallas as pl
from jax.experimental.pallas import tpu as pltpu
from jax.sharding import PartitionSpec as P

F32 = jnp.float32
BF16 = jnp.bfloat16
VMEM_BYTES = 16 * 1024 * 1024
LOAD_BYTES = 24 * 1024 * 1024
CONTRACT_LAST = (((1,), (1,)), ((), ()))
IN_VMEM = pl.BlockSpec(memory_space=pltpu.VMEM)
IN_PLACE = pl.BlockSpec(memory_space=pl.ANY)


def exchange(value, axis, size, step):
    return lax.ppermute(value, axis, [(i, i ^ step) for i in range(size)])


def pick_tile(width):
    return 256 if width % 256 == 0 else 128


def cost(flops, moved):
    return pl.CostEstimate(flops=flops, bytes_accessed=moved, transcendentals=0)


def params():
    return pltpu.CompilerParams(vmem_limit_bytes=VMEM_BYTES)


def small_kernel(body, outs, inputs, name, after=()):
    n_in, n_after = len(inputs), len(after)

    def kernel(*refs):
        body(refs[:n_in], refs[n_in + n_after :])

    moved = sum(a.size * a.dtype.itemsize for a in inputs)
    return pl.pallas_call(
        kernel,
        in_specs=[IN_VMEM] * n_in + [IN_PLACE] * n_after,
        out_specs=[IN_VMEM] * len(outs),
        out_shape=[jax.ShapeDtypeStruct(shape, dtype) for shape, dtype in outs],
        cost_estimate=cost(moved, moved),
        compiler_params=params(),
        name=name,
    )(*inputs, *after)


def load_weights(gate_weight, up_weight, down_weight, cores):
    depth = gate_weight.shape[0]
    units = gate_weight.shape[1] // cores
    cuts = 4
    rows, unit_rows = depth // cuts, units // cuts

    def kernel(gate, up, down, wide, tall, sems):
        first = pl.multiple_of(lax.axis_index("dp") * units, units) if cores > 1 else 0
        copies = []
        for i in range(cuts):
            for k, ref in enumerate((gate, up)):
                at = pl.ds(i * rows, rows)
                copies.append((ref.at[at, pl.ds(first, units)], wide.at[k, at]))
        for i in range(cuts):
            at = pl.multiple_of(first + i * unit_rows, unit_rows)
            copies.append((down.at[pl.ds(at, unit_rows)], tall.at[0, pl.ds(i * unit_rows, unit_rows)]))
        copies = [
            pltpu.make_async_copy(source, target, sems.at[i])
            for i, (source, target) in enumerate(copies)
        ]
        for copy in copies:
            copy.start()
        for copy in copies:
            copy.wait()

    return pl.pallas_call(
        kernel,
        in_specs=[IN_PLACE] * 3,
        out_specs=[IN_VMEM] * 2,
        out_shape=[
            jax.ShapeDtypeStruct((2, depth, units), BF16),
            jax.ShapeDtypeStruct((1, units, depth), BF16),
        ],
        scratch_shapes=[pltpu.SemaphoreType.DMA((3 * cuts,))],
        compiler_params=pltpu.CompilerParams(vmem_limit_bytes=LOAD_BYTES),
        cost_estimate=cost(0, 6 * depth * units),
        name="load_weights",
    )(gate_weight, up_weight, down_weight)


def project(inputs, weights, transposed, layout, n_pipe, n_tensor, after=()):
    cores = len(inputs)
    flat = [x for pair in inputs for x in pair]
    n_in, n_after, n_out, kinds = len(flat), len(after), len(layout), weights.shape[0]
    block, depth = inputs[0][0].shape
    tokens = block * n_tensor
    units = weights.shape[1] if transposed else weights.shape[2]
    tile = pick_tile(units)
    count = units // tile
    rows = tokens // n_pipe
    places = [piece for _, pieces in layout for piece in pieces]

    def kernel(*refs):
        x_refs = refs[:n_in]
        held = refs[n_in]
        out_refs = refs[n_in + 1 + n_after : n_in + 1 + n_after + n_out]
        natural, ordered = refs[n_in + 1 + n_after + n_out :]
        t = lax.axis_index("tensor")
        p = lax.axis_index("pipe")

        def work(j, carry):
            at = pl.multiple_of(j * tile, tile)
            for k in range(kinds):
                if transposed:
                    total = lax.dot_general(
                        ordered[...], held[k, pl.ds(at, tile), :], CONTRACT_LAST, preferred_element_type=F32
                    )
                else:
                    total = jnp.dot(
                        ordered[...], held[k, :, pl.ds(at, tile)], preferred_element_type=F32
                    )
                row = 0
                for ref in out_refs:
                    size = ref.shape[1]
                    ref[k, :, pl.ds(at, tile)] = total[row : row + size].astype(ref.dtype)
                    row += size
            return carry

        def place(a, s):
            return pl.ds(pl.multiple_of(a * tokens + (t ^ s) * block, block), block)

        for a in range(cores):
            natural[place(a, 0), :] = x_refs[2 * a][...]
            for s in range(1, n_tensor):
                natural[place(a, s), :] = x_refs[2 * a + 1][(s - 1) * block : s * block, :]
        for i, (s, a) in enumerate(places):
            start = pl.multiple_of(a * tokens + (p ^ s) * rows, rows)
            ordered[i * rows : (i + 1) * rows, :] = natural[pl.ds(start, rows), :]
        lax.fori_loop(0, count, work, 0)

    return pl.pallas_call(
        kernel,
        in_specs=[IN_VMEM] * (n_in + 1) + [IN_PLACE] * n_after,
        out_specs=[IN_VMEM] * n_out,
        out_shape=[
            jax.ShapeDtypeStruct((kinds, len(pieces) * rows, units), dtype)
            for dtype, pieces in layout
        ],
        scratch_shapes=[
            pltpu.VMEM((cores * tokens, depth), BF16),
            pltpu.VMEM((cores * tokens, depth), BF16),
        ],
        compiler_params=params(),
        cost_estimate=cost(0, 0) if transposed else cost(2 * cores * tokens * depth * units * kinds, 2 * depth * units * kinds),
        name="pull_back" if transposed else "project",
    )(*flat, weights, *after)


def contract(blocks, pieces, weights, transposed, cores, n_pipe, n_tensor, after=()):
    kinds, _, units = blocks[0].shape
    n_in, n_after = len(blocks), len(after)
    from_rows = blocks[0].shape[1] // cores
    tokens = from_rows * n_pipe
    to_rows = tokens // n_tensor
    width = weights.shape[1] if transposed else weights.shape[2]
    tile = pick_tile(width)
    count = width // tile

    def kernel(*refs):
        x_refs = refs[:n_in]
        held = refs[n_in]
        out_refs = refs[n_in + 1 + n_after : n_in + 1 + n_after + cores]
        natural, ordered = refs[n_in + 1 + n_after + cores :]
        t = lax.axis_index("tensor")
        p = lax.axis_index("pipe")

        def work(j, carry):
            at = pl.multiple_of(j * tile, tile)
            total = None
            for k in range(kinds):
                if transposed:
                    part = lax.dot_general(
                        ordered[k], held[k, pl.ds(at, tile), :], CONTRACT_LAST, preferred_element_type=F32
                    )
                else:
                    part = jnp.dot(
                        ordered[k], held[k, :, pl.ds(at, tile)], preferred_element_type=F32
                    )
                total = part if total is None else total + part
            for a in range(cores):
                part = total[a * tokens : (a + 1) * tokens]
                out_refs[a][:, pl.ds(at, tile)] = part.astype(out_refs[a].dtype)
            return carry

        for k in range(kinds):
            for a in range(cores):
                for s in range(n_pipe):
                    start = pl.multiple_of((p ^ s) * from_rows, from_rows)
                    place, row = pieces[s][a]
                    natural[pl.ds(start, from_rows), :] = x_refs[place][
                        k, row : row + from_rows, :
                    ]
                for s in range(n_tensor):
                    start = pl.multiple_of((t ^ s) * to_rows, to_rows)
                    at = a * tokens + s * to_rows
                    ordered[k, at : at + to_rows, :] = natural[pl.ds(start, to_rows), :]
        lax.fori_loop(0, count, work, 0)

    return pl.pallas_call(
        kernel,
        in_specs=[IN_VMEM] * (n_in + 1) + [IN_PLACE] * n_after,
        out_specs=[IN_VMEM] * cores,
        out_shape=[
            jax.ShapeDtypeStruct((tokens, width), BF16 if a else F32) for a in range(cores)
        ],
        scratch_shapes=[
            pltpu.VMEM((tokens, units), BF16),
            pltpu.VMEM((kinds, cores * tokens, units), BF16),
        ],
        compiler_params=params(),
        cost_estimate=cost(2 * cores * tokens * units * width * kinds, 2 * units * width * kinds),
        name="input_grad" if transposed else "layer_output",
    )(*blocks, weights, *after)


def gather_first(value, n_tensor):
    came = {s: exchange(value, "tensor", n_tensor, s) for s in range(n_tensor - 1, 0, -1)}
    return [value] + [came[s] for s in range(1, n_tensor)]


def gather_tokens(blocks, other, cores, after=()):
    own, came = blocks[0], blocks[1:]
    rows, width = own.shape

    def body(ins, outs):
        for s, ref in enumerate(ins):
            outs[0][s * rows : (s + 1) * rows, :] = ref[...]

    shape = (rows * len(came), width)
    (rest,) = small_kernel(body, [(shape, BF16)], came, "assemble", after)
    if cores == 1:
        return [(own, rest)]
    return [(own, rest), (other, exchange(rest, "dp", cores, 1))]


def finish(partials, cores, n_tensor, after=()):
    if cores > 1:
        other = exchange(partials[1], "dp", cores, 1)
        rows, width = other.shape[0] // n_tensor, other.shape[1]

        def body(ins, outs):
            for s in range(n_tensor):
                at = slice(s * rows, (s + 1) * rows)
                outs[s][...] = (ins[0][at] + ins[1][at].astype(F32)).astype(outs[s].dtype)

        parts = small_kernel(
            body,
            [((rows, width), BF16 if s else F32) for s in range(n_tensor)],
            [partials[0], other],
            "add_core",
            after,
        )
    else:
        rows = partials[0].shape[0] // n_tensor
        parts = [
            partials[0][s * rows : (s + 1) * rows].astype(BF16 if s else F32)
            for s in range(n_tensor)
        ]

    came = [exchange(parts[s], "tensor", n_tensor, s) for s in range(1, n_tensor)]
    total = parts[0]
    for value in came:
        total = total + value.astype(F32)
    return came, total.astype(BF16)


def slope_values(grad, gate, up):
    gate, up = gate.astype(F32), up.astype(F32)
    sigma = jax.nn.sigmoid(gate)
    gate_slope = (grad * up * sigma * (1.0 + gate * (1.0 - sigma))).astype(BF16)
    up_slope = (grad * gate * sigma).astype(BF16)
    return gate_slope, up_slope


def direct(
    n_pipe, n_tensor, forward_acts, backward_grad, stored_gate, stored_up, gate_weight, up_weight, down_weight
):
    layout = [(BF16 if s else F32, [(s, 0)]) for s in range(n_pipe)]
    pieces = [[(s, 0)] for s in range(n_pipe)]

    def total_of(parts):
        total = parts[0]
        for s in range(1, n_pipe):
            total = total + exchange(parts[s], "pipe", n_pipe, s).astype(F32)
        return total

    def gather(value):
        return [value] + [exchange(value, "pipe", n_pipe, s) for s in range(1, n_pipe)]

    wide, tall = load_weights(gate_weight, up_weight, down_weight, 1)
    grads = gather_tokens(gather_first(backward_grad, n_tensor), None, 1)
    acts = gather_tokens(gather_first(forward_acts, n_tensor), None, 1)
    grad = total_of(project(grads, tall, True, layout, n_pipe, n_tensor))[0]
    slopes = gather(jnp.stack(slope_values(grad, stored_gate, stored_up)))
    summed = total_of(project(acts, wide, False, layout, n_pipe, n_tensor))
    hidden = gather((jax.nn.silu(summed[:1]) * summed[1:]).astype(BF16))
    back = contract(slopes, pieces, wide, True, 1, n_pipe, n_tensor)
    out = contract(hidden, pieces, tall, False, 1, n_pipe, n_tensor)
    return finish(out, 1, n_tensor)[1], finish(back, 1, n_tensor)[1]


def balanced(
    n_tensor, forward_acts, backward_grad, stored_gate, stored_up, gate_weight, up_weight, down_weight
):
    cores, n_pipe, x, y = 2, 4, 1, 2
    units = gate_weight.shape[1] // cores
    rows = stored_gate.shape[0]
    straight = [(BF16 if s else F32, [(s, 0), (s, 1)]) for s in range(n_pipe)]
    balanced_layout = [
        (F32, [(0, 0), (0, 1), (1, 1), (2, 0)]),
        (BF16, [(3, 0), (1, 0)]),
        (BF16, [(3, 1), (2, 1)]),
    ]
    straight_pieces = [[(s, 0), (s, rows)] for s in range(n_pipe)]
    balanced_pieces = straight_pieces[:3] + [[(3, 0), (4, 0)]]


    def swap(value, step):
        return exchange(value, "pipe", n_pipe, step)

    def slopes_body(ins, outs):
        keep, came = ins[0], ins[1:n_pipe]
        for a in range(cores):
            at = slice(a * rows, (a + 1) * rows)
            grad = keep[0, at]
            for ref in came:
                grad = grad + ref[0, at].astype(F32)
            stored = ins[n_pipe + a]
            gate_slope, up_slope = slope_values(grad, stored[0], stored[1])
            outs[0][0, at] = gate_slope
            outs[0][1, at] = up_slope

    def pass_on_body(ins, outs):
        keep, came_x, came_y = ins
        for k in range(2):
            on_x = keep[k, 2 * rows : 3 * rows] + came_y[k, :rows].astype(F32)
            on_y = keep[k, 3 * rows : 4 * rows] + came_x[k, :rows].astype(F32)
            outs[0][k] = on_x.astype(BF16)
            outs[1][k] = on_y.astype(BF16)

    def hidden_body(ins, outs):
        keep, came_x, came_y, then_x, then_y = ins
        for a, near, far in ((0, came_x, then_y), (1, came_y, then_x)):
            at = slice(a * rows, (a + 1) * rows)
            gate, up = [
                keep[k, at] + near[k, rows:].astype(F32) + far[k].astype(F32) for k in range(2)
            ]
            outs[0][0, at] = (jax.nn.silu(gate) * up).astype(BF16)

    def stored_body(ins, outs):
        core = lax.axis_index("dp")
        for k in range(2):
            for c in range(cores):
                start = pl.multiple_of((core ^ c) * units, units)
                outs[c][k] = ins[k][:, pl.ds(start, units)]

    acts = gather_first(forward_acts, n_tensor)
    grads = gather_first(backward_grad, n_tensor)
    wide, tall = load_weights(gate_weight, up_weight, down_weight, cores)
    other_acts = exchange(forward_acts, "dp", cores, 1)
    other_grads = exchange(backward_grad, "dp", cores, 1)
    acts = gather_tokens(acts, other_acts, cores, after=[tall, other_acts])
    keep, for_x, for_y = project(
        acts, wide, False, balanced_layout, n_pipe, n_tensor, after=[other_grads]
    )
    came_x, came_y = swap(for_x, x), swap(for_y, y)
    mine, other = small_kernel(
        stored_body, [((2, rows, units), BF16)] * 2, [stored_gate, stored_up], "stored", after=[keep]
    )
    other = exchange(other, "dp", cores, 1)
    grads = gather_tokens(grads, other_grads, cores, after=[keep])
    parts = project(grads, tall, True, straight, n_pipe, n_tensor, after=[other])
    parts = [parts[0]] + [swap(parts[s], s) for s in (3, 1, 2)]

    half = ((2, rows, units), BF16)
    on_x, on_y = small_kernel(
        pass_on_body, [half, half], [keep, came_x, came_y], "pass_on", after=[parts[0]]
    )
    sums = [keep, came_x, came_y, swap(on_x, x), swap(on_y, y)]
    (hidden,) = small_kernel(hidden_body, [((1, cores * rows, units), BF16)], sums, "hidden")
    hidden_all = [hidden] + [swap(hidden, s) for s in range(1, n_pipe)]

    (slopes,) = small_kernel(
        slopes_body,
        [((2, cores * rows, units), BF16)],
        [*parts, mine, other],
        "slopes",
        after=[hidden],
    )
    slopes_x, slopes_y = swap(slopes, x), swap(slopes, y)

    out = contract(
        hidden_all, straight_pieces, tall, False, cores, n_pipe, n_tensor, after=[slopes]
    )
    slopes_all = [
        slopes,
        slopes_x,
        slopes_y,
        swap(slopes_x[:, :rows], y),
        swap(slopes_y[:, rows:], x),
    ]
    came, layer_output = finish(out, cores, n_tensor)
    back = contract(
        slopes_all,
        balanced_pieces,
        wide,
        True,
        cores,
        n_pipe,
        n_tensor,
        after=came[:2],
    )
    _, input_grad = finish(back, cores, n_tensor)
    return layer_output, input_grad


def solution(mesh):
    in_specs = (
        P(("dp", "tensor"), "pipe"),
        P(("dp", "tensor"), "pipe"),
        P(("dp", "pipe"), "tensor"),
        P(("dp", "pipe"), "tensor"),
        P("pipe", "tensor"),
        P("pipe", "tensor"),
        P("tensor", "pipe"),
    )
    out_specs = (P(("dp", "tensor"), "pipe"), P(("dp", "tensor"), "pipe"))

    def whole(*args):
        n_pipe, n_tensor = mesh.shape["pipe"], mesh.shape["tensor"]
        hidden_width = args[4].shape[1] // n_tensor
        if mesh.shape["dp"] == 2 and n_pipe == 4 and hidden_width % 256 == 0:
            body = functools.partial(balanced, n_tensor)
        else:
            body = functools.partial(direct, n_pipe, n_tensor)
        return jax.shard_map(
            body, mesh=mesh, in_specs=in_specs, out_specs=out_specs, check_vma=False
        )(*args)

    return whole
```

```python
import functools

import jax
import jax.numpy as jnp
from jax import lax
from jax.experimental import pallas as pl
from jax.experimental.pallas import tpu as pltpu
from jax.sharding import PartitionSpec as P

F32 = jnp.float32
BF16 = jnp.bfloat16
VMEM_BYTES = 16 * 1024 * 1024
FIRST_LOAD_BYTES = 40 * 1024 * 1024
LOAD_BYTES = 30 * 1024 * 1024
CONTRACT_LAST = (((1,), (1,)), ((), ()))
IN_VMEM = pl.BlockSpec(memory_space=pltpu.VMEM)
IN_PLACE = pl.BlockSpec(memory_space=pl.ANY)


def exchange(value, axis, size, step):
    return lax.ppermute(value, axis, [(i, i ^ step) for i in range(size)])


def pick_tile(width):
    return 256 if width % 256 == 0 else 128


def cost(flops, moved):
    return pl.CostEstimate(flops=flops, bytes_accessed=moved, transcendentals=0)


def params():
    return pltpu.CompilerParams(vmem_limit_bytes=VMEM_BYTES)


def small_kernel(body, outs, inputs, name, after=()):
    n_in, n_after = len(inputs), len(after)

    def kernel(*refs):
        body(refs[:n_in], refs[n_in + n_after :])

    moved = sum(a.size * a.dtype.itemsize for a in inputs)
    return pl.pallas_call(
        kernel,
        in_specs=[IN_VMEM] * n_in + [IN_PLACE] * n_after,
        out_specs=[IN_VMEM] * len(outs),
        out_shape=[jax.ShapeDtypeStruct(shape, dtype) for shape, dtype in outs],
        cost_estimate=cost(moved, moved),
        compiler_params=params(),
        name=name,
    )(*inputs, *after)


def load(weights, by_rows, cores, limit, after=()):
    kinds, n_after = len(weights), len(after)
    shape = weights[0].shape
    units = (shape[0] if by_rows else shape[1]) // cores
    part = (units, shape[1]) if by_rows else (shape[0], units)
    cuts = 4
    rows = part[0] // cuts

    def kernel(*refs):
        held, sems = refs[kinds + n_after :]
        first = pl.multiple_of(lax.axis_index("dp") * units, units) if cores > 1 else 0
        copies = []
        for i in range(cuts):
            for k in range(kinds):
                if by_rows:
                    source = refs[k].at[pl.ds(pl.multiple_of(first + i * rows, rows), rows)]
                else:
                    source = refs[k].at[pl.ds(i * rows, rows), pl.ds(first, units)]
                target = held.at[k, pl.ds(i * rows, rows)]
                copies.append(pltpu.make_async_copy(source, target, sems.at[i * kinds + k]))
        for copy in copies:
            copy.start()
        for copy in copies:
            copy.wait()

    return pl.pallas_call(
        kernel,
        in_specs=[IN_PLACE] * (kinds + n_after),
        out_specs=IN_VMEM,
        out_shape=jax.ShapeDtypeStruct((kinds,) + part, BF16),
        scratch_shapes=[pltpu.SemaphoreType.DMA((kinds * cuts,))],
        compiler_params=pltpu.CompilerParams(vmem_limit_bytes=limit),
        cost_estimate=cost(0, 0),
        name="load_rows" if by_rows else "load_columns",
    )(*weights, *after)


def project(inputs, weights, transposed, layout, n_pipe, n_tensor, after=()):
    cores = len(inputs)
    flat = [x for pair in inputs for x in pair]
    n_in, n_after, n_out, kinds = len(flat), len(after), len(layout), weights.shape[0]
    block, depth = inputs[0][0].shape
    tokens = block * n_tensor
    units = weights.shape[1] if transposed else weights.shape[2]
    tile = pick_tile(units)
    count = units // tile
    rows = tokens // n_pipe
    places = [piece for _, pieces in layout for piece in pieces]

    def kernel(*refs):
        x_refs = refs[:n_in]
        held = refs[n_in]
        out_refs = refs[n_in + 1 + n_after : n_in + 1 + n_after + n_out]
        natural, ordered = refs[n_in + 1 + n_after + n_out :]
        t = lax.axis_index("tensor")
        p = lax.axis_index("pipe")

        def work(j, carry):
            at = pl.multiple_of(j * tile, tile)
            for k in range(kinds):
                if transposed:
                    total = lax.dot_general(
                        ordered[...], held[k, pl.ds(at, tile), :], CONTRACT_LAST, preferred_element_type=F32
                    )
                else:
                    total = jnp.dot(
                        ordered[...], held[k, :, pl.ds(at, tile)], preferred_element_type=F32
                    )
                row = 0
                for ref in out_refs:
                    size = ref.shape[1]
                    ref[k, :, pl.ds(at, tile)] = total[row : row + size].astype(ref.dtype)
                    row += size
            return carry

        def place(a, s):
            return pl.ds(pl.multiple_of(a * tokens + (t ^ s) * block, block), block)

        for a in range(cores):
            natural[place(a, 0), :] = x_refs[2 * a][...]
            for s in range(1, n_tensor):
                natural[place(a, s), :] = x_refs[2 * a + 1][(s - 1) * block : s * block, :]
        for i, (s, a) in enumerate(places):
            start = pl.multiple_of(a * tokens + (p ^ s) * rows, rows)
            ordered[i * rows : (i + 1) * rows, :] = natural[pl.ds(start, rows), :]
        lax.fori_loop(0, count, work, 0)

    return pl.pallas_call(
        kernel,
        in_specs=[IN_VMEM] * (n_in + 1) + [IN_PLACE] * n_after,
        out_specs=[IN_VMEM] * n_out,
        out_shape=[
            jax.ShapeDtypeStruct((kinds, len(pieces) * rows, units), dtype)
            for dtype, pieces in layout
        ],
        scratch_shapes=[
            pltpu.VMEM((cores * tokens, depth), BF16),
            pltpu.VMEM((cores * tokens, depth), BF16),
        ],
        compiler_params=params(),
        cost_estimate=cost(0, 0) if transposed else cost(2 * cores * tokens * depth * units * kinds, 2 * depth * units * kinds),
        name="pull_back" if transposed else "project",
    )(*flat, weights, *after)


def contract(blocks, weights, transposed, cores, n_pipe, n_tensor, factors=None, after=()):
    kinds, units = weights.shape[0], blocks[0].shape[2]
    extra = [] if factors is None else [factors]
    n_in, n_after = len(blocks), len(after)
    from_rows = blocks[0].shape[1] // cores
    tokens = from_rows * n_pipe
    to_rows = tokens // n_tensor
    width = weights.shape[1] if transposed else weights.shape[2]
    tile = pick_tile(width)
    count = width // tile

    def kernel(*refs):
        x_refs = refs[:n_in]
        held = refs[n_in]
        factor = refs[n_in + 1] if extra else None
        n_refs = n_in + 1 + len(extra) + n_after
        out_refs = refs[n_refs : n_refs + cores]
        natural, ordered = refs[n_refs + cores :]
        t = lax.axis_index("tensor")
        p = lax.axis_index("pipe")

        def work(j, carry):
            at = pl.multiple_of(j * tile, tile)
            total = None
            for k in range(kinds):
                if transposed:
                    part = lax.dot_general(
                        ordered[k], held[k, pl.ds(at, tile), :], CONTRACT_LAST, preferred_element_type=F32
                    )
                else:
                    part = jnp.dot(
                        ordered[k], held[k, :, pl.ds(at, tile)], preferred_element_type=F32
                    )
                total = part if total is None else total + part
            for a in range(cores):
                part = total[a * tokens : (a + 1) * tokens]
                out_refs[a][:, pl.ds(at, tile)] = part.astype(out_refs[a].dtype)
            return carry

        for k in range(kinds):
            for a in range(cores):
                for s in range(n_pipe):
                    start = pl.multiple_of((p ^ s) * from_rows, from_rows)
                    block = x_refs[s][0 if extra else k, a * from_rows : (a + 1) * from_rows, :]
                    if extra:
                        at = a * tokens + s * from_rows
                        scale = factor[k, at : at + from_rows, :]
                        block = (block.astype(F32) * scale).astype(BF16)
                    natural[pl.ds(start, from_rows), :] = block
                for s in range(n_tensor):
                    start = pl.multiple_of((t ^ s) * to_rows, to_rows)
                    at = a * tokens + s * to_rows
                    ordered[k, at : at + to_rows, :] = natural[pl.ds(start, to_rows), :]
        lax.fori_loop(0, count, work, 0)

    return pl.pallas_call(
        kernel,
        in_specs=[IN_VMEM] * (n_in + 1 + len(extra)) + [IN_PLACE] * n_after,
        out_specs=[IN_VMEM] * cores,
        out_shape=[
            jax.ShapeDtypeStruct((tokens, width), BF16 if a else F32) for a in range(cores)
        ],
        scratch_shapes=[
            pltpu.VMEM((tokens, units), BF16),
            pltpu.VMEM((kinds, cores * tokens, units), BF16),
        ],
        compiler_params=params(),
        cost_estimate=cost(2 * cores * tokens * units * width * kinds, 2 * units * width * kinds),
        name="input_grad" if transposed else "layer_output",
    )(*blocks, weights, *extra, *after)


def gather_first(value, n_tensor):
    came = {s: exchange(value, "tensor", n_tensor, s) for s in range(n_tensor - 1, 0, -1)}
    return [value] + [came[s] for s in range(1, n_tensor)]


def gather_tokens(blocks, other, cores, after=()):
    own, came = blocks[0], blocks[1:]
    rows, width = own.shape

    def body(ins, outs):
        for s, ref in enumerate(ins):
            outs[0][s * rows : (s + 1) * rows, :] = ref[...]

    shape = (rows * len(came), width)
    (rest,) = small_kernel(body, [(shape, BF16)], came, "assemble", after)
    if cores == 1:
        return [(own, rest)]
    return [(own, rest), (other, exchange(rest, "dp", cores, 1))]


def finish(partials, cores, n_tensor, after=()):
    if cores > 1:
        other = exchange(partials[1], "dp", cores, 1)
        rows, width = other.shape[0] // n_tensor, other.shape[1]

        def body(ins, outs):
            for s in range(n_tensor):
                at = slice(s * rows, (s + 1) * rows)
                outs[s][...] = (ins[0][at] + ins[1][at].astype(F32)).astype(outs[s].dtype)

        parts = small_kernel(
            body,
            [((rows, width), BF16 if s else F32) for s in range(n_tensor)],
            [partials[0], other],
            "add_core",
            after,
        )
    else:
        rows = partials[0].shape[0] // n_tensor
        parts = [
            partials[0][s * rows : (s + 1) * rows].astype(BF16 if s else F32)
            for s in range(n_tensor)
        ]

    came = [exchange(parts[s], "tensor", n_tensor, s) for s in range(1, n_tensor)]
    total = parts[0]
    for value in came:
        total = total + value.astype(F32)
    return came, total.astype(BF16)


def slope_factors(gate, up):
    gate, up = gate.astype(F32), up.astype(F32)
    sigma = jax.nn.sigmoid(gate)
    return up * sigma * (1.0 + gate * (1.0 - sigma)), gate * sigma


def direct(
    n_pipe, n_tensor, forward_acts, backward_grad, stored_gate, stored_up, gate_weight, up_weight, down_weight
):
    layout = [(BF16 if s else F32, [(s, 0)]) for s in range(n_pipe)]

    def total_of(parts):
        total = parts[0]
        for s in range(1, n_pipe):
            total = total + exchange(parts[s], "pipe", n_pipe, s).astype(F32)
        return total

    def gather(value):
        return [value] + [exchange(value, "pipe", n_pipe, s) for s in range(1, n_pipe)]

    tall = load([down_weight], True, 1, LOAD_BYTES)
    wide = load([gate_weight, up_weight], False, 1, LOAD_BYTES)
    grads = gather_tokens(gather_first(backward_grad, n_tensor), None, 1)
    acts = gather_tokens(gather_first(forward_acts, n_tensor), None, 1)
    grad = total_of(project(grads, tall, True, layout, n_pipe, n_tensor))[0]
    slopes = [(grad * f).astype(BF16) for f in slope_factors(stored_gate, stored_up)]
    slopes = gather(jnp.stack(slopes))
    summed = total_of(project(acts, wide, False, layout, n_pipe, n_tensor))
    hidden = gather((jax.nn.silu(summed[:1]) * summed[1:]).astype(BF16))
    back = contract(slopes, wide, True, 1, n_pipe, n_tensor)
    out = contract(hidden, tall, False, 1, n_pipe, n_tensor)
    return finish(out, 1, n_tensor)[1], finish(back, 1, n_tensor)[1]


def balanced(
    n_tensor, forward_acts, backward_grad, stored_gate, stored_up, gate_weight, up_weight, down_weight
):
    cores, n_pipe, x, y = 2, 4, 1, 2
    units = gate_weight.shape[1] // cores
    rows = stored_gate.shape[0]
    straight = [(BF16 if s else F32, [(s, 0), (s, 1)]) for s in range(n_pipe)]
    balanced_layout = [
        (F32, [(0, 0), (0, 1), (1, 1), (2, 0)]),
        (BF16, [(3, 0), (1, 0)]),
        (BF16, [(3, 1), (2, 1)]),
    ]

    def swap(value, step):
        return exchange(value, "pipe", n_pipe, step)

    def stack_body(ins, outs):
        for k in range(2):
            outs[0][k] = ins[k][...]

    def split_body(ins, outs):
        core = lax.axis_index("dp")
        for s, ref in enumerate(ins):
            for c in range(cores):
                start = pl.multiple_of((core ^ c) * units, units)
                outs[c][:, s * rows : (s + 1) * rows, :] = ref[:, :, pl.ds(start, units)]

    def factors_body(ins, outs):
        tokens = n_pipe * rows
        for a in range(cores):
            for s in range(n_pipe):
                at = slice(s * rows, (s + 1) * rows)
                values = slope_factors(ins[a][0, at], ins[a][1, at])
                for k in range(2):
                    outs[0][k, a * tokens + s * rows : a * tokens + (s + 1) * rows] = values[k]

    def total_body(ins, outs):
        total = ins[0][...]
        for ref in ins[1:]:
            total = total + ref[...].astype(F32)
        outs[0][...] = total.astype(BF16)

    def pass_on_body(ins, outs):
        keep, came_x, came_y = ins
        for k in range(2):
            on_x = keep[k, 2 * rows : 3 * rows] + came_y[k, :rows].astype(F32)
            on_y = keep[k, 3 * rows : 4 * rows] + came_x[k, :rows].astype(F32)
            outs[0][k] = on_x.astype(BF16)
            outs[1][k] = on_y.astype(BF16)

    def hidden_body(ins, outs):
        keep, came_x, came_y, then_x, then_y = ins
        for a, near, far in ((0, came_x, then_y), (1, came_y, then_x)):
            at = slice(a * rows, (a + 1) * rows)
            gate, up = [
                keep[k, at] + near[k, rows:].astype(F32) + far[k].astype(F32) for k in range(2)
            ]
            outs[0][0, at] = (jax.nn.silu(gate) * up).astype(BF16)

    grads = gather_first(backward_grad, n_tensor)
    other_grads = exchange(backward_grad, "dp", cores, 1)
    tall = load([down_weight], True, cores, FIRST_LOAD_BYTES)
    (stored,) = small_kernel(
        stack_body,
        [((2,) + stored_gate.shape, BF16)],
        [stored_gate, stored_up],
        "stack_stored",
        after=[tall],
    )
    stored_x, stored_y = swap(stored, x), swap(stored, y)
    stored_far = swap(stored, x ^ y)
    grads = gather_tokens(grads, other_grads, cores, after=[tall, other_grads, stored])
    acts = gather_first(forward_acts, n_tensor)
    other_acts = exchange(forward_acts, "dp", cores, 1)

    parts = project(grads, tall, True, straight, n_pipe, n_tensor, after=[stored_x, stored_y])
    parts = [parts[0]] + [swap(parts[s], s) for s in (3, 1, 2)]
    wide = load([gate_weight, up_weight], False, cores, LOAD_BYTES, after=[parts[0]])
    (grad,) = small_kernel(
        total_body, [((1, cores * rows, units), BF16)], parts, "hidden_grad", after=[wide, *acts[1:]]
    )
    grad_all = [grad] + [swap(grad, s) for s in range(1, n_pipe)]

    mine, other = small_kernel(
        split_body,
        [((2, n_pipe * rows, units), BF16)] * 2,
        [stored, stored_x, stored_y, stored_far],
        "split_stored",
        after=[grad],
    )
    other = exchange(other, "dp", cores, 1)
    acts = gather_tokens(acts, other_acts, cores, after=[grad])
    keep, for_x, for_y = project(
        acts, wide, False, balanced_layout, n_pipe, n_tensor, after=[other_acts, grad]
    )
    came_x, came_y = swap(for_x, x), swap(for_y, y)
    (factors,) = small_kernel(
        factors_body,
        [((2, cores * n_pipe * rows, units), F32)],
        [mine, other],
        "slope_factors",
        after=[keep],
    )
    back = contract(grad_all, wide, True, cores, n_pipe, n_tensor, factors=factors)

    half = ((2, rows, units), BF16)
    on_x, on_y = small_kernel(
        pass_on_body, [half, half], [keep, came_x, came_y], "pass_on", after=[back[0]]
    )
    came, input_grad = finish(back, cores, n_tensor)
    sums = [keep, came_x, came_y, swap(on_x, x), swap(on_y, y)]
    (hidden,) = small_kernel(hidden_body, [((1, cores * rows, units), BF16)], sums, "hidden")
    hidden_all = [hidden] + [swap(hidden, s) for s in range(1, n_pipe)]
    out = contract(hidden_all, tall, False, cores, n_pipe, n_tensor, after=came)
    _, layer_output = finish(out, cores, n_tensor)
    return layer_output, input_grad


def solution(mesh):
    in_specs = (
        P(("dp", "tensor"), "pipe"),
        P(("dp", "tensor"), "pipe"),
        P(("dp", "pipe"), "tensor"),
        P(("dp", "pipe"), "tensor"),
        P("pipe", "tensor"),
        P("pipe", "tensor"),
        P("tensor", "pipe"),
    )
    out_specs = (P(("dp", "tensor"), "pipe"), P(("dp", "tensor"), "pipe"))

    def whole(*args):
        n_pipe, n_tensor = mesh.shape["pipe"], mesh.shape["tensor"]
        hidden_width = args[4].shape[1] // n_tensor
        if mesh.shape["dp"] == 2 and n_pipe == 4 and hidden_width % 256 == 0:
            body = functools.partial(balanced, n_tensor)
        else:
            body = functools.partial(direct, n_pipe, n_tensor)
        return jax.shard_map(
            body, mesh=mesh, in_specs=in_specs, out_specs=out_specs, check_vma=False
        )(*args)

    return whole
```

```python
import functools

import jax
import jax.numpy as jnp
from jax import lax
from jax.experimental import pallas as pl
from jax.experimental.pallas import tpu as pltpu
from jax.sharding import PartitionSpec as P

F32 = jnp.float32
BF16 = jnp.bfloat16
VMEM_BYTES = 16 * 1024 * 1024
LOAD_BYTES = 24 * 1024 * 1024
CONTRACT_LAST = (((1,), (1,)), ((), ()))
IN_VMEM = pl.BlockSpec(memory_space=pltpu.VMEM)
IN_PLACE = pl.BlockSpec(memory_space=pl.ANY)


def exchange(value, axis, size, step):
    return lax.ppermute(value, axis, [(i, i ^ step) for i in range(size)])


def pick_tile(width):
    return 256 if width % 256 == 0 else 128


def cost(flops, moved):
    return pl.CostEstimate(flops=flops, bytes_accessed=moved, transcendentals=0)


def params():
    return pltpu.CompilerParams(vmem_limit_bytes=VMEM_BYTES)


def small_kernel(body, outs, inputs, name, after=()):
    n_in, n_after = len(inputs), len(after)

    def kernel(*refs):
        body(refs[:n_in], refs[n_in + n_after :])

    moved = sum(a.size * a.dtype.itemsize for a in inputs)
    return pl.pallas_call(
        kernel,
        in_specs=[IN_VMEM] * n_in + [IN_PLACE] * n_after,
        out_specs=[IN_VMEM] * len(outs),
        out_shape=[jax.ShapeDtypeStruct(shape, dtype) for shape, dtype in outs],
        cost_estimate=cost(moved, moved),
        compiler_params=params(),
        name=name,
    )(*inputs, *after)


def load_weights(gate_weight, up_weight, down_weight, cores):
    depth = gate_weight.shape[0]
    units = gate_weight.shape[1] // cores
    cuts = 4
    rows, unit_rows = depth // cuts, units // cuts

    def kernel(gate, up, down, wide, tall, sems):
        first = pl.multiple_of(lax.axis_index("dp") * units, units) if cores > 1 else 0
        copies = []
        for i in range(cuts):
            for k, ref in enumerate((gate, up)):
                at = pl.ds(i * rows, rows)
                copies.append((ref.at[at, pl.ds(first, units)], wide.at[k, at]))
        for i in range(cuts):
            at = pl.multiple_of(first + i * unit_rows, unit_rows)
            copies.append((down.at[pl.ds(at, unit_rows)], tall.at[0, pl.ds(i * unit_rows, unit_rows)]))
        copies = [
            pltpu.make_async_copy(source, target, sems.at[i])
            for i, (source, target) in enumerate(copies)
        ]
        for copy in copies:
            copy.start()
        for copy in copies:
            copy.wait()

    return pl.pallas_call(
        kernel,
        in_specs=[IN_PLACE] * 3,
        out_specs=[IN_VMEM] * 2,
        out_shape=[
            jax.ShapeDtypeStruct((2, depth, units), BF16),
            jax.ShapeDtypeStruct((1, units, depth), BF16),
        ],
        scratch_shapes=[pltpu.SemaphoreType.DMA((3 * cuts,))],
        compiler_params=pltpu.CompilerParams(vmem_limit_bytes=LOAD_BYTES),
        cost_estimate=cost(0, 6 * depth * units),
        name="load_weights",
    )(gate_weight, up_weight, down_weight)


def project(inputs, weights, transposed, layout, n_pipe, n_tensor, after=()):
    cores = len(inputs)
    flat = [x for pair in inputs for x in pair]
    n_in, n_after, n_out, kinds = len(flat), len(after), len(layout), weights.shape[0]
    block, depth = inputs[0][0].shape
    tokens = block * n_tensor
    units = weights.shape[1] if transposed else weights.shape[2]
    tile = pick_tile(units)
    count = units // tile
    rows = tokens // n_pipe
    places = [piece for _, pieces in layout for piece in pieces]

    def kernel(*refs):
        x_refs = refs[:n_in]
        held = refs[n_in]
        out_refs = refs[n_in + 1 + n_after : n_in + 1 + n_after + n_out]
        natural, ordered = refs[n_in + 1 + n_after + n_out :]
        t = lax.axis_index("tensor")
        p = lax.axis_index("pipe")

        def work(j, carry):
            at = pl.multiple_of(j * tile, tile)
            for k in range(kinds):
                if transposed:
                    total = lax.dot_general(
                        ordered[...], held[k, pl.ds(at, tile), :], CONTRACT_LAST, preferred_element_type=F32
                    )
                else:
                    total = jnp.dot(
                        ordered[...], held[k, :, pl.ds(at, tile)], preferred_element_type=F32
                    )
                row = 0
                for ref in out_refs:
                    size = ref.shape[1]
                    ref[k, :, pl.ds(at, tile)] = total[row : row + size].astype(ref.dtype)
                    row += size
            return carry

        def place(a, s):
            return pl.ds(pl.multiple_of(a * tokens + (t ^ s) * block, block), block)

        for a in range(cores):
            natural[place(a, 0), :] = x_refs[2 * a][...]
            for s in range(1, n_tensor):
                natural[place(a, s), :] = x_refs[2 * a + 1][(s - 1) * block : s * block, :]
        for i, (s, a) in enumerate(places):
            start = pl.multiple_of(a * tokens + (p ^ s) * rows, rows)
            ordered[i * rows : (i + 1) * rows, :] = natural[pl.ds(start, rows), :]
        lax.fori_loop(0, count, work, 0)

    return pl.pallas_call(
        kernel,
        in_specs=[IN_VMEM] * (n_in + 1) + [IN_PLACE] * n_after,
        out_specs=[IN_VMEM] * n_out,
        out_shape=[
            jax.ShapeDtypeStruct((kinds, len(pieces) * rows, units), dtype)
            for dtype, pieces in layout
        ],
        scratch_shapes=[
            pltpu.VMEM((cores * tokens, depth), BF16),
            pltpu.VMEM((cores * tokens, depth), BF16),
        ],
        compiler_params=params(),
        cost_estimate=cost(0, 0) if transposed else cost(2 * cores * tokens * depth * units * kinds, 2 * depth * units * kinds),
        name="pull_back" if transposed else "project",
    )(*flat, weights, *after)


def contract(blocks, pieces, weights, transposed, cores, n_pipe, n_tensor, half=None, after=()):
    kinds, _, units = blocks[0].shape
    n_in, n_after = len(blocks), len(after)
    from_rows = blocks[0].shape[1] // cores
    tokens = from_rows * n_pipe
    to_rows = tokens // n_tensor
    width = weights.shape[1] if transposed else weights.shape[2]
    width = width if half is None else width // 2
    tile = pick_tile(width)
    count = width // tile
    base = width if half == 1 else 0

    def kernel(*refs):
        x_refs = refs[:n_in]
        held = refs[n_in]
        out_refs = refs[n_in + 1 + n_after : n_in + 1 + n_after + cores]
        natural, ordered = refs[n_in + 1 + n_after + cores :]
        t = lax.axis_index("tensor")
        p = lax.axis_index("pipe")

        def work(j, carry):
            at = pl.multiple_of(j * tile, tile)
            total = None
            for k in range(kinds):
                if transposed:
                    part = lax.dot_general(
                        ordered[k], held[k, pl.ds(base + at, tile), :], CONTRACT_LAST, preferred_element_type=F32
                    )
                else:
                    part = jnp.dot(
                        ordered[k], held[k, :, pl.ds(base + at, tile)], preferred_element_type=F32
                    )
                total = part if total is None else total + part
            for a in range(cores):
                part = total[a * tokens : (a + 1) * tokens]
                out_refs[a][:, pl.ds(at, tile)] = part.astype(out_refs[a].dtype)
            return carry

        for k in range(kinds):
            for a in range(cores):
                for s in range(n_pipe):
                    start = pl.multiple_of((p ^ s) * from_rows, from_rows)
                    place, row = pieces[s][a]
                    natural[pl.ds(start, from_rows), :] = x_refs[place][
                        k, row : row + from_rows, :
                    ]
                for s in range(n_tensor):
                    start = pl.multiple_of((t ^ s) * to_rows, to_rows)
                    at = a * tokens + s * to_rows
                    ordered[k, at : at + to_rows, :] = natural[pl.ds(start, to_rows), :]
        lax.fori_loop(0, count, work, 0)

    return pl.pallas_call(
        kernel,
        in_specs=[IN_VMEM] * (n_in + 1) + [IN_PLACE] * n_after,
        out_specs=[IN_VMEM] * cores,
        out_shape=[
            jax.ShapeDtypeStruct((tokens, width), BF16 if a else F32) for a in range(cores)
        ],
        scratch_shapes=[
            pltpu.VMEM((tokens, units), BF16),
            pltpu.VMEM((kinds, cores * tokens, units), BF16),
        ],
        compiler_params=params(),
        cost_estimate=cost(2 * cores * tokens * units * width * kinds, 2 * units * width * kinds),
        name="input_grad" if transposed else "layer_output",
    )(*blocks, weights, *after)


def gather_first(value, n_tensor):
    came = {s: exchange(value, "tensor", n_tensor, s) for s in range(n_tensor - 1, 0, -1)}
    return [value] + [came[s] for s in range(1, n_tensor)]


def gather_tokens(blocks, other, cores, after=()):
    own, came = blocks[0], blocks[1:]
    rows, width = own.shape

    def body(ins, outs):
        for s, ref in enumerate(ins):
            outs[0][s * rows : (s + 1) * rows, :] = ref[...]

    shape = (rows * len(came), width)
    (rest,) = small_kernel(body, [(shape, BF16)], came, "assemble", after)
    if cores == 1:
        return [(own, rest)]
    return [(own, rest), (other, exchange(rest, "dp", cores, 1))]


def finish(partials, cores, n_tensor, after=()):
    if cores > 1:
        other = exchange(partials[1], "dp", cores, 1)
        rows, width = other.shape[0] // n_tensor, other.shape[1]

        def body(ins, outs):
            for s in range(n_tensor):
                at = slice(s * rows, (s + 1) * rows)
                outs[s][...] = (ins[0][at] + ins[1][at].astype(F32)).astype(outs[s].dtype)

        parts = small_kernel(
            body,
            [((rows, width), BF16 if s else F32) for s in range(n_tensor)],
            [partials[0], other],
            "add_core",
            after,
        )
    else:
        rows = partials[0].shape[0] // n_tensor
        parts = [
            partials[0][s * rows : (s + 1) * rows].astype(BF16 if s else F32)
            for s in range(n_tensor)
        ]

    came = [exchange(parts[s], "tensor", n_tensor, s) for s in range(1, n_tensor)]
    total = parts[0]
    for value in came:
        total = total + value.astype(F32)
    return came, total.astype(BF16)


def slope_values(grad, gate, up):
    gate, up = gate.astype(F32), up.astype(F32)
    sigma = jax.nn.sigmoid(gate)
    gate_slope = (grad * up * sigma * (1.0 + gate * (1.0 - sigma))).astype(BF16)
    up_slope = (grad * gate * sigma).astype(BF16)
    return gate_slope, up_slope


def direct(
    n_pipe, n_tensor, forward_acts, backward_grad, stored_gate, stored_up, gate_weight, up_weight, down_weight
):
    layout = [(BF16 if s else F32, [(s, 0)]) for s in range(n_pipe)]
    pieces = [[(s, 0)] for s in range(n_pipe)]

    def total_of(parts):
        total = parts[0]
        for s in range(1, n_pipe):
            total = total + exchange(parts[s], "pipe", n_pipe, s).astype(F32)
        return total

    def gather(value):
        return [value] + [exchange(value, "pipe", n_pipe, s) for s in range(1, n_pipe)]

    wide, tall = load_weights(gate_weight, up_weight, down_weight, 1)
    grads = gather_tokens(gather_first(backward_grad, n_tensor), None, 1)
    acts = gather_tokens(gather_first(forward_acts, n_tensor), None, 1)
    grad = total_of(project(grads, tall, True, layout, n_pipe, n_tensor))[0]
    slopes = gather(jnp.stack(slope_values(grad, stored_gate, stored_up)))
    summed = total_of(project(acts, wide, False, layout, n_pipe, n_tensor))
    hidden = gather((jax.nn.silu(summed[:1]) * summed[1:]).astype(BF16))
    back = contract(slopes, pieces, wide, True, 1, n_pipe, n_tensor)
    out = contract(hidden, pieces, tall, False, 1, n_pipe, n_tensor)
    return finish(out, 1, n_tensor)[1], finish(back, 1, n_tensor)[1]


def balanced(
    n_tensor, forward_acts, backward_grad, stored_gate, stored_up, gate_weight, up_weight, down_weight
):
    cores, n_pipe, x, y = 2, 4, 1, 2
    units = gate_weight.shape[1] // cores
    rows = stored_gate.shape[0]
    straight = [(BF16 if s else F32, [(s, 0), (s, 1)]) for s in range(n_pipe)]
    balanced_layout = [
        (F32, [(0, 0), (0, 1), (1, 1), (2, 0)]),
        (BF16, [(3, 0), (1, 0)]),
        (BF16, [(3, 1), (2, 1)]),
    ]
    straight_pieces = [[(s, 0), (s, rows)] for s in range(n_pipe)]
    balanced_pieces = straight_pieces[:3] + [[(3, 0), (4, 0)]]


    def swap(value, step):
        return exchange(value, "pipe", n_pipe, step)

    def slopes_body(ins, outs):
        keep, came = ins[0], ins[1:n_pipe]
        for a in range(cores):
            at = slice(a * rows, (a + 1) * rows)
            grad = keep[0, at]
            for ref in came:
                grad = grad + ref[0, at].astype(F32)
            stored = ins[n_pipe + a]
            gate_slope, up_slope = slope_values(grad, stored[0], stored[1])
            outs[0][0, at] = gate_slope
            outs[0][1, at] = up_slope

    def pass_on_body(ins, outs):
        keep, came_x, came_y = ins
        for k in range(2):
            on_x = keep[k, 2 * rows : 3 * rows] + came_y[k, :rows].astype(F32)
            on_y = keep[k, 3 * rows : 4 * rows] + came_x[k, :rows].astype(F32)
            outs[0][k] = on_x.astype(BF16)
            outs[1][k] = on_y.astype(BF16)

    def hidden_body(ins, outs):
        keep, came_x, came_y, then_x, then_y = ins
        for a, near, far in ((0, came_x, then_y), (1, came_y, then_x)):
            at = slice(a * rows, (a + 1) * rows)
            gate, up = [
                keep[k, at] + near[k, rows:].astype(F32) + far[k].astype(F32) for k in range(2)
            ]
            outs[0][0, at] = (jax.nn.silu(gate) * up).astype(BF16)

    def stored_body(ins, outs):
        core = lax.axis_index("dp")
        for k in range(2):
            for c in range(cores):
                start = pl.multiple_of((core ^ c) * units, units)
                outs[c][k] = ins[k][:, pl.ds(start, units)]

    acts = gather_first(forward_acts, n_tensor)
    grads = gather_first(backward_grad, n_tensor)
    wide, tall = load_weights(gate_weight, up_weight, down_weight, cores)
    other_acts = exchange(forward_acts, "dp", cores, 1)
    other_grads = exchange(backward_grad, "dp", cores, 1)
    acts = gather_tokens(acts, other_acts, cores, after=[tall, other_acts, grads[1]])
    keep, for_x, for_y = project(
        acts, wide, False, balanced_layout, n_pipe, n_tensor, after=[other_grads]
    )
    came_x, came_y = swap(for_x, x), swap(for_y, y)
    mine, other = small_kernel(
        stored_body, [((2, rows, units), BF16)] * 2, [stored_gate, stored_up], "stored", after=[keep]
    )
    other = exchange(other, "dp", cores, 1)
    grads = gather_tokens(grads, other_grads, cores, after=[keep])
    parts = project(grads, tall, True, straight, n_pipe, n_tensor, after=[other])
    parts = [parts[0]] + [swap(parts[s], s) for s in (3, 1, 2)]

    half = ((2, rows, units), BF16)
    on_x, on_y = small_kernel(
        pass_on_body, [half, half], [keep, came_x, came_y], "pass_on", after=[parts[0]]
    )
    sums = [keep, came_x, came_y, swap(on_x, x), swap(on_y, y)]
    (hidden,) = small_kernel(hidden_body, [((1, cores * rows, units), BF16)], sums, "hidden")
    hidden_all = [hidden] + [swap(hidden, s) for s in range(1, n_pipe)]

    (slopes,) = small_kernel(
        slopes_body,
        [((2, cores * rows, units), BF16)],
        [*parts, mine, other],
        "slopes",
        after=[hidden],
    )
    slopes_x, slopes_y = swap(slopes, x), swap(slopes, y)

    out = contract(
        hidden_all, straight_pieces, tall, False, cores, n_pipe, n_tensor, after=[slopes]
    )
    slopes_all = [
        slopes,
        slopes_x,
        slopes_y,
        swap(slopes_x[:, :rows], y),
        swap(slopes_y[:, rows:], x),
    ]
    came, layer_output = finish(out, cores, n_tensor)
    add_core = came[0]
    back = []
    for half in range(2):
        part = contract(
            slopes_all,
            balanced_pieces,
            wide,
            True,
            cores,
            n_pipe,
            n_tensor,
            half=half,
            after=came if half else [],
        )
        back.append(finish(part, cores, n_tensor)[1])
    return layer_output, jnp.concatenate(back, axis=1)


def solution(mesh):
    in_specs = (
        P(("dp", "tensor"), "pipe"),
        P(("dp", "tensor"), "pipe"),
        P(("dp", "pipe"), "tensor"),
        P(("dp", "pipe"), "tensor"),
        P("pipe", "tensor"),
        P("pipe", "tensor"),
        P("tensor", "pipe"),
    )
    out_specs = (P(("dp", "tensor"), "pipe"), P(("dp", "tensor"), "pipe"))

    def whole(*args):
        n_pipe, n_tensor = mesh.shape["pipe"], mesh.shape["tensor"]
        hidden_width = args[4].shape[1] // n_tensor
        if mesh.shape["dp"] == 2 and n_pipe == 4 and hidden_width % 256 == 0:
            body = functools.partial(balanced, n_tensor)
        else:
            body = functools.partial(direct, n_pipe, n_tensor)
        return jax.shard_map(
            body, mesh=mesh, in_specs=in_specs, out_specs=out_specs, check_vma=False
        )(*args)

    return whole
```

```python
import functools

import jax
import jax.numpy as jnp
from jax import lax
from jax.experimental import pallas as pl
from jax.experimental.pallas import tpu as pltpu
from jax.sharding import PartitionSpec as P

F32 = jnp.float32
BF16 = jnp.bfloat16
VMEM_BYTES = 16 * 1024 * 1024
LOAD_BYTES = 24 * 1024 * 1024
CONTRACT_LAST = (((1,), (1,)), ((), ()))
IN_VMEM = pl.BlockSpec(memory_space=pltpu.VMEM)
IN_PLACE = pl.BlockSpec(memory_space=pl.ANY)


def exchange(value, axis, size, step):
    return lax.ppermute(value, axis, [(i, i ^ step) for i in range(size)])


def pick_tile(width):
    return 256 if width % 256 == 0 else 128


def cost(flops, moved):
    return pl.CostEstimate(flops=flops, bytes_accessed=moved, transcendentals=0)


def params():
    return pltpu.CompilerParams(vmem_limit_bytes=VMEM_BYTES)


def small_kernel(body, outs, inputs, name, after=()):
    n_in, n_after = len(inputs), len(after)

    def kernel(*refs):
        body(refs[:n_in], refs[n_in + n_after :])

    moved = sum(a.size * a.dtype.itemsize for a in inputs)
    return pl.pallas_call(
        kernel,
        in_specs=[IN_VMEM] * n_in + [IN_PLACE] * n_after,
        out_specs=[IN_VMEM] * len(outs),
        out_shape=[jax.ShapeDtypeStruct(shape, dtype) for shape, dtype in outs],
        cost_estimate=cost(moved, moved),
        compiler_params=params(),
        name=name,
    )(*inputs, *after)


def load_weights(gate_weight, up_weight, down_weight, cores):
    depth = gate_weight.shape[0]
    units = gate_weight.shape[1] // cores
    cuts = 4
    rows, unit_rows = depth // cuts, units // cuts

    def kernel(gate, up, down, wide, tall, sems):
        first = pl.multiple_of(lax.axis_index("dp") * units, units) if cores > 1 else 0
        copies = []
        for i in range(cuts):
            for k, ref in enumerate((gate, up)):
                at = pl.ds(i * rows, rows)
                copies.append((ref.at[at, pl.ds(first, units)], wide.at[k, at]))
        for i in range(cuts):
            at = pl.multiple_of(first + i * unit_rows, unit_rows)
            copies.append((down.at[pl.ds(at, unit_rows)], tall.at[0, pl.ds(i * unit_rows, unit_rows)]))
        copies = [
            pltpu.make_async_copy(source, target, sems.at[i])
            for i, (source, target) in enumerate(copies)
        ]
        for copy in copies:
            copy.start()
        for copy in copies:
            copy.wait()

    return pl.pallas_call(
        kernel,
        in_specs=[IN_PLACE] * 3,
        out_specs=[IN_VMEM] * 2,
        out_shape=[
            jax.ShapeDtypeStruct((2, depth, units), BF16),
            jax.ShapeDtypeStruct((1, units, depth), BF16),
        ],
        scratch_shapes=[pltpu.SemaphoreType.DMA((3 * cuts,))],
        compiler_params=pltpu.CompilerParams(vmem_limit_bytes=LOAD_BYTES),
        cost_estimate=cost(0, 6 * depth * units),
        name="load_weights",
    )(gate_weight, up_weight, down_weight)


def project(inputs, weights, transposed, layout, n_pipe, n_tensor, after=()):
    cores = len(inputs)
    flat = [x for pair in inputs for x in pair]
    n_in, n_after, n_out, kinds = len(flat), len(after), len(layout), weights.shape[0]
    block, depth = inputs[0][0].shape
    tokens = block * n_tensor
    units = weights.shape[1] if transposed else weights.shape[2]
    tile = pick_tile(units)
    count = units // tile
    rows = tokens // n_pipe

    def kernel(*refs):
        x_refs = refs[:n_in]
        held = refs[n_in]
        out_refs = refs[n_in + 1 + n_after : n_in + 1 + n_after + n_out]
        natural, ordered = refs[n_in + 1 + n_after + n_out :]
        t = lax.axis_index("tensor")
        p = lax.axis_index("pipe")

        def work(j, carry):
            at = pl.multiple_of(j * tile, tile)
            for k in range(kinds):
                if transposed:
                    total = lax.dot_general(
                        ordered[...], held[k, pl.ds(at, tile), :], CONTRACT_LAST, preferred_element_type=F32
                    )
                else:
                    total = jnp.dot(
                        ordered[...], held[k, :, pl.ds(at, tile)], preferred_element_type=F32
                    )
                for ref, (_, pieces) in zip(out_refs, layout):
                    for i, (s, a) in enumerate(pieces):
                        row = (s * cores + a) * rows
                        part = total[row : row + rows].astype(ref.dtype)
                        ref[k, i * rows : (i + 1) * rows, pl.ds(at, tile)] = part
            return carry

        def own_block(a, s):
            if s == 0:
                return x_refs[2 * a][...]
            return x_refs[2 * a + 1][(s - 1) * block : s * block, :]

        for a in range(cores):
            if block == rows:
                for s in range(n_tensor):
                    start = pl.multiple_of(((p ^ t ^ s) * cores + a) * rows, rows)
                    ordered[pl.ds(start, rows), :] = own_block(a, s)
                continue
            for s in range(n_tensor):
                start = pl.multiple_of((t ^ s) * block, block)
                natural[pl.ds(start, block), :] = own_block(a, s)
            for s in range(n_pipe):
                start = pl.multiple_of((p ^ s) * rows, rows)
                at = (s * cores + a) * rows
                ordered[at : at + rows, :] = natural[pl.ds(start, rows), :]
        lax.fori_loop(0, count, work, 0, unroll=True)

    return pl.pallas_call(
        kernel,
        in_specs=[IN_VMEM] * (n_in + 1) + [IN_PLACE] * n_after,
        out_specs=[IN_VMEM] * n_out,
        out_shape=[
            jax.ShapeDtypeStruct((kinds, len(pieces) * rows, units), dtype)
            for dtype, pieces in layout
        ],
        scratch_shapes=[
            pltpu.VMEM((tokens, depth), BF16),
            pltpu.VMEM((cores * tokens, depth), BF16),
        ],
        compiler_params=params(),
        cost_estimate=cost(0, 0) if transposed else cost(2 * cores * tokens * depth * units * kinds, 2 * depth * units * kinds),
        name="pull_back" if transposed else "project",
    )(*flat, weights, *after)


def contract(blocks, pieces, weights, transposed, cores, n_pipe, n_tensor, after=()):
    kinds, _, units = blocks[0].shape
    n_in, n_after = len(blocks), len(after)
    from_rows = blocks[0].shape[1] // cores
    tokens = from_rows * n_pipe
    to_rows = tokens // n_tensor
    width = weights.shape[1] if transposed else weights.shape[2]
    tile = pick_tile(width)
    count = width // tile

    def kernel(*refs):
        x_refs = refs[:n_in]
        held = refs[n_in]
        out_refs = refs[n_in + 1 + n_after : n_in + 1 + n_after + cores]
        natural, ordered = refs[n_in + 1 + n_after + cores :]
        t = lax.axis_index("tensor")
        p = lax.axis_index("pipe")

        def work(j, carry):
            at = pl.multiple_of(j * tile, tile)
            total = None
            for k in range(kinds):
                if transposed:
                    part = lax.dot_general(
                        ordered[k], held[k, pl.ds(at, tile), :], CONTRACT_LAST, preferred_element_type=F32
                    )
                else:
                    part = jnp.dot(
                        ordered[k], held[k, :, pl.ds(at, tile)], preferred_element_type=F32
                    )
                total = part if total is None else total + part
            for a in range(cores):
                part = total[a * tokens : (a + 1) * tokens]
                out_refs[a][:, pl.ds(at, tile)] = part.astype(out_refs[a].dtype)
            return carry

        def came(k, a, s):
            place, row = pieces[s][a]
            return x_refs[place][k, row : row + from_rows, :]

        for k in range(kinds):
            for a in range(cores):
                if from_rows == to_rows:
                    for s in range(n_pipe):
                        start = pl.multiple_of(a * tokens + (t ^ p ^ s) * to_rows, to_rows)
                        ordered[k, pl.ds(start, to_rows), :] = came(k, a, s)
                    continue
                for s in range(n_pipe):
                    start = pl.multiple_of((p ^ s) * from_rows, from_rows)
                    natural[pl.ds(start, from_rows), :] = came(k, a, s)
                for s in range(n_tensor):
                    start = pl.multiple_of((t ^ s) * to_rows, to_rows)
                    at = a * tokens + s * to_rows
                    ordered[k, at : at + to_rows, :] = natural[pl.ds(start, to_rows), :]
        lax.fori_loop(0, count, work, 0, unroll=True)

    return pl.pallas_call(
        kernel,
        in_specs=[IN_VMEM] * (n_in + 1) + [IN_PLACE] * n_after,
        out_specs=[IN_VMEM] * cores,
        out_shape=[
            jax.ShapeDtypeStruct((tokens, width), BF16 if a else F32) for a in range(cores)
        ],
        scratch_shapes=[
            pltpu.VMEM((tokens, units), BF16),
            pltpu.VMEM((kinds, cores * tokens, units), BF16),
        ],
        compiler_params=params(),
        cost_estimate=cost(2 * cores * tokens * units * width * kinds, 2 * units * width * kinds),
        name="input_grad" if transposed else "layer_output",
    )(*blocks, weights, *after)


def gather_first(value, n_tensor):
    came = {s: exchange(value, "tensor", n_tensor, s) for s in range(n_tensor - 1, 0, -1)}
    return [value] + [came[s] for s in range(1, n_tensor)]


def gather_tokens(blocks, other, cores, after=()):
    own, came = blocks[0], blocks[1:]
    rows, width = own.shape

    def body(ins, outs):
        for s, ref in enumerate(ins):
            outs[0][s * rows : (s + 1) * rows, :] = ref[...]

    shape = (rows * len(came), width)
    (rest,) = small_kernel(body, [(shape, BF16)], came, "assemble", after)
    if cores == 1:
        return [(own, rest)]
    return [(own, rest), (other, exchange(rest, "dp", cores, 1))]


def finish(partials, cores, n_tensor, after=()):
    if cores > 1:
        other = exchange(partials[1], "dp", cores, 1)
        rows, width = other.shape[0] // n_tensor, other.shape[1]

        def body(ins, outs):
            for s in range(n_tensor):
                at = slice(s * rows, (s + 1) * rows)
                outs[s][...] = (ins[0][at] + ins[1][at].astype(F32)).astype(outs[s].dtype)

        parts = small_kernel(
            body,
            [((rows, width), BF16 if s else F32) for s in range(n_tensor)],
            [partials[0], other],
            "add_core",
            after,
        )
    else:
        rows = partials[0].shape[0] // n_tensor
        parts = [
            partials[0][s * rows : (s + 1) * rows].astype(BF16 if s else F32)
            for s in range(n_tensor)
        ]

    came = [exchange(parts[s], "tensor", n_tensor, s) for s in range(n_tensor - 1, 0, -1)]
    total = parts[0]
    for value in came:
        total = total + value.astype(F32)
    return came, total.astype(BF16)


def slope_values(grad, gate, up):
    gate, up = gate.astype(F32), up.astype(F32)
    sigma = jax.nn.sigmoid(gate)
    gate_slope = (grad * up * sigma * (1.0 + gate * (1.0 - sigma))).astype(BF16)
    up_slope = (grad * gate * sigma).astype(BF16)
    return gate_slope, up_slope


def direct(
    n_pipe, n_tensor, forward_acts, backward_grad, stored_gate, stored_up, gate_weight, up_weight, down_weight
):
    layout = [(BF16 if s else F32, [(s, 0)]) for s in range(n_pipe)]
    pieces = [[(s, 0)] for s in range(n_pipe)]

    def total_of(parts):
        total = parts[0]
        for s in range(1, n_pipe):
            total = total + exchange(parts[s], "pipe", n_pipe, s).astype(F32)
        return total

    def gather(value):
        return [value] + [exchange(value, "pipe", n_pipe, s) for s in range(1, n_pipe)]

    wide, tall = load_weights(gate_weight, up_weight, down_weight, 1)
    grads = gather_tokens(gather_first(backward_grad, n_tensor), None, 1)
    acts = gather_tokens(gather_first(forward_acts, n_tensor), None, 1)
    grad = total_of(project(grads, tall, True, layout, n_pipe, n_tensor))[0]
    slopes = gather(jnp.stack(slope_values(grad, stored_gate, stored_up)))
    summed = total_of(project(acts, wide, False, layout, n_pipe, n_tensor))
    hidden = gather((jax.nn.silu(summed[:1]) * summed[1:]).astype(BF16))
    back = contract(slopes, pieces, wide, True, 1, n_pipe, n_tensor)
    out = contract(hidden, pieces, tall, False, 1, n_pipe, n_tensor)
    return finish(out, 1, n_tensor)[1], finish(back, 1, n_tensor)[1]


def balanced(
    n_tensor, forward_acts, backward_grad, stored_gate, stored_up, gate_weight, up_weight, down_weight
):
    cores, n_pipe, x, y = 2, 4, 1, 2
    units = gate_weight.shape[1] // cores
    rows = stored_gate.shape[0]
    straight = [(BF16 if s else F32, [(s, 0), (s, 1)]) for s in range(n_pipe)]
    balanced_layout = [
        (F32, [(0, 0), (0, 1), (1, 1), (2, 0)]),
        (BF16, [(3, 0), (1, 0)]),
        (BF16, [(3, 1), (2, 1)]),
    ]
    straight_pieces = [[(s, 0), (s, rows)] for s in range(n_pipe)]
    balanced_pieces = straight_pieces[:3] + [[(3, 0), (4, 0)]]


    def swap(value, step):
        return exchange(value, "pipe", n_pipe, step)

    def slopes_body(ins, outs):
        keep, came = ins[0], ins[1:n_pipe]
        for a in range(cores):
            at = slice(a * rows, (a + 1) * rows)
            grad = keep[0, at]
            for ref in came:
                grad = grad + ref[0, at].astype(F32)
            stored = ins[n_pipe + a]
            gate_slope, up_slope = slope_values(grad, stored[0], stored[1])
            outs[0][0, at] = gate_slope
            outs[0][1, at] = up_slope

    def pass_on_body(ins, outs):
        keep, came_x, came_y = ins
        for k in range(2):
            on_x = keep[k, 2 * rows : 3 * rows] + came_y[k, :rows].astype(F32)
            on_y = keep[k, 3 * rows : 4 * rows] + came_x[k, :rows].astype(F32)
            outs[0][k] = on_x.astype(BF16)
            outs[1][k] = on_y.astype(BF16)

    def hidden_body(ins, outs):
        keep, came_x, came_y, then_x, then_y = ins
        for a, near, far in ((0, came_x, then_y), (1, came_y, then_x)):
            at = slice(a * rows, (a + 1) * rows)
            gate, up = [
                keep[k, at] + near[k, rows:].astype(F32) + far[k].astype(F32) for k in range(2)
            ]
            outs[0][0, at] = (jax.nn.silu(gate) * up).astype(BF16)

    def stored_body(ins, outs):
        core = lax.axis_index("dp")
        for k in range(2):
            for c in range(cores):
                start = pl.multiple_of((core ^ c) * units, units)
                outs[c][k] = ins[k][:, pl.ds(start, units)]

    acts = gather_first(forward_acts, n_tensor)
    grads = gather_first(backward_grad, n_tensor)
    wide, tall = load_weights(gate_weight, up_weight, down_weight, cores)
    other_acts = exchange(forward_acts, "dp", cores, 1)
    other_grads = exchange(backward_grad, "dp", cores, 1)
    acts = gather_tokens(acts, other_acts, cores, after=[tall, other_acts, grads[1]])
    keep, for_x, for_y = project(
        acts, wide, False, balanced_layout, n_pipe, n_tensor, after=[other_grads]
    )
    came_x, came_y = swap(for_x, x), swap(for_y, y)
    mine, other = small_kernel(
        stored_body, [((2, rows, units), BF16)] * 2, [stored_gate, stored_up], "stored", after=[keep]
    )
    other = exchange(other, "dp", cores, 1)
    grads = gather_tokens(grads, other_grads, cores, after=[keep])
    parts = project(grads, tall, True, straight, n_pipe, n_tensor, after=[other])
    parts = [parts[0]] + [swap(parts[s], s) for s in (3, 1, 2)]

    half = ((2, rows, units), BF16)
    on_x, on_y = small_kernel(
        pass_on_body, [half, half], [keep, came_x, came_y], "pass_on", after=[parts[0]]
    )
    sums = [keep, came_x, came_y, swap(on_x, x), swap(on_y, y)]
    (hidden,) = small_kernel(hidden_body, [((1, cores * rows, units), BF16)], sums, "hidden")
    hidden_all = [hidden] + [swap(hidden, s) for s in range(1, n_pipe)]

    (slopes,) = small_kernel(
        slopes_body,
        [((2, cores * rows, units), BF16)],
        [*parts, mine, other],
        "slopes",
        after=[hidden],
    )
    slopes_x, slopes_y = swap(slopes, x), swap(slopes, y)

    out = contract(
        hidden_all, straight_pieces, tall, False, cores, n_pipe, n_tensor, after=[slopes]
    )
    slopes_all = [
        slopes,
        slopes_x,
        slopes_y,
        swap(slopes_x[:, :rows], y),
        swap(slopes_y[:, rows:], x),
    ]
    came, layer_output = finish(out, cores, n_tensor)
    back = contract(
        slopes_all,
        balanced_pieces,
        wide,
        True,
        cores,
        n_pipe,
        n_tensor,
    )

    def copy_body(ins, outs):
        outs[0][...] = ins[0][...]

    (held,) = small_kernel(copy_body, [(back[1].shape, BF16)], back[1:], "hold", after=came)
    _, input_grad = finish([back[0], held], cores, n_tensor)
    return layer_output, input_grad


def solution(mesh):
    in_specs = (
        P(("dp", "tensor"), "pipe"),
        P(("dp", "tensor"), "pipe"),
        P(("dp", "pipe"), "tensor"),
        P(("dp", "pipe"), "tensor"),
        P("pipe", "tensor"),
        P("pipe", "tensor"),
        P("tensor", "pipe"),
    )
    out_specs = (P(("dp", "tensor"), "pipe"), P(("dp", "tensor"), "pipe"))

    def whole(*args):
        n_pipe, n_tensor = mesh.shape["pipe"], mesh.shape["tensor"]
        hidden_width = args[4].shape[1] // n_tensor
        if mesh.shape["dp"] == 2 and n_pipe == 4 and hidden_width % 256 == 0:
            body = functools.partial(balanced, n_tensor)
        else:
            body = functools.partial(direct, n_pipe, n_tensor)
        return jax.shard_map(
            body, mesh=mesh, in_specs=in_specs, out_specs=out_specs, check_vma=False
        )(*args)

    return whole
```

```python
import functools

import jax
import jax.numpy as jnp
from jax import lax
from jax.experimental import pallas as pl
from jax.experimental.pallas import tpu as pltpu
from jax.sharding import PartitionSpec as P

F32 = jnp.float32
BF16 = jnp.bfloat16
VMEM_BYTES = 16 * 1024 * 1024
LOAD_BYTES = 24 * 1024 * 1024
CONTRACT_LAST = (((1,), (1,)), ((), ()))
IN_VMEM = pl.BlockSpec(memory_space=pltpu.VMEM)
IN_PLACE = pl.BlockSpec(memory_space=pl.ANY)


def exchange(value, axis, size, step):
    return lax.ppermute(value, axis, [(i, i ^ step) for i in range(size)])


def pick_tile(width):
    return 256 if width % 256 == 0 else 128


def cost(flops, moved):
    return pl.CostEstimate(flops=flops, bytes_accessed=moved, transcendentals=0)


def params():
    return pltpu.CompilerParams(vmem_limit_bytes=VMEM_BYTES)


def small_kernel(body, outs, inputs, name, after=()):
    n_in, n_after = len(inputs), len(after)

    def kernel(*refs):
        body(refs[:n_in], refs[n_in + n_after :])

    moved = sum(a.size * a.dtype.itemsize for a in inputs)
    return pl.pallas_call(
        kernel,
        in_specs=[IN_VMEM] * n_in + [IN_PLACE] * n_after,
        out_specs=[IN_VMEM] * len(outs),
        out_shape=[jax.ShapeDtypeStruct(shape, dtype) for shape, dtype in outs],
        cost_estimate=cost(moved, moved),
        compiler_params=params(),
        name=name,
    )(*inputs, *after)


def load_weights(gate_weight, up_weight, down_weight, cores):
    depth = gate_weight.shape[0]
    units = gate_weight.shape[1] // cores
    cuts = 4
    rows, unit_rows = depth // cuts, units // cuts

    def kernel(gate, up, down, wide, tall, sems):
        first = pl.multiple_of(lax.axis_index("dp") * units, units) if cores > 1 else 0
        copies = []
        for i in range(cuts):
            for k, ref in enumerate((gate, up)):
                at = pl.ds(i * rows, rows)
                copies.append((ref.at[at, pl.ds(first, units)], wide.at[k, at]))
        for i in range(cuts):
            at = pl.multiple_of(first + i * unit_rows, unit_rows)
            copies.append((down.at[pl.ds(at, unit_rows)], tall.at[0, pl.ds(i * unit_rows, unit_rows)]))
        copies = [
            pltpu.make_async_copy(source, target, sems.at[i])
            for i, (source, target) in enumerate(copies)
        ]
        for copy in copies:
            copy.start()
        for copy in copies:
            copy.wait()

    return pl.pallas_call(
        kernel,
        in_specs=[IN_PLACE] * 3,
        out_specs=[IN_VMEM] * 2,
        out_shape=[
            jax.ShapeDtypeStruct((2, depth, units), BF16),
            jax.ShapeDtypeStruct((1, units, depth), BF16),
        ],
        scratch_shapes=[pltpu.SemaphoreType.DMA((3 * cuts,))],
        compiler_params=pltpu.CompilerParams(vmem_limit_bytes=LOAD_BYTES),
        cost_estimate=cost(0, 6 * depth * units),
        name="load_weights",
    )(gate_weight, up_weight, down_weight)


def project(inputs, weights, transposed, layout, n_pipe, n_tensor, after=()):
    cores = len(inputs)
    flat = [x for pair in inputs for x in pair]
    n_in, n_after, n_out, kinds = len(flat), len(after), len(layout), weights.shape[0]
    block, depth = inputs[0][0].shape
    tokens = block * n_tensor
    units = weights.shape[1] if transposed else weights.shape[2]
    tile = pick_tile(units)
    count = units // tile
    rows = tokens // n_pipe

    def kernel(*refs):
        x_refs = refs[:n_in]
        held = refs[n_in]
        out_refs = refs[n_in + 1 + n_after : n_in + 1 + n_after + n_out]
        natural, ordered = refs[n_in + 1 + n_after + n_out :]
        t = lax.axis_index("tensor")
        p = lax.axis_index("pipe")

        def work(j, carry):
            at = pl.multiple_of(j * tile, tile)
            for k in range(kinds):
                if transposed:
                    total = lax.dot_general(
                        ordered[...], held[k, pl.ds(at, tile), :], CONTRACT_LAST, preferred_element_type=F32
                    )
                else:
                    total = jnp.dot(
                        ordered[...], held[k, :, pl.ds(at, tile)], preferred_element_type=F32
                    )
                for ref, (_, pieces) in zip(out_refs, layout):
                    for i, (s, a) in enumerate(pieces):
                        row = (s * cores + a) * rows
                        part = total[row : row + rows].astype(ref.dtype)
                        ref[k, i * rows : (i + 1) * rows, pl.ds(at, tile)] = part
            return carry

        def own_block(a, s):
            if s == 0:
                return x_refs[2 * a][...]
            return x_refs[2 * a + 1][(s - 1) * block : s * block, :]

        for a in range(cores):
            if block == rows:
                for s in range(n_tensor):
                    start = pl.multiple_of(((p ^ t ^ s) * cores + a) * rows, rows)
                    ordered[pl.ds(start, rows), :] = own_block(a, s)
                continue
            for s in range(n_tensor):
                start = pl.multiple_of((t ^ s) * block, block)
                natural[pl.ds(start, block), :] = own_block(a, s)
            for s in range(n_pipe):
                start = pl.multiple_of((p ^ s) * rows, rows)
                at = (s * cores + a) * rows
                ordered[at : at + rows, :] = natural[pl.ds(start, rows), :]
        lax.fori_loop(0, count, work, 0, unroll=True)

    return pl.pallas_call(
        kernel,
        in_specs=[IN_VMEM] * (n_in + 1) + [IN_PLACE] * n_after,
        out_specs=[IN_VMEM] * n_out,
        out_shape=[
            jax.ShapeDtypeStruct((kinds, len(pieces) * rows, units), dtype)
            for dtype, pieces in layout
        ],
        scratch_shapes=[
            pltpu.VMEM((tokens, depth), BF16),
            pltpu.VMEM((cores * tokens, depth), BF16),
        ],
        compiler_params=params(),
        cost_estimate=cost(0, 0) if transposed else cost(2 * cores * tokens * depth * units * kinds, 2 * depth * units * kinds),
        name="pull_back" if transposed else "project",
    )(*flat, weights, *after)


def contract(blocks, pieces, weights, transposed, cores, n_pipe, n_tensor, after=()):
    kinds, _, units = blocks[0].shape
    n_in, n_after = len(blocks), len(after)
    from_rows = blocks[0].shape[1] // cores
    tokens = from_rows * n_pipe
    to_rows = tokens // n_tensor
    width = weights.shape[1] if transposed else weights.shape[2]
    tile = pick_tile(width)
    count = width // tile

    def kernel(*refs):
        x_refs = refs[:n_in]
        held = refs[n_in]
        out_refs = refs[n_in + 1 + n_after : n_in + 1 + n_after + cores]
        natural, ordered = refs[n_in + 1 + n_after + cores :]
        t = lax.axis_index("tensor")
        p = lax.axis_index("pipe")

        def work(j, carry):
            at = pl.multiple_of(j * tile, tile)
            total = None
            for k in range(kinds):
                if transposed:
                    part = lax.dot_general(
                        ordered[k], held[k, pl.ds(at, tile), :], CONTRACT_LAST, preferred_element_type=F32
                    )
                else:
                    part = jnp.dot(
                        ordered[k], held[k, :, pl.ds(at, tile)], preferred_element_type=F32
                    )
                total = part if total is None else total + part
            for a in range(cores):
                part = total[a * tokens : (a + 1) * tokens]
                out_refs[a][:, pl.ds(at, tile)] = part.astype(out_refs[a].dtype)
            return carry

        def came(k, a, s):
            place, row = pieces[s][a]
            return x_refs[place][k, row : row + from_rows, :]

        for k in range(kinds):
            for a in range(cores):
                if from_rows == to_rows:
                    for s in range(n_pipe):
                        start = pl.multiple_of(a * tokens + (t ^ p ^ s) * to_rows, to_rows)
                        ordered[k, pl.ds(start, to_rows), :] = came(k, a, s)
                    continue
                for s in range(n_pipe):
                    start = pl.multiple_of((p ^ s) * from_rows, from_rows)
                    natural[pl.ds(start, from_rows), :] = came(k, a, s)
                for s in range(n_tensor):
                    start = pl.multiple_of((t ^ s) * to_rows, to_rows)
                    at = a * tokens + s * to_rows
                    ordered[k, at : at + to_rows, :] = natural[pl.ds(start, to_rows), :]
        lax.fori_loop(0, count, work, 0, unroll=True)

    return pl.pallas_call(
        kernel,
        in_specs=[IN_VMEM] * (n_in + 1) + [IN_PLACE] * n_after,
        out_specs=[IN_VMEM] * cores,
        out_shape=[
            jax.ShapeDtypeStruct((tokens, width), BF16 if a else F32) for a in range(cores)
        ],
        scratch_shapes=[
            pltpu.VMEM((tokens, units), BF16),
            pltpu.VMEM((kinds, cores * tokens, units), BF16),
        ],
        compiler_params=params(),
        cost_estimate=cost(2 * cores * tokens * units * width * kinds, 2 * units * width * kinds),
        name="input_grad" if transposed else "layer_output",
    )(*blocks, weights, *after)


def gather_first(value, n_tensor):
    came = {s: exchange(value, "tensor", n_tensor, s) for s in range(n_tensor - 1, 0, -1)}
    return [value] + [came[s] for s in range(1, n_tensor)]


def gather_tokens(blocks, other, cores, after=()):
    own, came = blocks[0], blocks[1:]
    rows, width = own.shape

    def body(ins, outs):
        for s, ref in enumerate(ins):
            outs[0][s * rows : (s + 1) * rows, :] = ref[...]

    shape = (rows * len(came), width)
    (rest,) = small_kernel(body, [(shape, BF16)], came, "assemble", after)
    if cores == 1:
        return [(own, rest)]
    return [(own, rest), (other, exchange(rest, "dp", cores, 1))]


def finish(partials, cores, n_tensor, after=()):
    if cores > 1:
        other = exchange(partials[1], "dp", cores, 1)
        rows, width = other.shape[0] // n_tensor, other.shape[1]

        def body(ins, outs):
            for s in range(n_tensor):
                at = slice(s * rows, (s + 1) * rows)
                outs[s][...] = (ins[0][at] + ins[1][at].astype(F32)).astype(outs[s].dtype)

        parts = small_kernel(
            body,
            [((rows, width), BF16 if s else F32) for s in range(n_tensor)],
            [partials[0], other],
            "add_core",
            after,
        )
    else:
        rows = partials[0].shape[0] // n_tensor
        parts = [
            partials[0][s * rows : (s + 1) * rows].astype(BF16 if s else F32)
            for s in range(n_tensor)
        ]

    came = [exchange(parts[s], "tensor", n_tensor, s) for s in range(n_tensor - 1, 0, -1)]
    total = parts[0]
    for value in came:
        total = total + value.astype(F32)
    return came, total.astype(BF16)


def slope_values(grad, gate, up):
    gate, up = gate.astype(F32), up.astype(F32)
    sigma = jax.nn.sigmoid(gate)
    gate_slope = (grad * up * sigma * (1.0 + gate * (1.0 - sigma))).astype(BF16)
    up_slope = (grad * gate * sigma).astype(BF16)
    return gate_slope, up_slope


def direct(
    n_pipe, n_tensor, forward_acts, backward_grad, stored_gate, stored_up, gate_weight, up_weight, down_weight
):
    layout = [(BF16 if s else F32, [(s, 0)]) for s in range(n_pipe)]
    pieces = [[(s, 0)] for s in range(n_pipe)]

    def total_of(parts):
        total = parts[0]
        for s in range(1, n_pipe):
            total = total + exchange(parts[s], "pipe", n_pipe, s).astype(F32)
        return total

    def gather(value):
        return [value] + [exchange(value, "pipe", n_pipe, s) for s in range(1, n_pipe)]

    wide, tall = load_weights(gate_weight, up_weight, down_weight, 1)
    grads = gather_tokens(gather_first(backward_grad, n_tensor), None, 1)
    acts = gather_tokens(gather_first(forward_acts, n_tensor), None, 1)
    grad = total_of(project(grads, tall, True, layout, n_pipe, n_tensor))[0]
    slopes = gather(jnp.stack(slope_values(grad, stored_gate, stored_up)))
    summed = total_of(project(acts, wide, False, layout, n_pipe, n_tensor))
    hidden = gather((jax.nn.silu(summed[:1]) * summed[1:]).astype(BF16))
    back = contract(slopes, pieces, wide, True, 1, n_pipe, n_tensor)
    out = contract(hidden, pieces, tall, False, 1, n_pipe, n_tensor)
    return finish(out, 1, n_tensor)[1], finish(back, 1, n_tensor)[1]


def balanced(
    n_tensor, forward_acts, backward_grad, stored_gate, stored_up, gate_weight, up_weight, down_weight
):
    cores, n_pipe, x, y = 2, 4, 1, 2
    units = gate_weight.shape[1] // cores
    rows = stored_gate.shape[0]
    straight = [(BF16 if s else F32, [(s, 0), (s, 1)]) for s in range(n_pipe)]
    balanced_layout = [
        (F32, [(0, 0), (0, 1), (1, 1), (2, 0)]),
        (BF16, [(3, 0), (1, 0)]),
        (BF16, [(3, 1), (2, 1)]),
    ]
    straight_pieces = [[(s, 0), (s, rows)] for s in range(n_pipe)]
    balanced_pieces = straight_pieces[:3] + [[(3, 0), (4, 0)]]


    def swap(value, step):
        return exchange(value, "pipe", n_pipe, step)

    def slopes_body(ins, outs):
        keep, came = ins[0], ins[1:n_pipe]
        for a in range(cores):
            at = slice(a * rows, (a + 1) * rows)
            grad = keep[0, at]
            for ref in came:
                grad = grad + ref[0, at].astype(F32)
            stored = ins[n_pipe + a]
            gate_slope, up_slope = slope_values(grad, stored[0], stored[1])
            outs[0][0, at] = gate_slope
            outs[0][1, at] = up_slope

    def pass_on_body(ins, outs):
        keep, came_x, came_y = ins
        for k in range(2):
            on_x = keep[k, 2 * rows : 3 * rows] + came_y[k, :rows].astype(F32)
            on_y = keep[k, 3 * rows : 4 * rows] + came_x[k, :rows].astype(F32)
            outs[0][k] = on_x.astype(BF16)
            outs[1][k] = on_y.astype(BF16)

    def hidden_body(ins, outs):
        keep, came_x, came_y, then_x, then_y = ins
        for a, near, far in ((0, came_x, then_y), (1, came_y, then_x)):
            at = slice(a * rows, (a + 1) * rows)
            gate, up = [
                keep[k, at] + near[k, rows:].astype(F32) + far[k].astype(F32) for k in range(2)
            ]
            outs[0][0, at] = (jax.nn.silu(gate) * up).astype(BF16)

    def stored_body(ins, outs):
        core = lax.axis_index("dp")
        for k in range(2):
            for c in range(cores):
                start = pl.multiple_of((core ^ c) * units, units)
                outs[c][k] = ins[k][:, pl.ds(start, units)]

    acts = gather_first(forward_acts, n_tensor)
    grads = gather_first(backward_grad, n_tensor)
    wide, tall = load_weights(gate_weight, up_weight, down_weight, cores)
    other_acts = exchange(forward_acts, "dp", cores, 1)
    other_grads = exchange(backward_grad, "dp", cores, 1)
    acts = gather_tokens(acts, other_acts, cores, after=[tall, other_acts, grads[1]])
    keep, for_x, for_y = project(
        acts, wide, False, balanced_layout, n_pipe, n_tensor
    )
    came_x, came_y = swap(for_x, x), swap(for_y, y)
    mine, other = small_kernel(
        stored_body, [((2, rows, units), BF16)] * 2, [stored_gate, stored_up], "stored", after=[keep]
    )
    other = exchange(other, "dp", cores, 1)
    grads = gather_tokens(grads, other_grads, cores, after=[keep])
    parts = project(grads, tall, True, straight, n_pipe, n_tensor, after=[other])
    parts = [parts[0]] + [swap(parts[s], s) for s in (3, 1, 2)]

    half = ((2, rows, units), BF16)
    on_x, on_y = small_kernel(
        pass_on_body, [half, half], [keep, came_x, came_y], "pass_on", after=[parts[0]]
    )
    sums = [keep, came_x, came_y, swap(on_x, x), swap(on_y, y)]
    (hidden,) = small_kernel(hidden_body, [((1, cores * rows, units), BF16)], sums, "hidden")
    hidden_all = [hidden] + [swap(hidden, s) for s in range(1, n_pipe)]

    (slopes,) = small_kernel(
        slopes_body,
        [((2, cores * rows, units), BF16)],
        [*parts, mine, other],
        "slopes",
        after=[hidden],
    )
    slopes_x, slopes_y = swap(slopes, x), swap(slopes, y)

    out = contract(
        hidden_all, straight_pieces, tall, False, cores, n_pipe, n_tensor, after=[slopes]
    )
    slopes_all = [
        slopes,
        slopes_x,
        slopes_y,
        swap(slopes_x[:, :rows], y),
        swap(slopes_y[:, rows:], x),
    ]
    came, layer_output = finish(out, cores, n_tensor)
    back = contract(
        slopes_all,
        balanced_pieces,
        wide,
        True,
        cores,
        n_pipe,
        n_tensor,
    )

    def copy_body(ins, outs):
        outs[0][...] = ins[0][...]

    (held,) = small_kernel(copy_body, [(back[1].shape, BF16)], back[1:], "hold", after=came[:1])
    _, input_grad = finish([back[0], held], cores, n_tensor)
    return layer_output, input_grad


def solution(mesh):
    in_specs = (
        P(("dp", "tensor"), "pipe"),
        P(("dp", "tensor"), "pipe"),
        P(("dp", "pipe"), "tensor"),
        P(("dp", "pipe"), "tensor"),
        P("pipe", "tensor"),
        P("pipe", "tensor"),
        P("tensor", "pipe"),
    )
    out_specs = (P(("dp", "tensor"), "pipe"), P(("dp", "tensor"), "pipe"))

    def whole(*args):
        n_pipe, n_tensor = mesh.shape["pipe"], mesh.shape["tensor"]
        hidden_width = args[4].shape[1] // n_tensor
        if mesh.shape["dp"] == 2 and n_pipe == 4 and hidden_width % 256 == 0:
            body = functools.partial(balanced, n_tensor)
        else:
            body = functools.partial(direct, n_pipe, n_tensor)
        return jax.shard_map(
            body, mesh=mesh, in_specs=in_specs, out_specs=out_specs, check_vma=False
        )(*args)

    return whole
```

```python
import functools

import jax
import jax.numpy as jnp
from jax import lax
from jax.experimental import pallas as pl
from jax.experimental.pallas import tpu as pltpu
from jax.sharding import PartitionSpec as P

F32 = jnp.float32
BF16 = jnp.bfloat16
VMEM_BYTES = 16 * 1024 * 1024
LOAD_BYTES = 24 * 1024 * 1024
CONTRACT_LAST = (((1,), (1,)), ((), ()))
IN_VMEM = pl.BlockSpec(memory_space=pltpu.VMEM)
IN_PLACE = pl.BlockSpec(memory_space=pl.ANY)


def exchange(value, axis, size, step):
    return lax.ppermute(value, axis, [(i, i ^ step) for i in range(size)])


def pick_tile(width):
    return 256 if width % 256 == 0 else 128


def cost(flops, moved):
    return pl.CostEstimate(flops=flops, bytes_accessed=moved, transcendentals=0)


def params():
    return pltpu.CompilerParams(vmem_limit_bytes=VMEM_BYTES)


def small_kernel(body, outs, inputs, name, after=()):
    n_in, n_after = len(inputs), len(after)

    def kernel(*refs):
        body(refs[:n_in], refs[n_in + n_after :])

    moved = sum(a.size * a.dtype.itemsize for a in inputs)
    return pl.pallas_call(
        kernel,
        in_specs=[IN_VMEM] * n_in + [IN_PLACE] * n_after,
        out_specs=[IN_VMEM] * len(outs),
        out_shape=[jax.ShapeDtypeStruct(shape, dtype) for shape, dtype in outs],
        cost_estimate=cost(moved, moved),
        compiler_params=params(),
        name=name,
    )(*inputs, *after)


def load_weights(gate_weight, up_weight, down_weight, cores):
    depth = gate_weight.shape[0]
    units = gate_weight.shape[1] // cores
    cuts = 4
    rows, unit_rows = depth // cuts, units // cuts

    def kernel(gate, up, down, wide, tall, sems):
        first = pl.multiple_of(lax.axis_index("dp") * units, units) if cores > 1 else 0
        copies = []
        for i in range(cuts):
            for k, ref in enumerate((gate, up)):
                at = pl.ds(i * rows, rows)
                copies.append((ref.at[at, pl.ds(first, units)], wide.at[k, at]))
        for i in range(cuts):
            at = pl.multiple_of(first + i * unit_rows, unit_rows)
            copies.append((down.at[pl.ds(at, unit_rows)], tall.at[0, pl.ds(i * unit_rows, unit_rows)]))
        copies = [
            pltpu.make_async_copy(source, target, sems.at[i])
            for i, (source, target) in enumerate(copies)
        ]
        for copy in copies:
            copy.start()
        for copy in copies:
            copy.wait()

    return pl.pallas_call(
        kernel,
        in_specs=[IN_PLACE] * 3,
        out_specs=[IN_VMEM] * 2,
        out_shape=[
            jax.ShapeDtypeStruct((2, depth, units), BF16),
            jax.ShapeDtypeStruct((1, units, depth), BF16),
        ],
        scratch_shapes=[pltpu.SemaphoreType.DMA((3 * cuts,))],
        compiler_params=pltpu.CompilerParams(vmem_limit_bytes=LOAD_BYTES),
        cost_estimate=cost(0, 6 * depth * units),
        name="load_weights",
    )(gate_weight, up_weight, down_weight)


def project(inputs, weights, transposed, layout, n_pipe, n_tensor, after=()):
    cores = len(inputs)
    flat = [x for pair in inputs for x in pair]
    n_in, n_after, n_out, kinds = len(flat), len(after), len(layout), weights.shape[0]
    block, depth = inputs[0][0].shape
    tokens = block * n_tensor
    units = weights.shape[1] if transposed else weights.shape[2]
    tile = pick_tile(units)
    count = units // tile
    rows = tokens // n_pipe

    def kernel(*refs):
        x_refs = refs[:n_in]
        held = refs[n_in]
        out_refs = refs[n_in + 1 + n_after : n_in + 1 + n_after + n_out]
        natural, ordered = refs[n_in + 1 + n_after + n_out :]
        t = lax.axis_index("tensor")
        p = lax.axis_index("pipe")

        def work(j, carry):
            at = pl.multiple_of(j * tile, tile)
            for k in range(kinds):
                if transposed:
                    total = lax.dot_general(
                        ordered[...], held[k, pl.ds(at, tile), :], CONTRACT_LAST, preferred_element_type=F32
                    )
                else:
                    total = jnp.dot(
                        ordered[...], held[k, :, pl.ds(at, tile)], preferred_element_type=F32
                    )
                for ref, (_, pieces) in zip(out_refs, layout):
                    for i, (s, a) in enumerate(pieces):
                        row = (s * cores + a) * rows
                        part = total[row : row + rows].astype(ref.dtype)
                        ref[k, i * rows : (i + 1) * rows, pl.ds(at, tile)] = part
            return carry

        def own_block(a, s):
            if s == 0:
                return x_refs[2 * a][...]
            return x_refs[2 * a + 1][(s - 1) * block : s * block, :]

        for a in range(cores):
            if block == rows:
                for s in range(n_tensor):
                    start = pl.multiple_of(((p ^ t ^ s) * cores + a) * rows, rows)
                    ordered[pl.ds(start, rows), :] = own_block(a, s)
                continue
            for s in range(n_tensor):
                start = pl.multiple_of((t ^ s) * block, block)
                natural[pl.ds(start, block), :] = own_block(a, s)
            for s in range(n_pipe):
                start = pl.multiple_of((p ^ s) * rows, rows)
                at = (s * cores + a) * rows
                ordered[at : at + rows, :] = natural[pl.ds(start, rows), :]
        lax.fori_loop(0, count, work, 0, unroll=True)

    return pl.pallas_call(
        kernel,
        in_specs=[IN_VMEM] * (n_in + 1) + [IN_PLACE] * n_after,
        out_specs=[IN_VMEM] * n_out,
        out_shape=[
            jax.ShapeDtypeStruct((kinds, len(pieces) * rows, units), dtype)
            for dtype, pieces in layout
        ],
        scratch_shapes=[
            pltpu.VMEM((tokens, depth), BF16),
            pltpu.VMEM((cores * tokens, depth), BF16),
        ],
        compiler_params=params(),
        cost_estimate=cost(0, 0) if transposed else cost(2 * cores * tokens * depth * units * kinds, 2 * depth * units * kinds),
        name="pull_back" if transposed else "project",
    )(*flat, weights, *after)


def contract(blocks, pieces, weights, transposed, cores, n_pipe, n_tensor, after=()):
    kinds, _, units = blocks[0].shape
    n_in, n_after = len(blocks), len(after)
    from_rows = blocks[0].shape[1] // cores
    tokens = from_rows * n_pipe
    to_rows = tokens // n_tensor
    width = weights.shape[1] if transposed else weights.shape[2]
    tile = pick_tile(width)
    count = width // tile

    def kernel(*refs):
        x_refs = refs[:n_in]
        held = refs[n_in]
        out_refs = refs[n_in + 1 + n_after : n_in + 1 + n_after + cores]
        natural, ordered = refs[n_in + 1 + n_after + cores :]
        t = lax.axis_index("tensor")
        p = lax.axis_index("pipe")

        def work(j, carry):
            at = pl.multiple_of(j * tile, tile)
            total = None
            for k in range(kinds):
                if transposed:
                    part = lax.dot_general(
                        ordered[k], held[k, pl.ds(at, tile), :], CONTRACT_LAST, preferred_element_type=F32
                    )
                else:
                    part = jnp.dot(
                        ordered[k], held[k, :, pl.ds(at, tile)], preferred_element_type=F32
                    )
                total = part if total is None else total + part
            for a in range(cores):
                part = total[a * tokens : (a + 1) * tokens]
                out_refs[a][:, pl.ds(at, tile)] = part.astype(out_refs[a].dtype)
            return carry

        def came(k, a, s):
            place, row = pieces[s][a]
            return x_refs[place][k, row : row + from_rows, :]

        for k in range(kinds):
            for a in range(cores):
                if from_rows == to_rows:
                    for s in range(n_pipe):
                        start = pl.multiple_of(a * tokens + (t ^ p ^ s) * to_rows, to_rows)
                        ordered[k, pl.ds(start, to_rows), :] = came(k, a, s)
                    continue
                for s in range(n_pipe):
                    start = pl.multiple_of((p ^ s) * from_rows, from_rows)
                    natural[pl.ds(start, from_rows), :] = came(k, a, s)
                for s in range(n_tensor):
                    start = pl.multiple_of((t ^ s) * to_rows, to_rows)
                    at = a * tokens + s * to_rows
                    ordered[k, at : at + to_rows, :] = natural[pl.ds(start, to_rows), :]
        lax.fori_loop(0, count, work, 0, unroll=True)

    return pl.pallas_call(
        kernel,
        in_specs=[IN_VMEM] * (n_in + 1) + [IN_PLACE] * n_after,
        out_specs=[IN_VMEM] * cores,
        out_shape=[
            jax.ShapeDtypeStruct((tokens, width), BF16 if a else F32) for a in range(cores)
        ],
        scratch_shapes=[
            pltpu.VMEM((tokens, units), BF16),
            pltpu.VMEM((kinds, cores * tokens, units), BF16),
        ],
        compiler_params=params(),
        cost_estimate=cost(0, 0) if transposed else cost(2 * cores * tokens * units * width * kinds, 2 * units * width * kinds),
        name="input_grad" if transposed else "layer_output",
    )(*blocks, weights, *after)


def gather_first(value, n_tensor):
    came = {s: exchange(value, "tensor", n_tensor, s) for s in range(n_tensor - 1, 0, -1)}
    return [value] + [came[s] for s in range(1, n_tensor)]


def gather_tokens(blocks, other, cores, after=()):
    own, came = blocks[0], blocks[1:]
    rows, width = own.shape

    def body(ins, outs):
        for s, ref in enumerate(ins):
            outs[0][s * rows : (s + 1) * rows, :] = ref[...]

    shape = (rows * len(came), width)
    (rest,) = small_kernel(body, [(shape, BF16)], came, "assemble", after)
    if cores == 1:
        return [(own, rest)]
    return [(own, rest), (other, exchange(rest, "dp", cores, 1))]


def finish(partials, cores, n_tensor, after=()):
    if cores > 1:
        other = exchange(partials[1], "dp", cores, 1)
        rows, width = other.shape[0] // n_tensor, other.shape[1]

        def body(ins, outs):
            for s in range(n_tensor):
                at = slice(s * rows, (s + 1) * rows)
                outs[s][...] = (ins[0][at] + ins[1][at].astype(F32)).astype(outs[s].dtype)

        parts = small_kernel(
            body,
            [((rows, width), BF16 if s else F32) for s in range(n_tensor)],
            [partials[0], other],
            "add_core",
            after,
        )
    else:
        rows = partials[0].shape[0] // n_tensor
        parts = [
            partials[0][s * rows : (s + 1) * rows].astype(BF16 if s else F32)
            for s in range(n_tensor)
        ]

    came = [exchange(parts[s], "tensor", n_tensor, s) for s in range(n_tensor - 1, 0, -1)]
    total = parts[0]
    for value in came:
        total = total + value.astype(F32)
    return came, total.astype(BF16)


def slope_values(grad, gate, up):
    gate, up = gate.astype(F32), up.astype(F32)
    sigma = jax.nn.sigmoid(gate)
    gate_slope = (grad * up * sigma * (1.0 + gate * (1.0 - sigma))).astype(BF16)
    up_slope = (grad * gate * sigma).astype(BF16)
    return gate_slope, up_slope


def direct(
    n_pipe, n_tensor, forward_acts, backward_grad, stored_gate, stored_up, gate_weight, up_weight, down_weight
):
    layout = [(BF16 if s else F32, [(s, 0)]) for s in range(n_pipe)]
    pieces = [[(s, 0)] for s in range(n_pipe)]

    def total_of(parts):
        total = parts[0]
        for s in range(1, n_pipe):
            total = total + exchange(parts[s], "pipe", n_pipe, s).astype(F32)
        return total

    def gather(value):
        return [value] + [exchange(value, "pipe", n_pipe, s) for s in range(1, n_pipe)]

    wide, tall = load_weights(gate_weight, up_weight, down_weight, 1)
    grads = gather_tokens(gather_first(backward_grad, n_tensor), None, 1)
    acts = gather_tokens(gather_first(forward_acts, n_tensor), None, 1)
    grad = total_of(project(grads, tall, True, layout, n_pipe, n_tensor))[0]
    slopes = gather(jnp.stack(slope_values(grad, stored_gate, stored_up)))
    summed = total_of(project(acts, wide, False, layout, n_pipe, n_tensor))
    hidden = gather((jax.nn.silu(summed[:1]) * summed[1:]).astype(BF16))
    back = contract(slopes, pieces, wide, True, 1, n_pipe, n_tensor)
    out = contract(hidden, pieces, tall, False, 1, n_pipe, n_tensor)
    return finish(out, 1, n_tensor)[1], finish(back, 1, n_tensor)[1]


def balanced(
    n_tensor, forward_acts, backward_grad, stored_gate, stored_up, gate_weight, up_weight, down_weight
):
    cores, n_pipe, x, y = 2, 4, 1, 2
    units = gate_weight.shape[1] // cores
    rows = stored_gate.shape[0]
    straight = [(BF16 if s else F32, [(s, 0), (s, 1)]) for s in range(n_pipe)]
    balanced_layout = [
        (F32, [(0, 0), (0, 1), (1, 1), (2, 0)]),
        (BF16, [(3, 0), (1, 0)]),
        (BF16, [(3, 1), (2, 1)]),
    ]
    straight_pieces = [[(s, 0), (s, rows)] for s in range(n_pipe)]
    balanced_pieces = straight_pieces[:3] + [[(3, 0), (4, 0)]]


    def swap(value, step):
        return exchange(value, "pipe", n_pipe, step)

    def slopes_body(ins, outs):
        keep, came = ins[0], ins[1:n_pipe]
        for a in range(cores):
            at = slice(a * rows, (a + 1) * rows)
            grad = keep[0, at]
            for ref in came:
                grad = grad + ref[0, at].astype(F32)
            stored = ins[n_pipe + a]
            gate_slope, up_slope = slope_values(grad, stored[0], stored[1])
            outs[0][0, at] = gate_slope
            outs[0][1, at] = up_slope

    def pass_on_body(ins, outs):
        keep, came_x, came_y = ins
        for k in range(2):
            on_x = keep[k, 2 * rows : 3 * rows] + came_y[k, :rows].astype(F32)
            on_y = keep[k, 3 * rows : 4 * rows] + came_x[k, :rows].astype(F32)
            outs[0][k] = on_x.astype(BF16)
            outs[1][k] = on_y.astype(BF16)

    def hidden_body(ins, outs):
        keep, came_x, came_y, then_x, then_y = ins
        for a, near, far in ((0, came_x, then_y), (1, came_y, then_x)):
            at = slice(a * rows, (a + 1) * rows)
            gate, up = [
                keep[k, at] + near[k, rows:].astype(F32) + far[k].astype(F32) for k in range(2)
            ]
            outs[0][0, at] = (jax.nn.silu(gate) * up).astype(BF16)

    def stored_body(ins, outs):
        core = lax.axis_index("dp")
        for k in range(2):
            for c in range(cores):
                start = pl.multiple_of((core ^ c) * units, units)
                outs[c][k] = ins[k][:, pl.ds(start, units)]

    grads = gather_first(backward_grad, n_tensor)
    acts = gather_first(forward_acts, n_tensor)
    wide, tall = load_weights(gate_weight, up_weight, down_weight, cores)
    other_grads = exchange(backward_grad, "dp", cores, 1)
    other_acts = exchange(forward_acts, "dp", cores, 1)
    grads = gather_tokens(grads, other_grads, cores, after=[tall, other_grads])
    parts = project(grads, tall, True, straight, n_pipe, n_tensor)
    parts = [parts[0]] + [swap(parts[s], s) for s in (3, 1, 2)]

    mine, other = small_kernel(
        stored_body,
        [((2, rows, units), BF16)] * 2,
        [stored_gate, stored_up],
        "stored",
        after=[parts[0]],
    )
    other = exchange(other, "dp", cores, 1)
    (slopes,) = small_kernel(
        slopes_body, [((2, cores * rows, units), BF16)], [*parts, mine, other], "slopes", after=acts[:0:-1]
    )
    slopes_x, slopes_y = swap(slopes, x), swap(slopes, y)

    acts = gather_tokens(acts, other_acts, cores, after=[slopes])
    keep, for_x, for_y = project(
        acts, wide, False, balanced_layout, n_pipe, n_tensor, after=[slopes]
    )
    came_x, came_y = swap(for_x, x), swap(for_y, y)
    half = ((2, rows, units), BF16)

    def halves_body(ins, outs):
        outs[0][...] = ins[0][:, :rows]
        outs[1][...] = ins[1][:, rows:]

    far_y, far_x = small_kernel(
        halves_body, [half, half], [slopes_x, slopes_y], "forward_halves", after=[keep]
    )
    slopes_all = [slopes, slopes_x, slopes_y, swap(far_y, y), swap(far_x, x)]
    back = contract(
        slopes_all, balanced_pieces, wide, True, cores, n_pipe, n_tensor
    )
    on_x, on_y = small_kernel(
        pass_on_body, [half, half], [keep, came_x, came_y], "pass_on", after=[back[0]]
    )
    came, input_grad = finish(back, cores, n_tensor)

    sums = [keep, came_x, came_y, swap(on_x, x), swap(on_y, y)]
    (hidden,) = small_kernel(
        hidden_body, [((1, cores * rows, units), BF16)], sums, "hidden"
    )
    hidden_all = [hidden] + [swap(hidden, s) for s in range(1, n_pipe)]
    out = contract(hidden_all, straight_pieces, tall, False, cores, n_pipe, n_tensor)

    def copy_body(ins, outs):
        outs[0][...] = ins[0][...]

    (held,) = small_kernel(copy_body, [(out[1].shape, BF16)], out[1:], "hold", after=came)
    _, layer_output = finish([out[0], held], cores, n_tensor)
    return layer_output, input_grad


def solution(mesh):
    in_specs = (
        P(("dp", "tensor"), "pipe"),
        P(("dp", "tensor"), "pipe"),
        P(("dp", "pipe"), "tensor"),
        P(("dp", "pipe"), "tensor"),
        P("pipe", "tensor"),
        P("pipe", "tensor"),
        P("tensor", "pipe"),
    )
    out_specs = (P(("dp", "tensor"), "pipe"), P(("dp", "tensor"), "pipe"))

    def whole(*args):
        n_pipe, n_tensor = mesh.shape["pipe"], mesh.shape["tensor"]
        hidden_width = args[4].shape[1] // n_tensor
        if mesh.shape["dp"] == 2 and n_pipe == 4 and hidden_width % 256 == 0:
            body = functools.partial(balanced, n_tensor)
        else:
            body = functools.partial(direct, n_pipe, n_tensor)
        return jax.shard_map(
            body, mesh=mesh, in_specs=in_specs, out_specs=out_specs, check_vma=False
        )(*args)

    return whole
```

```python
import functools

import jax
import jax.numpy as jnp
from jax import lax
from jax.experimental import pallas as pl
from jax.experimental.pallas import tpu as pltpu
from jax.sharding import PartitionSpec as P

F32 = jnp.float32
BF16 = jnp.bfloat16
VMEM_BYTES = 16 * 1024 * 1024
LOAD_BYTES = 24 * 1024 * 1024
CONTRACT_LAST = (((1,), (1,)), ((), ()))
IN_VMEM = pl.BlockSpec(memory_space=pltpu.VMEM)
IN_PLACE = pl.BlockSpec(memory_space=pl.ANY)


def exchange(value, axis, size, step):
    return lax.ppermute(value, axis, [(i, i ^ step) for i in range(size)])


def pick_tile(width):
    return 256 if width % 256 == 0 else 128


def cost(flops, moved):
    return pl.CostEstimate(flops=flops, bytes_accessed=moved, transcendentals=0)


def params():
    return pltpu.CompilerParams(vmem_limit_bytes=VMEM_BYTES)


def small_kernel(body, outs, inputs, name, after=()):
    n_in, n_after = len(inputs), len(after)

    def kernel(*refs):
        body(refs[:n_in], refs[n_in + n_after :])

    moved = sum(a.size * a.dtype.itemsize for a in inputs)
    return pl.pallas_call(
        kernel,
        in_specs=[IN_VMEM] * n_in + [IN_PLACE] * n_after,
        out_specs=[IN_VMEM] * len(outs),
        out_shape=[jax.ShapeDtypeStruct(shape, dtype) for shape, dtype in outs],
        cost_estimate=cost(moved, moved),
        compiler_params=params(),
        name=name,
    )(*inputs, *after)


def load_weights(gate_weight, up_weight, down_weight, cores):
    depth = gate_weight.shape[0]
    units = gate_weight.shape[1] // cores
    cuts = 4
    rows, unit_rows = depth // cuts, units // cuts

    def kernel(gate, up, down, wide, tall, sems):
        first = pl.multiple_of(lax.axis_index("dp") * units, units) if cores > 1 else 0
        copies = []
        for i in range(cuts):
            for k, ref in enumerate((gate, up)):
                at = pl.ds(i * rows, rows)
                copies.append((ref.at[at, pl.ds(first, units)], wide.at[k, at]))
        for i in range(cuts):
            at = pl.multiple_of(first + i * unit_rows, unit_rows)
            copies.append((down.at[pl.ds(at, unit_rows)], tall.at[0, pl.ds(i * unit_rows, unit_rows)]))
        copies = [
            pltpu.make_async_copy(source, target, sems.at[i])
            for i, (source, target) in enumerate(copies)
        ]
        for copy in copies:
            copy.start()
        for copy in copies:
            copy.wait()

    return pl.pallas_call(
        kernel,
        in_specs=[IN_PLACE] * 3,
        out_specs=[IN_VMEM] * 2,
        out_shape=[
            jax.ShapeDtypeStruct((2, depth, units), BF16),
            jax.ShapeDtypeStruct((1, units, depth), BF16),
        ],
        scratch_shapes=[pltpu.SemaphoreType.DMA((3 * cuts,))],
        compiler_params=pltpu.CompilerParams(vmem_limit_bytes=LOAD_BYTES),
        cost_estimate=cost(0, 6 * depth * units),
        name="load_weights",
    )(gate_weight, up_weight, down_weight)


def project(inputs, weights, transposed, layout, n_pipe, n_tensor, after=()):
    cores = len(inputs)
    flat = [x for pair in inputs for x in pair]
    n_in, n_after, n_out, kinds = len(flat), len(after), len(layout), weights.shape[0]
    block, depth = inputs[0][0].shape
    tokens = block * n_tensor
    units = weights.shape[1] if transposed else weights.shape[2]
    tile = pick_tile(units)
    count = units // tile
    rows = tokens // n_pipe

    def kernel(*refs):
        x_refs = refs[:n_in]
        held = refs[n_in]
        out_refs = refs[n_in + 1 + n_after : n_in + 1 + n_after + n_out]
        natural, ordered = refs[n_in + 1 + n_after + n_out :]
        t = lax.axis_index("tensor")
        p = lax.axis_index("pipe")

        def work(j, carry):
            at = pl.multiple_of(j * tile, tile)
            for k in range(kinds):
                if transposed:
                    total = lax.dot_general(
                        ordered[...], held[k, pl.ds(at, tile), :], CONTRACT_LAST, preferred_element_type=F32
                    )
                else:
                    total = jnp.dot(
                        ordered[...], held[k, :, pl.ds(at, tile)], preferred_element_type=F32
                    )
                for ref, (_, pieces) in zip(out_refs, layout):
                    for i, (s, a) in enumerate(pieces):
                        row = (s * cores + a) * rows
                        part = total[row : row + rows].astype(ref.dtype)
                        ref[k, i * rows : (i + 1) * rows, pl.ds(at, tile)] = part
            return carry

        def own_block(a, s):
            if s == 0:
                return x_refs[2 * a][...]
            return x_refs[2 * a + 1][(s - 1) * block : s * block, :]

        for a in range(cores):
            if block == rows:
                for s in range(n_tensor):
                    start = pl.multiple_of(((p ^ t ^ s) * cores + a) * rows, rows)
                    ordered[pl.ds(start, rows), :] = own_block(a, s)
                continue
            for s in range(n_tensor):
                start = pl.multiple_of((t ^ s) * block, block)
                natural[pl.ds(start, block), :] = own_block(a, s)
            for s in range(n_pipe):
                start = pl.multiple_of((p ^ s) * rows, rows)
                at = (s * cores + a) * rows
                ordered[at : at + rows, :] = natural[pl.ds(start, rows), :]
        lax.fori_loop(0, count, work, 0, unroll=True)

    return pl.pallas_call(
        kernel,
        in_specs=[IN_VMEM] * (n_in + 1) + [IN_PLACE] * n_after,
        out_specs=[IN_VMEM] * n_out,
        out_shape=[
            jax.ShapeDtypeStruct((kinds, len(pieces) * rows, units), dtype)
            for dtype, pieces in layout
        ],
        scratch_shapes=[
            pltpu.VMEM((tokens, depth), BF16),
            pltpu.VMEM((cores * tokens, depth), BF16),
        ],
        compiler_params=params(),
        cost_estimate=cost(0, 0) if transposed else cost(2 * cores * tokens * depth * units * kinds, 2 * depth * units * kinds),
        name="pull_back" if transposed else "project",
    )(*flat, weights, *after)


def contract(blocks, pieces, weights, transposed, cores, n_pipe, n_tensor, cuts=1, after=()):
    kinds, _, units = blocks[0].shape
    n_in, n_after = len(blocks), len(after)
    from_rows = blocks[0].shape[1] // cores
    tokens = from_rows * n_pipe
    to_rows = tokens // n_tensor
    width = weights.shape[1] if transposed else weights.shape[2]
    tile = pick_tile(width)
    count = width // tile
    cut_width = width // cuts
    n_out = 1 + (cores - 1) * cuts

    def kernel(*refs):
        x_refs = refs[:n_in]
        held = refs[n_in]
        out_refs = refs[n_in + 1 + n_after : n_in + 1 + n_after + n_out]
        natural, ordered = refs[n_in + 1 + n_after + n_out :]
        t = lax.axis_index("tensor")
        p = lax.axis_index("pipe")

        def work(j):
            at = j * tile
            total = None
            for k in range(kinds):
                if transposed:
                    part = lax.dot_general(
                        ordered[k], held[k, at : at + tile, :], CONTRACT_LAST, preferred_element_type=F32
                    )
                else:
                    part = jnp.dot(
                        ordered[k], held[k, :, at : at + tile], preferred_element_type=F32
                    )
                total = part if total is None else total + part
            out_refs[0][:, at : at + tile] = total[:tokens]
            if cores > 1:
                ref = out_refs[1 + at // cut_width]
                place = at % cut_width
                ref[:, place : place + tile] = total[tokens:].astype(ref.dtype)

        def came(k, a, s):
            place, row = pieces[s][a]
            return x_refs[place][k, row : row + from_rows, :]

        for k in range(kinds):
            for a in range(cores):
                if from_rows == to_rows:
                    for s in range(n_pipe):
                        start = pl.multiple_of(a * tokens + (t ^ p ^ s) * to_rows, to_rows)
                        ordered[k, pl.ds(start, to_rows), :] = came(k, a, s)
                    continue
                for s in range(n_pipe):
                    start = pl.multiple_of((p ^ s) * from_rows, from_rows)
                    natural[pl.ds(start, from_rows), :] = came(k, a, s)
                for s in range(n_tensor):
                    start = pl.multiple_of((t ^ s) * to_rows, to_rows)
                    at = a * tokens + s * to_rows
                    ordered[k, at : at + to_rows, :] = natural[pl.ds(start, to_rows), :]
        for j in range(count):
            work(j)

    return pl.pallas_call(
        kernel,
        in_specs=[IN_VMEM] * (n_in + 1) + [IN_PLACE] * n_after,
        out_specs=[IN_VMEM] * n_out,
        out_shape=[jax.ShapeDtypeStruct((tokens, width), F32)]
        + [jax.ShapeDtypeStruct((tokens, cut_width), BF16)] * (n_out - 1),
        scratch_shapes=[
            pltpu.VMEM((tokens, units), BF16),
            pltpu.VMEM((kinds, cores * tokens, units), BF16),
        ],
        compiler_params=params(),
        cost_estimate=cost(2 * cores * tokens * units * width * kinds, 2 * units * width * kinds),
        name="input_grad" if transposed else "layer_output",
    )(*blocks, weights, *after)


def gather_first(value, n_tensor):
    came = {s: exchange(value, "tensor", n_tensor, s) for s in range(n_tensor - 1, 0, -1)}
    return [value] + [came[s] for s in range(1, n_tensor)]


def gather_tokens(blocks, other, cores, after=()):
    own, came = blocks[0], blocks[1:]
    rows, width = own.shape

    def body(ins, outs):
        for s, ref in enumerate(ins):
            outs[0][s * rows : (s + 1) * rows, :] = ref[...]

    shape = (rows * len(came), width)
    (rest,) = small_kernel(body, [(shape, BF16)], came, "assemble", after)
    if cores == 1:
        return [(own, rest)]
    return [(own, rest), (other, exchange(rest, "dp", cores, 1))]


def finish(partials, cores, n_tensor, after=()):
    if cores > 1:
        others = [exchange(x, "dp", cores, 1) for x in partials[1:]]
        rows, width = partials[0].shape[0] // n_tensor, partials[0].shape[1]
        cut = others[0].shape[1]

        def body(ins, outs):
            for s in range(n_tensor):
                at = slice(s * rows, (s + 1) * rows)
                for i, ref in enumerate(ins[1:]):
                    columns = slice(i * cut, (i + 1) * cut)
                    total = ins[0][at, columns] + ref[at].astype(F32)
                    outs[s][:, columns] = total.astype(outs[s].dtype)

        parts = small_kernel(
            body,
            [((rows, width), BF16 if s else F32) for s in range(n_tensor)],
            [partials[0], *others],
            "add_core",
            after,
        )
    else:
        rows = partials[0].shape[0] // n_tensor
        parts = [
            partials[0][s * rows : (s + 1) * rows].astype(BF16 if s else F32)
            for s in range(n_tensor)
        ]

    came = [exchange(parts[s], "tensor", n_tensor, s) for s in range(n_tensor - 1, 0, -1)]
    total = parts[0]
    for value in came:
        total = total + value.astype(F32)
    return came, total.astype(BF16)


def slope_values(grad, gate, up):
    gate, up = gate.astype(F32), up.astype(F32)
    sigma = jax.nn.sigmoid(gate)
    gate_slope = (grad * up * sigma * (1.0 + gate * (1.0 - sigma))).astype(BF16)
    up_slope = (grad * gate * sigma).astype(BF16)
    return gate_slope, up_slope


def direct(
    n_pipe, n_tensor, forward_acts, backward_grad, stored_gate, stored_up, gate_weight, up_weight, down_weight
):
    layout = [(BF16 if s else F32, [(s, 0)]) for s in range(n_pipe)]
    pieces = [[(s, 0)] for s in range(n_pipe)]

    def total_of(parts):
        total = parts[0]
        for s in range(1, n_pipe):
            total = total + exchange(parts[s], "pipe", n_pipe, s).astype(F32)
        return total

    def gather(value):
        return [value] + [exchange(value, "pipe", n_pipe, s) for s in range(1, n_pipe)]

    wide, tall = load_weights(gate_weight, up_weight, down_weight, 1)
    grads = gather_tokens(gather_first(backward_grad, n_tensor), None, 1)
    acts = gather_tokens(gather_first(forward_acts, n_tensor), None, 1)
    grad = total_of(project(grads, tall, True, layout, n_pipe, n_tensor))[0]
    slopes = gather(jnp.stack(slope_values(grad, stored_gate, stored_up)))
    summed = total_of(project(acts, wide, False, layout, n_pipe, n_tensor))
    hidden = gather((jax.nn.silu(summed[:1]) * summed[1:]).astype(BF16))
    back = contract(slopes, pieces, wide, True, 1, n_pipe, n_tensor)
    out = contract(hidden, pieces, tall, False, 1, n_pipe, n_tensor)
    return finish(out, 1, n_tensor)[1], finish(back, 1, n_tensor)[1]


def balanced(
    n_tensor, forward_acts, backward_grad, stored_gate, stored_up, gate_weight, up_weight, down_weight
):
    cores, n_pipe, x, y = 2, 4, 1, 2
    units = gate_weight.shape[1] // cores
    rows = stored_gate.shape[0]
    straight = [(BF16 if s else F32, [(s, 0), (s, 1)]) for s in range(n_pipe)]
    balanced_layout = [
        (F32, [(0, 0), (0, 1), (1, 1), (2, 0)]),
        (BF16, [(3, 0), (1, 0)]),
        (BF16, [(3, 1), (2, 1)]),
    ]
    straight_pieces = [[(s, 0), (s, rows)] for s in range(n_pipe)]


    def swap(value, step):
        return exchange(value, "pipe", n_pipe, step)

    def slopes_body(ins, outs):
        keep, came = ins[0], ins[1:n_pipe]
        for a in range(cores):
            at = slice(a * rows, (a + 1) * rows)
            grad = keep[0, at]
            for ref in came:
                grad = grad + ref[0, at].astype(F32)
            stored = ins[n_pipe + a]
            gate_slope, up_slope = slope_values(grad, stored[0], stored[1])
            outs[0][0, at] = gate_slope
            outs[0][1, at] = up_slope

    def pass_on_body(ins, outs):
        keep, came_x, came_y = ins
        for k in range(2):
            on_x = keep[k, 2 * rows : 3 * rows] + came_y[k, :rows].astype(F32)
            on_y = keep[k, 3 * rows : 4 * rows] + came_x[k, :rows].astype(F32)
            outs[0][k] = on_x.astype(BF16)
            outs[1][k] = on_y.astype(BF16)

    def hidden_body(ins, outs):
        keep, came_x, came_y, then_x, then_y = ins
        for a, near, far in ((0, came_x, then_y), (1, came_y, then_x)):
            at = slice(a * rows, (a + 1) * rows)
            gate, up = [
                keep[k, at] + near[k, rows:].astype(F32) + far[k].astype(F32) for k in range(2)
            ]
            outs[0][0, at] = (jax.nn.silu(gate) * up).astype(BF16)

    def stored_body(ins, outs):
        core = lax.axis_index("dp")
        for k in range(2):
            for c in range(cores):
                start = pl.multiple_of((core ^ c) * units, units)
                outs[c][k] = ins[k][:, pl.ds(start, units)]

    acts = gather_first(forward_acts, n_tensor)
    grads = gather_first(backward_grad, n_tensor)
    wide, tall = load_weights(gate_weight, up_weight, down_weight, cores)
    other_acts = exchange(forward_acts, "dp", cores, 1)
    other_grads = exchange(backward_grad, "dp", cores, 1)
    acts = gather_tokens(acts, other_acts, cores, after=[tall, other_acts, grads[1]])
    keep, for_x, for_y = project(
        acts, wide, False, balanced_layout, n_pipe, n_tensor
    )
    came_x, came_y = swap(for_x, x), swap(for_y, y)
    mine, other = small_kernel(
        stored_body, [((2, rows, units), BF16)] * 2, [stored_gate, stored_up], "stored", after=[keep]
    )
    other = exchange(other, "dp", cores, 1)
    grads = gather_tokens(grads, other_grads, cores, after=[keep])
    parts = project(grads, tall, True, straight, n_pipe, n_tensor, after=[other])
    parts = [parts[0]] + [swap(parts[s], s) for s in (3, 1, 2)]

    half = ((2, rows, units), BF16)
    on_x, on_y = small_kernel(
        pass_on_body, [half, half], [keep, came_x, came_y], "pass_on", after=[parts[0]]
    )
    sums = [keep, came_x, came_y, swap(on_x, x), swap(on_y, y)]
    (hidden,) = small_kernel(hidden_body, [((1, cores * rows, units), BF16)], sums, "hidden")
    hidden_all = [hidden] + [swap(hidden, s) for s in range(1, n_pipe)]

    (slopes,) = small_kernel(
        slopes_body,
        [((2, cores * rows, units), BF16)],
        [*parts, mine, other],
        "slopes",
        after=[hidden],
    )
    slopes_all = [slopes] + [swap(slopes, s) for s in range(1, n_pipe)]

    out = contract(
        hidden_all,
        straight_pieces,
        tall,
        False,
        cores,
        n_pipe,
        n_tensor,
        cuts=2,
        after=[slopes],
    )
    came, layer_output = finish(out, cores, n_tensor)
    back = contract(
        slopes_all,
        straight_pieces,
        wide,
        True,
        cores,
        n_pipe,
        n_tensor,
    )

    def copy_body(ins, outs):
        outs[0][...] = ins[0][...]

    (held,) = small_kernel(copy_body, [(back[1].shape, BF16)], back[1:], "hold", after=came)
    _, input_grad = finish([back[0], held], cores, n_tensor)
    return layer_output, input_grad


def solution(mesh):
    in_specs = (
        P(("dp", "tensor"), "pipe"),
        P(("dp", "tensor"), "pipe"),
        P(("dp", "pipe"), "tensor"),
        P(("dp", "pipe"), "tensor"),
        P("pipe", "tensor"),
        P("pipe", "tensor"),
        P("tensor", "pipe"),
    )
    out_specs = (P(("dp", "tensor"), "pipe"), P(("dp", "tensor"), "pipe"))

    def whole(*args):
        n_pipe, n_tensor = mesh.shape["pipe"], mesh.shape["tensor"]
        hidden_width = args[4].shape[1] // n_tensor
        if mesh.shape["dp"] == 2 and n_pipe == 4 and hidden_width % 256 == 0:
            body = functools.partial(balanced, n_tensor)
        else:
            body = functools.partial(direct, n_pipe, n_tensor)
        return jax.shard_map(
            body, mesh=mesh, in_specs=in_specs, out_specs=out_specs, check_vma=False
        )(*args)

    return whole
```

```python
import functools

import jax
import jax.numpy as jnp
from jax import lax
from jax.experimental import pallas as pl
from jax.experimental.pallas import tpu as pltpu
from jax.sharding import PartitionSpec as P

F32 = jnp.float32
BF16 = jnp.bfloat16
VMEM_BYTES = 16 * 1024 * 1024
LOAD_BYTES = 24 * 1024 * 1024
CONTRACT_LAST = (((1,), (1,)), ((), ()))
IN_VMEM = pl.BlockSpec(memory_space=pltpu.VMEM)
IN_PLACE = pl.BlockSpec(memory_space=pl.ANY)


def exchange(value, axis, size, step):
    return lax.ppermute(value, axis, [(i, i ^ step) for i in range(size)])


def pick_tile(width):
    return 256 if width % 256 == 0 else 128


def cost(flops, moved):
    return pl.CostEstimate(flops=flops, bytes_accessed=moved, transcendentals=0)


def params():
    return pltpu.CompilerParams(vmem_limit_bytes=VMEM_BYTES)


def small_kernel(body, outs, inputs, name, after=()):
    n_in, n_after = len(inputs), len(after)

    def kernel(*refs):
        body(refs[:n_in], refs[n_in + n_after :])

    moved = sum(a.size * a.dtype.itemsize for a in inputs)
    return pl.pallas_call(
        kernel,
        in_specs=[IN_VMEM] * n_in + [IN_PLACE] * n_after,
        out_specs=[IN_VMEM] * len(outs),
        out_shape=[jax.ShapeDtypeStruct(shape, dtype) for shape, dtype in outs],
        cost_estimate=cost(moved, moved),
        compiler_params=params(),
        name=name,
    )(*inputs, *after)


def load_weights(gate_weight, up_weight, down_weight, cores):
    depth = gate_weight.shape[0]
    units = gate_weight.shape[1] // cores
    cuts = 4
    rows, unit_rows = depth // cuts, units // cuts

    def kernel(gate, up, down, wide, tall, sems):
        first = pl.multiple_of(lax.axis_index("dp") * units, units) if cores > 1 else 0
        copies = []
        for i in range(cuts):
            for k, ref in enumerate((gate, up)):
                at = pl.ds(i * rows, rows)
                copies.append((ref.at[at, pl.ds(first, units)], wide.at[k, at]))
        for i in range(cuts):
            at = pl.multiple_of(first + i * unit_rows, unit_rows)
            copies.append((down.at[pl.ds(at, unit_rows)], tall.at[0, pl.ds(i * unit_rows, unit_rows)]))
        copies = [
            pltpu.make_async_copy(source, target, sems.at[i])
            for i, (source, target) in enumerate(copies)
        ]
        for copy in copies:
            copy.start()
        for copy in copies:
            copy.wait()

    return pl.pallas_call(
        kernel,
        in_specs=[IN_PLACE] * 3,
        out_specs=[IN_VMEM] * 2,
        out_shape=[
            jax.ShapeDtypeStruct((2, depth, units), BF16),
            jax.ShapeDtypeStruct((1, units, depth), BF16),
        ],
        scratch_shapes=[pltpu.SemaphoreType.DMA((3 * cuts,))],
        compiler_params=pltpu.CompilerParams(vmem_limit_bytes=LOAD_BYTES),
        cost_estimate=cost(0, 6 * depth * units),
        name="load_weights",
    )(gate_weight, up_weight, down_weight)


def project(inputs, weights, transposed, layout, n_pipe, n_tensor, after=()):
    cores = len(inputs)
    flat = [x for pair in inputs for x in pair]
    n_in, n_after, n_out, kinds = len(flat), len(after), len(layout), weights.shape[0]
    block, depth = inputs[0][0].shape
    tokens = block * n_tensor
    units = weights.shape[1] if transposed else weights.shape[2]
    tile = pick_tile(units)
    count = units // tile
    rows = tokens // n_pipe

    def kernel(*refs):
        x_refs = refs[:n_in]
        held = refs[n_in]
        out_refs = refs[n_in + 1 + n_after : n_in + 1 + n_after + n_out]
        natural, ordered = refs[n_in + 1 + n_after + n_out :]
        t = lax.axis_index("tensor")
        p = lax.axis_index("pipe")

        def work(j, carry):
            at = pl.multiple_of(j * tile, tile)
            for k in range(kinds):
                if transposed:
                    total = lax.dot_general(
                        ordered[...], held[k, pl.ds(at, tile), :], CONTRACT_LAST, preferred_element_type=F32
                    )
                else:
                    total = jnp.dot(
                        ordered[...], held[k, :, pl.ds(at, tile)], preferred_element_type=F32
                    )
                for ref, (_, pieces) in zip(out_refs, layout):
                    for i, (s, a) in enumerate(pieces):
                        row = (s * cores + a) * rows
                        part = total[row : row + rows].astype(ref.dtype)
                        ref[k, i * rows : (i + 1) * rows, pl.ds(at, tile)] = part
            return carry

        def own_block(a, s):
            if s == 0:
                return x_refs[2 * a][...]
            return x_refs[2 * a + 1][(s - 1) * block : s * block, :]

        for a in range(cores):
            if block == rows:
                for s in range(n_tensor):
                    start = pl.multiple_of(((p ^ t ^ s) * cores + a) * rows, rows)
                    ordered[pl.ds(start, rows), :] = own_block(a, s)
                continue
            for s in range(n_tensor):
                start = pl.multiple_of((t ^ s) * block, block)
                natural[pl.ds(start, block), :] = own_block(a, s)
            for s in range(n_pipe):
                start = pl.multiple_of((p ^ s) * rows, rows)
                at = (s * cores + a) * rows
                ordered[at : at + rows, :] = natural[pl.ds(start, rows), :]
        lax.fori_loop(0, count, work, 0, unroll=True)

    return pl.pallas_call(
        kernel,
        in_specs=[IN_VMEM] * (n_in + 1) + [IN_PLACE] * n_after,
        out_specs=[IN_VMEM] * n_out,
        out_shape=[
            jax.ShapeDtypeStruct((kinds, len(pieces) * rows, units), dtype)
            for dtype, pieces in layout
        ],
        scratch_shapes=[
            pltpu.VMEM((tokens, depth), BF16),
            pltpu.VMEM((cores * tokens, depth), BF16),
        ],
        compiler_params=params(),
        cost_estimate=cost(0, 0) if transposed else cost(2 * cores * tokens * depth * units * kinds, 2 * depth * units * kinds),
        name="pull_back" if transposed else "project",
    )(*flat, weights, *after)


def contract(blocks, pieces, weights, transposed, cores, n_pipe, n_tensor, after=()):
    kinds, _, units = blocks[0].shape
    n_in, n_after = len(blocks), len(after)
    from_rows = blocks[0].shape[1] // cores
    tokens = from_rows * n_pipe
    to_rows = tokens // n_tensor
    width = weights.shape[1] if transposed else weights.shape[2]
    tile = pick_tile(width)
    count = width // tile

    def kernel(*refs):
        x_refs = refs[:n_in]
        held = refs[n_in]
        out_refs = refs[n_in + 1 + n_after : n_in + 1 + n_after + cores]
        natural, ordered = refs[n_in + 1 + n_after + cores :]
        t = lax.axis_index("tensor")
        p = lax.axis_index("pipe")

        def work(j, carry):
            at = pl.multiple_of(j * tile, tile)
            total = None
            for k in range(kinds):
                if transposed:
                    part = lax.dot_general(
                        ordered[k], held[k, pl.ds(at, tile), :], CONTRACT_LAST, preferred_element_type=F32
                    )
                else:
                    part = jnp.dot(
                        ordered[k], held[k, :, pl.ds(at, tile)], preferred_element_type=F32
                    )
                total = part if total is None else total + part
            for a in range(cores):
                part = total[a * tokens : (a + 1) * tokens]
                out_refs[a][:, pl.ds(at, tile)] = part.astype(out_refs[a].dtype)
            return carry

        def came(k, a, s):
            place, row = pieces[s][a]
            return x_refs[place][k, row : row + from_rows, :]

        for k in range(kinds):
            for a in range(cores):
                if from_rows == to_rows:
                    for s in range(n_pipe):
                        start = pl.multiple_of(a * tokens + (t ^ p ^ s) * to_rows, to_rows)
                        ordered[k, pl.ds(start, to_rows), :] = came(k, a, s)
                    continue
                for s in range(n_pipe):
                    start = pl.multiple_of((p ^ s) * from_rows, from_rows)
                    natural[pl.ds(start, from_rows), :] = came(k, a, s)
                for s in range(n_tensor):
                    start = pl.multiple_of((t ^ s) * to_rows, to_rows)
                    at = a * tokens + s * to_rows
                    ordered[k, at : at + to_rows, :] = natural[pl.ds(start, to_rows), :]
        lax.fori_loop(0, count, work, 0, unroll=True)

    return pl.pallas_call(
        kernel,
        in_specs=[IN_VMEM] * (n_in + 1) + [IN_PLACE] * n_after,
        out_specs=[IN_VMEM] * cores,
        out_shape=[
            jax.ShapeDtypeStruct((tokens, width), BF16 if a else F32) for a in range(cores)
        ],
        scratch_shapes=[
            pltpu.VMEM((tokens, units), BF16),
            pltpu.VMEM((kinds, cores * tokens, units), BF16),
        ],
        compiler_params=params(),
        cost_estimate=cost(2 * cores * tokens * units * width * kinds, 2 * units * width * kinds),
        name="input_grad" if transposed else "layer_output",
    )(*blocks, weights, *after)


def gather_first(value, n_tensor):
    came = {s: exchange(value, "tensor", n_tensor, s) for s in range(n_tensor - 1, 0, -1)}
    return [value] + [came[s] for s in range(1, n_tensor)]


def gather_tokens(blocks, other, cores, after=()):
    own, came = blocks[0], blocks[1:]
    rows, width = own.shape

    def body(ins, outs):
        for s, ref in enumerate(ins):
            outs[0][s * rows : (s + 1) * rows, :] = ref[...]

    shape = (rows * len(came), width)
    (rest,) = small_kernel(body, [(shape, BF16)], came, "assemble", after)
    if cores == 1:
        return [(own, rest)]
    return [(own, rest), (other, exchange(rest, "dp", cores, 1))]


def finish(partials, cores, n_tensor, after=()):
    if cores > 1:
        other = exchange(partials[1], "dp", cores, 1)
        rows, width = other.shape[0] // n_tensor, other.shape[1]

        def body(ins, outs):
            for s in range(n_tensor):
                at = slice(s * rows, (s + 1) * rows)
                outs[s][...] = (ins[0][at] + ins[1][at].astype(F32)).astype(outs[s].dtype)

        parts = small_kernel(
            body,
            [((rows, width), BF16 if s else F32) for s in range(n_tensor)],
            [partials[0], other],
            "add_core",
            after,
        )
    else:
        rows = partials[0].shape[0] // n_tensor
        parts = [
            partials[0][s * rows : (s + 1) * rows].astype(BF16 if s else F32)
            for s in range(n_tensor)
        ]

    came = [exchange(parts[s], "tensor", n_tensor, s) for s in range(n_tensor - 1, 0, -1)]
    total = parts[0]
    for value in came:
        total = total + value.astype(F32)
    return came, total.astype(BF16)


def slope_values(grad, gate, up):
    gate, up = gate.astype(F32), up.astype(F32)
    sigma = jax.nn.sigmoid(gate)
    gate_slope = (grad * up * sigma * (1.0 + gate * (1.0 - sigma))).astype(BF16)
    up_slope = (grad * gate * sigma).astype(BF16)
    return gate_slope, up_slope


def direct(
    n_pipe, n_tensor, forward_acts, backward_grad, stored_gate, stored_up, gate_weight, up_weight, down_weight
):
    layout = [(BF16 if s else F32, [(s, 0)]) for s in range(n_pipe)]
    pieces = [[(s, 0)] for s in range(n_pipe)]

    def total_of(parts):
        total = parts[0]
        for s in range(1, n_pipe):
            total = total + exchange(parts[s], "pipe", n_pipe, s).astype(F32)
        return total

    def gather(value):
        return [value] + [exchange(value, "pipe", n_pipe, s) for s in range(1, n_pipe)]

    wide, tall = load_weights(gate_weight, up_weight, down_weight, 1)
    grads = gather_tokens(gather_first(backward_grad, n_tensor), None, 1)
    acts = gather_tokens(gather_first(forward_acts, n_tensor), None, 1)
    grad = total_of(project(grads, tall, True, layout, n_pipe, n_tensor))[0]
    slopes = gather(jnp.stack(slope_values(grad, stored_gate, stored_up)))
    summed = total_of(project(acts, wide, False, layout, n_pipe, n_tensor))
    hidden = gather((jax.nn.silu(summed[:1]) * summed[1:]).astype(BF16))
    back = contract(slopes, pieces, wide, True, 1, n_pipe, n_tensor)
    out = contract(hidden, pieces, tall, False, 1, n_pipe, n_tensor)
    return finish(out, 1, n_tensor)[1], finish(back, 1, n_tensor)[1]


def balanced(
    n_tensor, forward_acts, backward_grad, stored_gate, stored_up, gate_weight, up_weight, down_weight
):
    cores, n_pipe, x, y = 2, 4, 1, 2
    units = gate_weight.shape[1] // cores
    rows = stored_gate.shape[0]
    straight = [(BF16 if s else F32, [(s, 0), (s, 1)]) for s in range(n_pipe)]
    balanced_layout = [
        (F32, [(0, 0), (0, 1), (1, 1), (2, 0)]),
        (BF16, [(3, 0), (1, 0)]),
        (BF16, [(3, 1), (2, 1)]),
    ]
    straight_pieces = [[(s, 0), (s, rows)] for s in range(n_pipe)]
    balanced_pieces = straight_pieces[:3] + [[(3, 0), (4, 0)]]


    def swap(value, step):
        return exchange(value, "pipe", n_pipe, step)

    def slopes_body(ins, outs):
        keep, came = ins[0], ins[1:n_pipe]
        for a in range(cores):
            at = slice(a * rows, (a + 1) * rows)
            grad = keep[0, at]
            for ref in came:
                grad = grad + ref[0, at].astype(F32)
            stored = ins[n_pipe + a]
            gate_slope, up_slope = slope_values(grad, stored[0], stored[1])
            outs[0][0, at] = gate_slope
            outs[0][1, at] = up_slope

    def pass_on_body(ins, outs):
        keep, came_x, came_y = ins
        for k in range(2):
            on_x = keep[k, 2 * rows : 3 * rows] + came_y[k, :rows].astype(F32)
            on_y = keep[k, 3 * rows : 4 * rows] + came_x[k, :rows].astype(F32)
            outs[0][k] = on_x.astype(BF16)
            outs[1][k] = on_y.astype(BF16)

    def hidden_body(ins, outs):
        keep, came_x, came_y, then_x, then_y = ins
        for a, near, far in ((0, came_x, then_y), (1, came_y, then_x)):
            at = slice(a * rows, (a + 1) * rows)
            gate, up = [
                keep[k, at] + near[k, rows:].astype(F32) + far[k].astype(F32) for k in range(2)
            ]
            outs[0][0, at] = (jax.nn.silu(gate) * up).astype(BF16)

    def stored_body(ins, outs):
        core = lax.axis_index("dp")
        for k in range(2):
            for c in range(cores):
                start = pl.multiple_of((core ^ c) * units, units)
                outs[c][k] = ins[k][:, pl.ds(start, units)]

    acts = gather_first(forward_acts, n_tensor)
    grads = gather_first(backward_grad, n_tensor)
    wide, tall = load_weights(gate_weight, up_weight, down_weight, cores)
    other_acts = exchange(forward_acts, "dp", cores, 1)
    other_grads = exchange(backward_grad, "dp", cores, 1)
    acts = gather_tokens(acts, other_acts, cores, after=[tall, other_acts, grads[1]])
    keep, for_x, for_y = project(
        acts, wide, False, balanced_layout, n_pipe, n_tensor
    )
    came_x, came_y = swap(for_x, x), swap(for_y, y)
    mine, other = small_kernel(
        stored_body, [((2, rows, units), BF16)] * 2, [stored_gate, stored_up], "stored", after=[keep]
    )
    other = exchange(other, "dp", cores, 1)
    grads = gather_tokens(grads, other_grads, cores, after=[keep])
    parts = project(grads, tall, True, straight, n_pipe, n_tensor, after=[other])
    parts = [parts[0]] + [swap(parts[s], s) for s in (3, 1, 2)]

    half = ((2, rows, units), BF16)
    on_x, on_y = small_kernel(
        pass_on_body, [half, half], [keep, came_x, came_y], "pass_on", after=[parts[0]]
    )
    sums = [keep, came_x, came_y, swap(on_x, x), swap(on_y, y)]
    (hidden,) = small_kernel(hidden_body, [((1, cores * rows, units), BF16)], sums, "hidden")
    order = (2, 3, 1)
    hidden_all = [hidden] + [swap(hidden, s) for s in order]
    hidden_pieces = [straight_pieces[0]] + [straight_pieces[order.index(s) + 1] for s in (1, 2, 3)]

    (slopes,) = small_kernel(
        slopes_body,
        [((2, cores * rows, units), BF16)],
        [*parts, mine, other],
        "slopes",
        after=[hidden],
    )
    slopes_x, slopes_y = swap(slopes, x), swap(slopes, y)

    out = contract(
        hidden_all, hidden_pieces, tall, False, cores, n_pipe, n_tensor, after=[slopes]
    )
    slopes_all = [
        slopes,
        slopes_x,
        slopes_y,
        swap(slopes_x[:, :rows], y),
        swap(slopes_y[:, rows:], x),
    ]
    came, layer_output = finish(out, cores, n_tensor)
    back = contract(
        slopes_all,
        balanced_pieces,
        wide,
        True,
        cores,
        n_pipe,
        n_tensor,
    )

    def copy_body(ins, outs):
        outs[0][...] = ins[0][...]

    (held,) = small_kernel(copy_body, [(back[1].shape, BF16)], back[1:], "hold", after=came)
    _, input_grad = finish([back[0], held], cores, n_tensor)
    return layer_output, input_grad


def solution(mesh):
    in_specs = (
        P(("dp", "tensor"), "pipe"),
        P(("dp", "tensor"), "pipe"),
        P(("dp", "pipe"), "tensor"),
        P(("dp", "pipe"), "tensor"),
        P("pipe", "tensor"),
        P("pipe", "tensor"),
        P("tensor", "pipe"),
    )
    out_specs = (P(("dp", "tensor"), "pipe"), P(("dp", "tensor"), "pipe"))

    def whole(*args):
        n_pipe, n_tensor = mesh.shape["pipe"], mesh.shape["tensor"]
        hidden_width = args[4].shape[1] // n_tensor
        if mesh.shape["dp"] == 2 and n_pipe == 4 and hidden_width % 256 == 0:
            body = functools.partial(balanced, n_tensor)
        else:
            body = functools.partial(direct, n_pipe, n_tensor)
        return jax.shard_map(
            body, mesh=mesh, in_specs=in_specs, out_specs=out_specs, check_vma=False
        )(*args)

    return whole
```

```python
import functools

import jax
import jax.numpy as jnp
from jax import lax
from jax.experimental import pallas as pl
from jax.experimental.pallas import tpu as pltpu
from jax.sharding import PartitionSpec as P

F32 = jnp.float32
BF16 = jnp.bfloat16
VMEM_BYTES = 16 * 1024 * 1024
LOAD_BYTES = 24 * 1024 * 1024
CONTRACT_LAST = (((1,), (1,)), ((), ()))
IN_VMEM = pl.BlockSpec(memory_space=pltpu.VMEM)
IN_PLACE = pl.BlockSpec(memory_space=pl.ANY)


def exchange(value, axis, size, step):
    return lax.ppermute(value, axis, [(i, i ^ step) for i in range(size)])


def pick_tile(width):
    return 256 if width % 256 == 0 else 128


def cost(flops, moved):
    return pl.CostEstimate(flops=flops, bytes_accessed=moved, transcendentals=0)


def params():
    return pltpu.CompilerParams(vmem_limit_bytes=VMEM_BYTES)


def small_kernel(body, outs, inputs, name, after=()):
    n_in, n_after = len(inputs), len(after)

    def kernel(*refs):
        body(refs[:n_in], refs[n_in + n_after :])

    moved = sum(a.size * a.dtype.itemsize for a in inputs)
    return pl.pallas_call(
        kernel,
        in_specs=[IN_VMEM] * n_in + [IN_PLACE] * n_after,
        out_specs=[IN_VMEM] * len(outs),
        out_shape=[jax.ShapeDtypeStruct(shape, dtype) for shape, dtype in outs],
        cost_estimate=cost(moved, moved),
        compiler_params=params(),
        name=name,
    )(*inputs, *after)


def load_weights(gate_weight, up_weight, down_weight, cores):
    depth = gate_weight.shape[0]
    units = gate_weight.shape[1] // cores
    cuts = 4
    rows, unit_rows = depth // cuts, units // cuts

    def kernel(gate, up, down, wide, tall, sems):
        first = pl.multiple_of(lax.axis_index("dp") * units, units) if cores > 1 else 0
        copies = []
        for i in range(cuts):
            for k, ref in enumerate((gate, up)):
                at = pl.ds(i * rows, rows)
                copies.append((ref.at[at, pl.ds(first, units)], wide.at[k, at]))
        for i in range(cuts):
            at = pl.multiple_of(first + i * unit_rows, unit_rows)
            copies.append((down.at[pl.ds(at, unit_rows)], tall.at[0, pl.ds(i * unit_rows, unit_rows)]))
        copies = [
            pltpu.make_async_copy(source, target, sems.at[i])
            for i, (source, target) in enumerate(copies)
        ]
        for copy in copies:
            copy.start()
        for copy in copies:
            copy.wait()

    return pl.pallas_call(
        kernel,
        in_specs=[IN_PLACE] * 3,
        out_specs=[IN_VMEM] * 2,
        out_shape=[
            jax.ShapeDtypeStruct((2, depth, units), BF16),
            jax.ShapeDtypeStruct((1, units, depth), BF16),
        ],
        scratch_shapes=[pltpu.SemaphoreType.DMA((3 * cuts,))],
        compiler_params=pltpu.CompilerParams(vmem_limit_bytes=LOAD_BYTES),
        cost_estimate=cost(0, 6 * depth * units),
        name="load_weights",
    )(gate_weight, up_weight, down_weight)


def project(inputs, weights, transposed, layout, n_pipe, n_tensor, after=()):
    cores = len(inputs)
    flat = [x for pair in inputs for x in pair]
    n_in, n_after, n_out, kinds = len(flat), len(after), len(layout), weights.shape[0]
    block, depth = inputs[0][0].shape
    tokens = block * n_tensor
    units = weights.shape[1] if transposed else weights.shape[2]
    tile = pick_tile(units)
    count = units // tile
    rows = tokens // n_pipe

    def kernel(*refs):
        x_refs = refs[:n_in]
        held = refs[n_in]
        out_refs = refs[n_in + 1 + n_after : n_in + 1 + n_after + n_out]
        natural, ordered = refs[n_in + 1 + n_after + n_out :]
        t = lax.axis_index("tensor")
        p = lax.axis_index("pipe")

        def work(j, carry):
            at = pl.multiple_of(j * tile, tile)
            for k in range(kinds):
                if transposed:
                    total = lax.dot_general(
                        ordered[...], held[k, pl.ds(at, tile), :], CONTRACT_LAST, preferred_element_type=F32
                    )
                else:
                    total = jnp.dot(
                        ordered[...], held[k, :, pl.ds(at, tile)], preferred_element_type=F32
                    )
                for ref, (_, pieces) in zip(out_refs, layout):
                    for i, (s, a) in enumerate(pieces):
                        row = (s * cores + a) * rows
                        part = total[row : row + rows].astype(ref.dtype)
                        ref[k, i * rows : (i + 1) * rows, pl.ds(at, tile)] = part
            return carry

        def own_block(a, s):
            if s == 0:
                return x_refs[2 * a][...]
            return x_refs[2 * a + 1][(s - 1) * block : s * block, :]

        for a in range(cores):
            if block == rows:
                for s in range(n_tensor):
                    start = pl.multiple_of(((p ^ t ^ s) * cores + a) * rows, rows)
                    ordered[pl.ds(start, rows), :] = own_block(a, s)
                continue
            for s in range(n_tensor):
                start = pl.multiple_of((t ^ s) * block, block)
                natural[pl.ds(start, block), :] = own_block(a, s)
            for s in range(n_pipe):
                start = pl.multiple_of((p ^ s) * rows, rows)
                at = (s * cores + a) * rows
                ordered[at : at + rows, :] = natural[pl.ds(start, rows), :]
        lax.fori_loop(0, count, work, 0, unroll=True)

    return pl.pallas_call(
        kernel,
        in_specs=[IN_VMEM] * (n_in + 1) + [IN_PLACE] * n_after,
        out_specs=[IN_VMEM] * n_out,
        out_shape=[
            jax.ShapeDtypeStruct((kinds, len(pieces) * rows, units), dtype)
            for dtype, pieces in layout
        ],
        scratch_shapes=[
            pltpu.VMEM((tokens, depth), BF16),
            pltpu.VMEM((cores * tokens, depth), BF16),
        ],
        compiler_params=params(),
        cost_estimate=cost(0, 0) if transposed else cost(2 * cores * tokens * depth * units * kinds, 2 * depth * units * kinds),
        name="pull_back" if transposed else "project",
    )(*flat, weights, *after)


def contract(blocks, pieces, weights, transposed, cores, n_pipe, n_tensor, cuts=1, after=()):
    kinds, _, units = blocks[0].shape
    n_in, n_after = len(blocks), len(after)
    from_rows = blocks[0].shape[1] // cores
    tokens = from_rows * n_pipe
    to_rows = tokens // n_tensor
    width = weights.shape[1] if transposed else weights.shape[2]
    tile = pick_tile(width)
    count = width // tile
    cut_width = width // cuts
    n_out = 1 + (cores - 1) * cuts

    def kernel(*refs):
        x_refs = refs[:n_in]
        held = refs[n_in]
        out_refs = refs[n_in + 1 + n_after : n_in + 1 + n_after + n_out]
        natural, ordered = refs[n_in + 1 + n_after + n_out :]
        t = lax.axis_index("tensor")
        p = lax.axis_index("pipe")

        def work(j):
            at = j * tile
            total = None
            for k in range(kinds):
                if transposed:
                    part = lax.dot_general(
                        ordered[k], held[k, at : at + tile, :], CONTRACT_LAST, preferred_element_type=F32
                    )
                else:
                    part = jnp.dot(
                        ordered[k], held[k, :, at : at + tile], preferred_element_type=F32
                    )
                total = part if total is None else total + part
            out_refs[0][:, at : at + tile] = total[:tokens]
            if cores > 1:
                ref = out_refs[1 + at // cut_width]
                place = at % cut_width
                ref[:, place : place + tile] = total[tokens:].astype(ref.dtype)

        def came(k, a, s):
            place, row = pieces[s][a]
            return x_refs[place][k, row : row + from_rows, :]

        for k in range(kinds):
            for a in range(cores):
                if from_rows == to_rows:
                    for s in range(n_pipe):
                        start = pl.multiple_of(a * tokens + (t ^ p ^ s) * to_rows, to_rows)
                        ordered[k, pl.ds(start, to_rows), :] = came(k, a, s)
                    continue
                for s in range(n_pipe):
                    start = pl.multiple_of((p ^ s) * from_rows, from_rows)
                    natural[pl.ds(start, from_rows), :] = came(k, a, s)
                for s in range(n_tensor):
                    start = pl.multiple_of((t ^ s) * to_rows, to_rows)
                    at = a * tokens + s * to_rows
                    ordered[k, at : at + to_rows, :] = natural[pl.ds(start, to_rows), :]
        for j in range(count):
            work(j)

    return pl.pallas_call(
        kernel,
        in_specs=[IN_VMEM] * (n_in + 1) + [IN_PLACE] * n_after,
        out_specs=[IN_VMEM] * n_out,
        out_shape=[jax.ShapeDtypeStruct((tokens, width), F32)]
        + [jax.ShapeDtypeStruct((tokens, cut_width), BF16)] * (n_out - 1),
        scratch_shapes=[
            pltpu.VMEM((tokens, units), BF16),
            pltpu.VMEM((kinds, cores * tokens, units), BF16),
        ],
        compiler_params=params(),
        cost_estimate=cost(2 * cores * tokens * units * width * kinds, 2 * units * width * kinds),
        name="input_grad" if transposed else "layer_output",
    )(*blocks, weights, *after)


def gather_first(value, n_tensor):
    came = {s: exchange(value, "tensor", n_tensor, s) for s in range(n_tensor - 1, 0, -1)}
    return [value] + [came[s] for s in range(1, n_tensor)]


def gather_tokens(blocks, other, cores, after=()):
    own, came = blocks[0], blocks[1:]
    rows, width = own.shape

    def body(ins, outs):
        for s, ref in enumerate(ins):
            outs[0][s * rows : (s + 1) * rows, :] = ref[...]

    shape = (rows * len(came), width)
    (rest,) = small_kernel(body, [(shape, BF16)], came, "assemble", after)
    if cores == 1:
        return [(own, rest)]
    return [(own, rest), (other, exchange(rest, "dp", cores, 1))]


def finish(partials, cores, n_tensor, after=()):
    if cores > 1:
        others = [exchange(x, "dp", cores, 1) for x in partials[1:]]
        rows, width = partials[0].shape[0] // n_tensor, partials[0].shape[1]
        cut = others[0].shape[1]

        def body(ins, outs):
            for s in range(n_tensor):
                at = slice(s * rows, (s + 1) * rows)
                for i, ref in enumerate(ins[1:]):
                    columns = slice(i * cut, (i + 1) * cut)
                    total = ins[0][at, columns] + ref[at].astype(F32)
                    outs[s][:, columns] = total.astype(outs[s].dtype)

        parts = small_kernel(
            body,
            [((rows, width), BF16 if s else F32) for s in range(n_tensor)],
            [partials[0], *others],
            "add_core",
            after,
        )
    else:
        rows = partials[0].shape[0] // n_tensor
        parts = [
            partials[0][s * rows : (s + 1) * rows].astype(BF16 if s else F32)
            for s in range(n_tensor)
        ]

    order = [n_tensor - 1] + list(range(1, n_tensor - 1))
    came = [exchange(parts[s], "tensor", n_tensor, s) for s in order]
    total = parts[0]
    for value in came:
        total = total + value.astype(F32)
    return came, total.astype(BF16)


def slope_values(grad, gate, up):
    gate, up = gate.astype(F32), up.astype(F32)
    sigma = jax.nn.sigmoid(gate)
    gate_slope = (grad * up * sigma * (1.0 + gate * (1.0 - sigma))).astype(BF16)
    up_slope = (grad * gate * sigma).astype(BF16)
    return gate_slope, up_slope


def direct(
    n_pipe, n_tensor, forward_acts, backward_grad, stored_gate, stored_up, gate_weight, up_weight, down_weight
):
    layout = [(BF16 if s else F32, [(s, 0)]) for s in range(n_pipe)]
    pieces = [[(s, 0)] for s in range(n_pipe)]

    def total_of(parts):
        total = parts[0]
        for s in range(1, n_pipe):
            total = total + exchange(parts[s], "pipe", n_pipe, s).astype(F32)
        return total

    def gather(value):
        return [value] + [exchange(value, "pipe", n_pipe, s) for s in range(1, n_pipe)]

    wide, tall = load_weights(gate_weight, up_weight, down_weight, 1)
    grads = gather_tokens(gather_first(backward_grad, n_tensor), None, 1)
    acts = gather_tokens(gather_first(forward_acts, n_tensor), None, 1)
    grad = total_of(project(grads, tall, True, layout, n_pipe, n_tensor))[0]
    slopes = gather(jnp.stack(slope_values(grad, stored_gate, stored_up)))
    summed = total_of(project(acts, wide, False, layout, n_pipe, n_tensor))
    hidden = gather((jax.nn.silu(summed[:1]) * summed[1:]).astype(BF16))
    back = contract(slopes, pieces, wide, True, 1, n_pipe, n_tensor)
    out = contract(hidden, pieces, tall, False, 1, n_pipe, n_tensor)
    return finish(out, 1, n_tensor)[1], finish(back, 1, n_tensor)[1]


def balanced(
    n_tensor, forward_acts, backward_grad, stored_gate, stored_up, gate_weight, up_weight, down_weight
):
    cores, n_pipe, x, y = 2, 4, 1, 2
    units = gate_weight.shape[1] // cores
    rows = stored_gate.shape[0]
    straight = [(BF16 if s else F32, [(s, 0), (s, 1)]) for s in range(n_pipe)]
    balanced_layout = [
        (F32, [(0, 0), (0, 1), (1, 1), (2, 0)]),
        (BF16, [(3, 0), (1, 0)]),
        (BF16, [(3, 1), (2, 1)]),
    ]
    straight_pieces = [[(s, 0), (s, rows)] for s in range(n_pipe)]
    balanced_pieces = straight_pieces[:3] + [[(3, 0), (4, 0)]]


    def swap(value, step):
        return exchange(value, "pipe", n_pipe, step)

    def slopes_body(ins, outs):
        keep, came = ins[0], ins[1:n_pipe]
        for a in range(cores):
            at = slice(a * rows, (a + 1) * rows)
            grad = keep[0, at]
            for ref in came:
                grad = grad + ref[0, at].astype(F32)
            stored = ins[n_pipe + a]
            gate_slope, up_slope = slope_values(grad, stored[0], stored[1])
            outs[0][0, at] = gate_slope
            outs[0][1, at] = up_slope

    def pass_on_body(ins, outs):
        keep, came_x, came_y = ins
        for k in range(2):
            on_x = keep[k, 2 * rows : 3 * rows] + came_y[k, :rows].astype(F32)
            on_y = keep[k, 3 * rows : 4 * rows] + came_x[k, :rows].astype(F32)
            outs[0][k] = on_x.astype(BF16)
            outs[1][k] = on_y.astype(BF16)

    def hidden_body(ins, outs):
        keep, came_x, came_y, then_x, then_y = ins
        for a, near, far in ((0, came_x, then_y), (1, came_y, then_x)):
            at = slice(a * rows, (a + 1) * rows)
            gate, up = [
                keep[k, at] + near[k, rows:].astype(F32) + far[k].astype(F32) for k in range(2)
            ]
            outs[0][0, at] = (jax.nn.silu(gate) * up).astype(BF16)

    def stored_body(ins, outs):
        core = lax.axis_index("dp")
        for k in range(2):
            for c in range(cores):
                start = pl.multiple_of((core ^ c) * units, units)
                outs[c][k] = ins[k][:, pl.ds(start, units)]

    acts = gather_first(forward_acts, n_tensor)
    grads = gather_first(backward_grad, n_tensor)
    wide, tall = load_weights(gate_weight, up_weight, down_weight, cores)
    other_acts = exchange(forward_acts, "dp", cores, 1)
    other_grads = exchange(backward_grad, "dp", cores, 1)
    acts = gather_tokens(acts, other_acts, cores, after=[tall, other_acts, grads[1]])
    keep, for_x, for_y = project(
        acts, wide, False, balanced_layout, n_pipe, n_tensor
    )
    came_x, came_y = swap(for_x, x), swap(for_y, y)
    mine, other = small_kernel(
        stored_body, [((2, rows, units), BF16)] * 2, [stored_gate, stored_up], "stored", after=[keep]
    )
    other = exchange(other, "dp", cores, 1)
    grads = gather_tokens(grads, other_grads, cores, after=[keep])
    parts = project(grads, tall, True, straight, n_pipe, n_tensor, after=[other])
    parts = [parts[0]] + [swap(parts[s], s) for s in (3, 1, 2)]

    half = ((2, rows, units), BF16)
    on_x, on_y = small_kernel(
        pass_on_body, [half, half], [keep, came_x, came_y], "pass_on", after=[parts[0]]
    )
    sums = [keep, came_x, came_y, swap(on_x, x), swap(on_y, y)]
    (hidden,) = small_kernel(hidden_body, [((1, cores * rows, units), BF16)], sums, "hidden")
    order = (2, 3, 1)
    hidden_all = [hidden] + [swap(hidden, s) for s in order]
    hidden_pieces = [straight_pieces[0]] + [straight_pieces[order.index(s) + 1] for s in (1, 2, 3)]

    (slopes,) = small_kernel(
        slopes_body,
        [((2, cores * rows, units), BF16)],
        [*parts, mine, other],
        "slopes",
        after=[hidden],
    )
    slopes_x, slopes_y = swap(slopes, x), swap(slopes, y)

    out = contract(
        hidden_all,
        hidden_pieces,
        tall,
        False,
        cores,
        n_pipe,
        n_tensor,
        cuts=2,
        after=[slopes],
    )
    slopes_all = [
        slopes,
        slopes_x,
        slopes_y,
        swap(slopes_x[:, :rows], y),
        swap(slopes_y[:, rows:], x),
    ]
    came, layer_output = finish(out, cores, n_tensor)
    back = contract(
        slopes_all, balanced_pieces, wide, True, cores, n_pipe, n_tensor, cuts=4
    )
    _, input_grad = finish(back, cores, n_tensor, after=came)
    return layer_output, input_grad


def solution(mesh):
    in_specs = (
        P(("dp", "tensor"), "pipe"),
        P(("dp", "tensor"), "pipe"),
        P(("dp", "pipe"), "tensor"),
        P(("dp", "pipe"), "tensor"),
        P("pipe", "tensor"),
        P("pipe", "tensor"),
        P("tensor", "pipe"),
    )
    out_specs = (P(("dp", "tensor"), "pipe"), P(("dp", "tensor"), "pipe"))

    def whole(*args):
        n_pipe, n_tensor = mesh.shape["pipe"], mesh.shape["tensor"]
        hidden_width = args[4].shape[1] // n_tensor
        if mesh.shape["dp"] == 2 and n_pipe == 4 and hidden_width % 256 == 0:
            body = functools.partial(balanced, n_tensor)
        else:
            body = functools.partial(direct, n_pipe, n_tensor)
        return jax.shard_map(
            body, mesh=mesh, in_specs=in_specs, out_specs=out_specs, check_vma=False
        )(*args)

    return whole
```

```python
import functools

import jax
import jax.numpy as jnp
from jax import lax
from jax.experimental import pallas as pl
from jax.experimental.pallas import tpu as pltpu
from jax.sharding import PartitionSpec as P

F32 = jnp.float32
BF16 = jnp.bfloat16
VMEM_BYTES = 16 * 1024 * 1024
LOAD_BYTES = 24 * 1024 * 1024
CONTRACT_LAST = (((1,), (1,)), ((), ()))
IN_VMEM = pl.BlockSpec(memory_space=pltpu.VMEM)
IN_PLACE = pl.BlockSpec(memory_space=pl.ANY)


def exchange(value, axis, size, step):
    return lax.ppermute(value, axis, [(i, i ^ step) for i in range(size)])


def pick_tile(width):
    return 256 if width % 256 == 0 else 128


def cost(flops, moved):
    return pl.CostEstimate(flops=flops, bytes_accessed=moved, transcendentals=0)


def params():
    return pltpu.CompilerParams(vmem_limit_bytes=VMEM_BYTES)


def small_kernel(body, outs, inputs, name, after=()):
    n_in, n_after = len(inputs), len(after)

    def kernel(*refs):
        body(refs[:n_in], refs[n_in + n_after :])

    moved = sum(a.size * a.dtype.itemsize for a in inputs)
    return pl.pallas_call(
        kernel,
        in_specs=[IN_VMEM] * n_in + [IN_PLACE] * n_after,
        out_specs=[IN_VMEM] * len(outs),
        out_shape=[jax.ShapeDtypeStruct(shape, dtype) for shape, dtype in outs],
        cost_estimate=cost(moved, moved),
        compiler_params=params(),
        name=name,
    )(*inputs, *after)


def load_weights(gate_weight, up_weight, down_weight, cores):
    depth = gate_weight.shape[0]
    units = gate_weight.shape[1] // cores
    cuts = 4
    rows, unit_rows = depth // cuts, units // cuts

    def kernel(gate, up, down, wide, tall, sems):
        first = pl.multiple_of(lax.axis_index("dp") * units, units) if cores > 1 else 0
        copies = []
        for i in range(cuts):
            for k, ref in enumerate((gate, up)):
                at = pl.ds(i * rows, rows)
                copies.append((ref.at[at, pl.ds(first, units)], wide.at[k, at]))
        for i in range(cuts):
            at = pl.multiple_of(first + i * unit_rows, unit_rows)
            copies.append((down.at[pl.ds(at, unit_rows)], tall.at[0, pl.ds(i * unit_rows, unit_rows)]))
        copies = [
            pltpu.make_async_copy(source, target, sems.at[i])
            for i, (source, target) in enumerate(copies)
        ]
        for copy in copies:
            copy.start()
        for copy in copies:
            copy.wait()

    return pl.pallas_call(
        kernel,
        in_specs=[IN_PLACE] * 3,
        out_specs=[IN_VMEM] * 2,
        out_shape=[
            jax.ShapeDtypeStruct((2, depth, units), BF16),
            jax.ShapeDtypeStruct((1, units, depth), BF16),
        ],
        scratch_shapes=[pltpu.SemaphoreType.DMA((3 * cuts,))],
        compiler_params=pltpu.CompilerParams(vmem_limit_bytes=LOAD_BYTES),
        cost_estimate=cost(0, 6 * depth * units),
        name="load_weights",
    )(gate_weight, up_weight, down_weight)


def project(inputs, weights, transposed, layout, n_pipe, n_tensor, after=()):
    cores = len(inputs)
    flat = [x for pair in inputs for x in pair]
    n_in, n_after, n_out, kinds = len(flat), len(after), len(layout), weights.shape[0]
    block, depth = inputs[0][0].shape
    tokens = block * n_tensor
    units = weights.shape[1] if transposed else weights.shape[2]
    tile = pick_tile(units)
    count = units // tile
    rows = tokens // n_pipe

    def kernel(*refs):
        x_refs = refs[:n_in]
        held = refs[n_in]
        out_refs = refs[n_in + 1 + n_after : n_in + 1 + n_after + n_out]
        natural, ordered = refs[n_in + 1 + n_after + n_out :]
        t = lax.axis_index("tensor")
        p = lax.axis_index("pipe")

        def work(j, carry):
            at = pl.multiple_of(j * tile, tile)
            for k in range(kinds):
                if transposed:
                    total = lax.dot_general(
                        ordered[...], held[k, pl.ds(at, tile), :], CONTRACT_LAST, preferred_element_type=F32
                    )
                else:
                    total = jnp.dot(
                        ordered[...], held[k, :, pl.ds(at, tile)], preferred_element_type=F32
                    )
                for ref, (_, pieces) in zip(out_refs, layout):
                    for i, (s, a) in enumerate(pieces):
                        row = (s * cores + a) * rows
                        part = total[row : row + rows].astype(ref.dtype)
                        ref[k, i * rows : (i + 1) * rows, pl.ds(at, tile)] = part
            return carry

        def own_block(a, s):
            if s == 0:
                return x_refs[2 * a][...]
            return x_refs[2 * a + 1][(s - 1) * block : s * block, :]

        for a in range(cores):
            if block == rows:
                for s in range(n_tensor):
                    start = pl.multiple_of(((p ^ t ^ s) * cores + a) * rows, rows)
                    ordered[pl.ds(start, rows), :] = own_block(a, s)
                continue
            for s in range(n_tensor):
                start = pl.multiple_of((t ^ s) * block, block)
                natural[pl.ds(start, block), :] = own_block(a, s)
            for s in range(n_pipe):
                start = pl.multiple_of((p ^ s) * rows, rows)
                at = (s * cores + a) * rows
                ordered[at : at + rows, :] = natural[pl.ds(start, rows), :]
        lax.fori_loop(0, count, work, 0, unroll=True)

    return pl.pallas_call(
        kernel,
        in_specs=[IN_VMEM] * (n_in + 1) + [IN_PLACE] * n_after,
        out_specs=[IN_VMEM] * n_out,
        out_shape=[
            jax.ShapeDtypeStruct((kinds, len(pieces) * rows, units), dtype)
            for dtype, pieces in layout
        ],
        scratch_shapes=[
            pltpu.VMEM((tokens, depth), BF16),
            pltpu.VMEM((cores * tokens, depth), BF16),
        ],
        compiler_params=params(),
        cost_estimate=cost(0, 0) if transposed else cost(2 * cores * tokens * depth * units * kinds, 2 * depth * units * kinds),
        name="pull_back" if transposed else "project",
    )(*flat, weights, *after)


def contract(blocks, pieces, weights, transposed, cores, n_pipe, n_tensor, cuts=1, after=()):
    kinds, _, units = blocks[0].shape
    n_in, n_after = len(blocks), len(after)
    from_rows = blocks[0].shape[1] // cores
    tokens = from_rows * n_pipe
    to_rows = tokens // n_tensor
    width = weights.shape[1] if transposed else weights.shape[2]
    tile = pick_tile(width)
    count = width // tile
    cut_width = width // cuts
    n_out = 1 + (cores - 1) * cuts

    def kernel(*refs):
        x_refs = refs[:n_in]
        held = refs[n_in]
        out_refs = refs[n_in + 1 + n_after : n_in + 1 + n_after + n_out]
        natural, ordered = refs[n_in + 1 + n_after + n_out :]
        t = lax.axis_index("tensor")
        p = lax.axis_index("pipe")

        def work(j):
            at = j * tile
            total = None
            for k in range(kinds):
                if transposed:
                    part = lax.dot_general(
                        ordered[k], held[k, at : at + tile, :], CONTRACT_LAST, preferred_element_type=F32
                    )
                else:
                    part = jnp.dot(
                        ordered[k], held[k, :, at : at + tile], preferred_element_type=F32
                    )
                total = part if total is None else total + part
            out_refs[0][:, at : at + tile] = total[:tokens]
            if cores > 1:
                ref = out_refs[1 + at // cut_width]
                place = at % cut_width
                ref[:, place : place + tile] = total[tokens:].astype(ref.dtype)

        def came(k, a, s):
            place, row = pieces[s][a]
            return x_refs[place][k, row : row + from_rows, :]

        for k in range(kinds):
            for a in range(cores):
                if from_rows == to_rows:
                    for s in range(n_pipe):
                        start = pl.multiple_of(a * tokens + (t ^ p ^ s) * to_rows, to_rows)
                        ordered[k, pl.ds(start, to_rows), :] = came(k, a, s)
                    continue
                for s in range(n_pipe):
                    start = pl.multiple_of((p ^ s) * from_rows, from_rows)
                    natural[pl.ds(start, from_rows), :] = came(k, a, s)
                for s in range(n_tensor):
                    start = pl.multiple_of((t ^ s) * to_rows, to_rows)
                    at = a * tokens + s * to_rows
                    ordered[k, at : at + to_rows, :] = natural[pl.ds(start, to_rows), :]
        for j in range(count):
            work(j)

    return pl.pallas_call(
        kernel,
        in_specs=[IN_VMEM] * (n_in + 1) + [IN_PLACE] * n_after,
        out_specs=[IN_VMEM] * n_out,
        out_shape=[jax.ShapeDtypeStruct((tokens, width), F32)]
        + [jax.ShapeDtypeStruct((tokens, cut_width), BF16)] * (n_out - 1),
        scratch_shapes=[
            pltpu.VMEM((tokens, units), BF16),
            pltpu.VMEM((kinds, cores * tokens, units), BF16),
        ],
        compiler_params=params(),
        cost_estimate=cost(2 * cores * tokens * units * width * kinds, 2 * units * width * kinds),
        name="input_grad" if transposed else "layer_output",
    )(*blocks, weights, *after)


def gather_first(value, n_tensor):
    came = {s: exchange(value, "tensor", n_tensor, s) for s in range(n_tensor - 1, 0, -1)}
    return [value] + [came[s] for s in range(1, n_tensor)]


def gather_tokens(blocks, other, cores, after=()):
    own, came = blocks[0], blocks[1:]
    rows, width = own.shape

    def body(ins, outs):
        for s, ref in enumerate(ins):
            outs[0][s * rows : (s + 1) * rows, :] = ref[...]

    shape = (rows * len(came), width)
    (rest,) = small_kernel(body, [(shape, BF16)], came, "assemble", after)
    if cores == 1:
        return [(own, rest)]
    return [(own, rest), (other, exchange(rest, "dp", cores, 1))]


def finish(partials, cores, n_tensor, after=()):
    if cores > 1:
        others = [exchange(x, "dp", cores, 1) for x in partials[1:]]
        rows, width = partials[0].shape[0] // n_tensor, partials[0].shape[1]
        cut = others[0].shape[1]

        def body(ins, outs):
            for s in range(n_tensor):
                at = slice(s * rows, (s + 1) * rows)
                for i, ref in enumerate(ins[1:]):
                    columns = slice(i * cut, (i + 1) * cut)
                    total = ins[0][at, columns] + ref[at].astype(F32)
                    outs[s][:, columns] = total.astype(outs[s].dtype)

        parts = small_kernel(
            body,
            [((rows, width), BF16 if s else F32) for s in range(n_tensor)],
            [partials[0], *others],
            "add_core",
            after,
        )
    else:
        rows = partials[0].shape[0] // n_tensor
        parts = [
            partials[0][s * rows : (s + 1) * rows].astype(BF16 if s else F32)
            for s in range(n_tensor)
        ]

    order = [n_tensor - 1] + list(range(1, n_tensor - 1))
    came = [exchange(parts[s], "tensor", n_tensor, s) for s in order]
    total = parts[0]
    for value in came:
        total = total + value.astype(F32)
    return came + list(parts[:1]), total.astype(BF16)


def slope_values(grad, gate, up):
    gate, up = gate.astype(F32), up.astype(F32)
    sigma = jax.nn.sigmoid(gate)
    gate_slope = (grad * up * sigma * (1.0 + gate * (1.0 - sigma))).astype(BF16)
    up_slope = (grad * gate * sigma).astype(BF16)
    return gate_slope, up_slope


def direct(
    n_pipe, n_tensor, forward_acts, backward_grad, stored_gate, stored_up, gate_weight, up_weight, down_weight
):
    layout = [(BF16 if s else F32, [(s, 0)]) for s in range(n_pipe)]
    pieces = [[(s, 0)] for s in range(n_pipe)]

    def total_of(parts):
        total = parts[0]
        for s in range(1, n_pipe):
            total = total + exchange(parts[s], "pipe", n_pipe, s).astype(F32)
        return total

    def gather(value):
        return [value] + [exchange(value, "pipe", n_pipe, s) for s in range(1, n_pipe)]

    wide, tall = load_weights(gate_weight, up_weight, down_weight, 1)
    grads = gather_tokens(gather_first(backward_grad, n_tensor), None, 1)
    acts = gather_tokens(gather_first(forward_acts, n_tensor), None, 1)
    grad = total_of(project(grads, tall, True, layout, n_pipe, n_tensor))[0]
    slopes = gather(jnp.stack(slope_values(grad, stored_gate, stored_up)))
    summed = total_of(project(acts, wide, False, layout, n_pipe, n_tensor))
    hidden = gather((jax.nn.silu(summed[:1]) * summed[1:]).astype(BF16))
    back = contract(slopes, pieces, wide, True, 1, n_pipe, n_tensor)
    out = contract(hidden, pieces, tall, False, 1, n_pipe, n_tensor)
    return finish(out, 1, n_tensor)[1], finish(back, 1, n_tensor)[1]


def balanced(
    n_tensor, forward_acts, backward_grad, stored_gate, stored_up, gate_weight, up_weight, down_weight
):
    cores, n_pipe, x, y = 2, 4, 1, 2
    units = gate_weight.shape[1] // cores
    rows = stored_gate.shape[0]
    straight = [(BF16 if s else F32, [(s, 0), (s, 1)]) for s in range(n_pipe)]
    balanced_layout = [
        (F32, [(0, 0), (0, 1), (1, 1), (2, 0)]),
        (BF16, [(3, 0), (1, 0)]),
        (BF16, [(3, 1), (2, 1)]),
    ]
    straight_pieces = [[(s, 0), (s, rows)] for s in range(n_pipe)]
    balanced_pieces = straight_pieces[:3] + [[(3, 0), (4, 0)]]


    def swap(value, step):
        return exchange(value, "pipe", n_pipe, step)

    def slopes_body(ins, outs):
        keep, came = ins[0], ins[1:n_pipe]
        for a in range(cores):
            at = slice(a * rows, (a + 1) * rows)
            grad = keep[0, at]
            for ref in came:
                grad = grad + ref[0, at].astype(F32)
            stored = ins[n_pipe + a]
            gate_slope, up_slope = slope_values(grad, stored[0], stored[1])
            outs[0][0, at] = gate_slope
            outs[0][1, at] = up_slope

    def pass_on_body(ins, outs):
        keep, came_x, came_y = ins
        for k in range(2):
            on_x = keep[k, 2 * rows : 3 * rows] + came_y[k, :rows].astype(F32)
            on_y = keep[k, 3 * rows : 4 * rows] + came_x[k, :rows].astype(F32)
            outs[0][k] = on_x.astype(BF16)
            outs[1][k] = on_y.astype(BF16)

    def hidden_body(ins, outs):
        keep, came_x, came_y, then_x, then_y = ins
        for a, near, far in ((0, came_x, then_y), (1, came_y, then_x)):
            at = slice(a * rows, (a + 1) * rows)
            gate, up = [
                keep[k, at] + near[k, rows:].astype(F32) + far[k].astype(F32) for k in range(2)
            ]
            outs[0][0, at] = (jax.nn.silu(gate) * up).astype(BF16)

    def stored_body(ins, outs):
        core = lax.axis_index("dp")
        for k in range(2):
            for c in range(cores):
                start = pl.multiple_of((core ^ c) * units, units)
                outs[c][k] = ins[k][:, pl.ds(start, units)]

    acts = gather_first(forward_acts, n_tensor)
    grads = gather_first(backward_grad, n_tensor)
    wide, tall = load_weights(gate_weight, up_weight, down_weight, cores)
    other_acts = exchange(forward_acts, "dp", cores, 1)
    other_grads = exchange(backward_grad, "dp", cores, 1)
    acts = gather_tokens(acts, other_acts, cores, after=[tall, other_acts, grads[1]])
    keep, for_x, for_y = project(
        acts, wide, False, balanced_layout, n_pipe, n_tensor
    )
    came_x, came_y = swap(for_x, x), swap(for_y, y)
    mine, other = small_kernel(
        stored_body, [((2, rows, units), BF16)] * 2, [stored_gate, stored_up], "stored", after=[keep]
    )
    other = exchange(other, "dp", cores, 1)
    grads = gather_tokens(grads, other_grads, cores, after=[keep])
    parts = project(grads, tall, True, straight, n_pipe, n_tensor, after=[other])
    parts = [parts[0]] + [swap(parts[s], s) for s in (3, 1, 2)]

    half = ((2, rows, units), BF16)
    on_x, on_y = small_kernel(
        pass_on_body, [half, half], [keep, came_x, came_y], "pass_on", after=[parts[0]]
    )
    sums = [keep, came_x, came_y, swap(on_x, x), swap(on_y, y)]
    (hidden,) = small_kernel(hidden_body, [((1, cores * rows, units), BF16)], sums, "hidden")
    order = (2, 3, 1)
    hidden_all = [hidden] + [swap(hidden, s) for s in order]
    hidden_pieces = [straight_pieces[0]] + [straight_pieces[order.index(s) + 1] for s in (1, 2, 3)]

    (slopes,) = small_kernel(
        slopes_body,
        [((2, cores * rows, units), BF16)],
        [*parts, mine, other],
        "slopes",
        after=[hidden],
    )
    slopes_x, slopes_y = swap(slopes, x), swap(slopes, y)

    out = contract(
        hidden_all,
        hidden_pieces,
        tall,
        False,
        cores,
        n_pipe,
        n_tensor,
        cuts=1,
        after=[slopes],
    )
    slopes_all = [
        slopes,
        slopes_x,
        slopes_y,
        swap(slopes_x[:, :rows], y),
        swap(slopes_y[:, rows:], x),
    ]
    came, layer_output = finish(out, cores, n_tensor)
    back = contract(
        slopes_all, balanced_pieces, wide, True, cores, n_pipe, n_tensor, cuts=4, after=came[3:]
    )
    _, input_grad = finish(back, cores, n_tensor, after=came[:3])
    return layer_output, input_grad


def solution(mesh):
    in_specs = (
        P(("dp", "tensor"), "pipe"),
        P(("dp", "tensor"), "pipe"),
        P(("dp", "pipe"), "tensor"),
        P(("dp", "pipe"), "tensor"),
        P("pipe", "tensor"),
        P("pipe", "tensor"),
        P("tensor", "pipe"),
    )
    out_specs = (P(("dp", "tensor"), "pipe"), P(("dp", "tensor"), "pipe"))

    def whole(*args):
        n_pipe, n_tensor = mesh.shape["pipe"], mesh.shape["tensor"]
        hidden_width = args[4].shape[1] // n_tensor
        if mesh.shape["dp"] == 2 and n_pipe == 4 and hidden_width % 256 == 0:
            body = functools.partial(balanced, n_tensor)
        else:
            body = functools.partial(direct, n_pipe, n_tensor)
        return jax.shard_map(
            body, mesh=mesh, in_specs=in_specs, out_specs=out_specs, check_vma=False
        )(*args)

    return whole
```
